32 devices in a mesh: blk: 2 (over x), tgt: 4 (over y, core), sec: 4 (over z).
Axes of the slice: x: 2, y: 2, z: 4, core: 2. Of those that a mesh axis runs over, the one named last changes fastest.
Arguments:
- modal_loads: bfloat16 [4096, 128], P('blk'), may hold values from -6 to 6
- receptance: bfloat16 [2, 4096, 4096], P(None, ('tgt', 'sec'), 'blk'), may hold values from -0.0625 to 0.0625
- shapes: bfloat16 [4096, 8, 128], P(('blk', 'tgt', 'sec')), may hold values from -0.1875 to 0.1875
- coupling: int32 [32, 8], P(('blk', 'tgt', 'sec')), may hold values from 0 to 31, all different within a row
- panel_coords: float32 [3, 4096], P(None, ('blk', 'tgt', 'sec')), may hold values from 0 to 1
- panel_areas: float32 [4096], P(('blk', 'tgt', 'sec')), may hold values from 0.1 to 1
Outputs:
- new_loads: float32 [4096, 128], P(('blk', 'tgt', 'sec'))
- pressure: bfloat16 [4096, 128], P(('blk', 'tgt', 'sec'))
The draws below stay inside these ranges and needn't reach their ends.
Inputs may be any that keep to these rules, and one draw needn't show every extreme that they name: `coupling`: each row names 8 different mode blocks; every mode block is named by some row.
All inputs are finite; a program needn't handle non-finite values.
Results may differ from the reference program's by a relative error of at most 0.009.
Values may be sent and summed in bfloat16 or wider, within the bound.
No kernel may reach another device: no remote copies, remote signals or barrier semaphores. Data moves between devices by JAX's collectives and lax.ppermute only.
A program may use at most 64 MiB of HBM per device.

```python
import math
import jax
import jax.numpy as jnp
from jax import lax

M = 4096
L = 64
MB = 128
K = 8
PBLK = 128
P_SIZE = 4096
NBLK = 32
MBLK = 32


def steps_of(rng, dims, cuts, low, top_value):
    def one(dim, parts):
        steps = jax.random.uniform(jax.random.fold_in(jax.random.fold_in(rng, 6), dim), (parts,), jnp.float32, low / len(cuts), top_value / len(cuts))
        return jnp.repeat(jnp.exp(steps), dims[dim] // parts).reshape((-1,) + (1,) * (len(dims) - dim - 1))

    loudness = one(*cuts[0])
    for cut in cuts[1:]:
        loudness = loudness * one(*cut)
    return loudness


def picks_of(key, rows, count, top, lift):
    sequence = jax.random.permutation(jax.random.fold_in(key, 1), count)
    boost = sequence
    for power in range(3):
        boost = boost * boost // count
    boost = boost * lift // count
    chance = jax.random.randint(jax.random.fold_in(key, 2), (rows, count), 0, 4096) + boost
    sure = jax.random.permutation(jax.random.fold_in(key, 3), rows)[jnp.arange(count) % rows]
    chance = jnp.where(jnp.arange(rows)[:, None] == sure[None, :], 1 << 14, chance)
    priority = chance * count + jnp.arange(count)
    return lax.top_k(priority.astype(jnp.int32), top)[1].astype(jnp.int32)


def bell_draw(rng, dims, deviation, reach, shards=(), dtype=jnp.bfloat16):
    level = steps_of(rng, dims, shards, -0.22, 0.18) if shards else 1.0
    entries = jax.random.normal(rng, dims, jnp.float32) * deviation * level
    return jnp.minimum(jnp.maximum(entries, -reach), reach).astype(dtype)


def setup_inputs(seed: int = 0) -> dict:
    key_of = jax.random.split(jax.random.key(seed), 7)
    return {
        "modal_loads": bell_draw(key_of[0], (M, 2 * L), 1.0, 6.0, ((0, 2),)),
        "receptance": bell_draw(key_of[1], (2, M, M), (2 * M) ** -0.5, 0.0625, ((1, 16), (2, 2))),
        "shapes": bell_draw(key_of[2], (P_SIZE, K, MB), (K * MB) ** -0.5, 0.1875, ((0, 32),)),
        "coupling": picks_of(key_of[3], NBLK, MBLK, K, 2048),
        "panel_coords": jnp.clip(1.0 * jax.random.uniform(key_of[4], (3, P_SIZE), jnp.float32) ** steps_of(key_of[4], (3, P_SIZE), ((1, 32),), -0.2, 0.2), 0.0, 1.0),
        "panel_areas": jnp.clip(jnp.exp(math.log(1.0) - 2.3025851 * jax.random.uniform(key_of[5], (P_SIZE,), jnp.float32) ** steps_of(key_of[5], (P_SIZE,), ((0, 32),), -0.2, 0.2)), 0.1, 1.0),
    }


wave_number = 40.0

def rotate_combine(leading, second):
    half_width = leading.shape[1] // 2
    return jnp.concatenate([leading[:, :half_width] - second[:, half_width:], leading[:, half_width:] + second[:, :half_width]], axis=1)

def pressure_block(target_geometry, source_geometry, source_vel, total_panels):
    delta_x = target_geometry[0][:, None] - source_geometry[0][None, :]
    delta_y = target_geometry[1][:, None] - source_geometry[1][None, :]
    delta_z = target_geometry[2][:, None] - source_geometry[2][None, :]
    source_area = source_geometry[3][None, :]
    distance = jnp.sqrt(delta_x * delta_x + delta_y * delta_y + delta_z * delta_z + source_area / total_panels)
    weight = source_area / (distance * math.sqrt(total_panels))
    phase_angle = wave_number * distance
    kernel = jnp.concatenate([(jnp.cos(phase_angle) * weight).astype(jnp.bfloat16), (jnp.sin(phase_angle) * weight).astype(jnp.bfloat16)], axis=0)
    products = lax.dot_general(kernel, source_vel, (((1,), (1,)), ((), ())), preferred_element_type=jnp.float32)
    target_count = target_geometry.shape[1]
    return rotate_combine(products[:target_count], products[target_count:])

def reference(modal_loads, receptance, shapes, coupling, panel_coords, panel_areas):
    case_width = modal_loads.shape[1]
    stacked = jnp.dot(receptance.reshape(2 * M, M), modal_loads, preferred_element_type=jnp.float32)
    amplitudes = rotate_combine(stacked[:M], stacked[M:]).astype(jnp.bfloat16)
    blocks = amplitudes.reshape(M // MB, MB, case_width)
    chosen = blocks[coupling]
    shaped = shapes.reshape(NBLK, PBLK, K, MB)
    velocity = jnp.einsum('bpkm,bkmc->bpc', shaped.astype(jnp.float32), chosen.astype(jnp.float32)).reshape(P_SIZE, case_width).astype(jnp.bfloat16)
    geometry = jnp.concatenate([panel_coords, panel_areas[None, :]], axis=0)
    vel_t = velocity.T
    block_rows = 256
    target_blocks = geometry.reshape(4, P_SIZE // block_rows, block_rows).transpose(1, 0, 2)

    def single_block(target_geometry):
        return pressure_block(target_geometry, geometry, vel_t, float(P_SIZE))
    pressure_f = lax.map(single_block, target_blocks).reshape(P_SIZE, case_width)
    pressure = pressure_f.astype(jnp.bfloat16)
    weighted = (panel_areas[:, None] * pressure.astype(jnp.float32)).astype(jnp.bfloat16)
    contrib = jnp.einsum('bpkm,bpc->bkmc', shaped.astype(jnp.float32), weighted.reshape(NBLK, PBLK, case_width).astype(jnp.float32))
    summed = jax.ops.segment_sum(contrib.reshape(NBLK * K, MB, case_width), coupling.reshape(-1), M // MB)
    new_loads = summed.reshape(M, case_width)
    return (new_loads, pressure)
```

```python
import functools
import math

import jax
import jax.numpy as jnp
import numpy as np
from jax import lax
from jax.experimental import pallas as pl
from jax.experimental.pallas import tpu as pltpu
from jax.sharding import PartitionSpec as P

wave_number = 40.0
turns = wave_number / (2.0 * math.pi)
bf16 = jnp.bfloat16
f32 = jnp.float32
AXES = ("blk", "tgt", "sec")
GEO = 16


def fit(values, terms):
    nodes = 0.125 + 0.125 * np.cos(np.pi * (np.arange(400) + 0.5) / 400)
    matrix = np.vander(nodes, terms, increasing=True)
    return [float(c) for c in np.linalg.lstsq(matrix, values(nodes), rcond=None)[0]]


sin_terms = fit(lambda u: math.sqrt(2.0) * np.sin(np.pi * np.sqrt(u)) / np.sqrt(u), 4)
cos_terms = fit(lambda u: math.sqrt(2.0) * np.cos(np.pi * np.sqrt(u)), 4)
round_shift = 1.5 * 2.0**23


def exchange_plane(x, mask):
    nb, nt = lax.axis_size("blk"), lax.axis_size("tgt")
    pairs = [
        (b * nt + t, (b ^ (mask & 1)) * nt + (t ^ (2 * (mask >> 1))))
        for b in range(nb)
        for t in range(nt)
    ]
    return lax.ppermute(x, ("blk", "tgt"), pairs)


def exchange_sec(x, mask):
    return lax.ppermute(x, "sec", [(s, s ^ mask) for s in range(lax.axis_size("sec"))])


def exchange_core(x):
    return lax.ppermute(x, "tgt", [(t, t ^ 1) for t in range(lax.axis_size("tgt"))])


def place():
    t = lax.axis_index("tgt")
    return lax.axis_index("blk"), t // 2, t % 2, lax.axis_index("sec")


def three_parts(x):
    first = x.astype(bf16).astype(f32)
    rest = x - first
    second = rest.astype(bf16).astype(f32)
    return first, second, rest - second


def amplitude_kernel(panels, where, r_ref, l_ref, xyz_ref, area_ref, cpl_ref, own_ref, s1_ref, s2_ref, s3_ref, geo_ref, acc, amp_t, geo):
    step = pl.program_id(0)
    rows = r_ref.shape[1]
    depth = r_ref.shape[2]
    term = jnp.dot(r_ref[...].reshape(2 * rows, depth), l_ref[...], preferred_element_type=f32)

    @pl.when(step == 0)
    def _():
        acc[...] = term
        scaled = (xyz_ref[...] - 0.5) * turns
        area = area_ref[...]
        norm = jnp.sum(scaled * scaled, axis=0, keepdims=True) + area * (turns * turns / panels)
        geo[...] = jnp.zeros_like(geo)
        for i, part in enumerate(three_parts(scaled)):
            geo[3 * i : 3 * i + 3, :] = part
        for i, part in enumerate(three_parts(norm)):
            geo[9 + i : 10 + i, :] = part
        for i, part in enumerate(three_parts(area)):
            geo[12 + i : 13 + i, :] = part
        geo[15:16, 0 : cpl_ref.shape[1]] = cpl_ref[...].astype(f32)

    @pl.when(step > 0)
    def _():
        acc[...] += term

    @pl.when(step == pl.num_programs(0) - 1)
    def _():
        width = acc.shape[1]
        half = width // 2
        lead, second = acc[0:rows, :], acc[rows:, :]
        turned = pltpu.roll(second, half, 1)
        lane = lax.broadcasted_iota(jnp.int32, turned.shape, 1)
        amp = lead + jnp.where(lane < half, -turned, turned)
        amp_t[...] = amp.T
        quarter = half // 4
        mine = where[0]
        blocks = rows // 128
        geo_ref[...] = geo[...].astype(bf16)
        for mask, out in enumerate((own_ref, s1_ref, s2_ref, s3_ref)):
            at = pl.multiple_of((mine ^ mask) * quarter, quarter)
            for part in range(2):
                piece = amp_t[pl.ds(part * half + at, quarter), :]
                for b in range(blocks):
                    r0 = b * 2 * quarter + part * quarter
                    out[r0 : r0 + quarter, :] = piece[:, b * 128 : (b + 1) * 128].astype(out.dtype)
            if mask:
                out[blocks * 2 * quarter :, :] = geo_ref[...]


def amplitude_parts(panels, where, receptance, loads, xyz, area, coupling):
    _, rows, depth = receptance.shape
    width = loads.shape[1]
    steps = 4
    part = depth // steps
    chunk = rows // 128 * (width // 4)
    whole = lambda shape: pl.BlockSpec(shape, lambda i: (0,) * len(shape))
    outs = [((chunk, 128), f32)] + [((chunk + GEO, 128), bf16)] * 3 + [((GEO, 128), bf16)]
    return pl.pallas_call(
        functools.partial(amplitude_kernel, panels),
        grid=(steps,),
        in_specs=[
            pl.BlockSpec(memory_space=pltpu.SMEM),
            pl.BlockSpec((2, rows, part), lambda i: (0, 0, i)),
            pl.BlockSpec((part, width), lambda i: (i, 0)),
            whole(xyz.shape),
            whole(area.shape),
            whole(coupling.shape),
        ],
        out_specs=[whole(s) for s, _ in outs],
        out_shape=[jax.ShapeDtypeStruct(s, d) for s, d in outs],
        scratch_shapes=[
            pltpu.VMEM((2 * rows, width), f32),
            pltpu.VMEM((width, rows), f32),
            pltpu.VMEM((GEO, 128), f32),
        ],
        compiler_params=pltpu.CompilerParams(vmem_limit_bytes=32 << 20),
        cost_estimate=pl.CostEstimate(flops=4 * rows * depth * width, bytes_accessed=4 * rows * depth, transcendentals=0),
        name="amplitude_parts",
    )(where, receptance, loads, xyz, area, coupling)


def amplitude_sum_kernel(own_ref, geo_ref, x_ref, y_ref, d_ref, out_ref):
    n = own_ref.shape[0]
    out_ref[0:n, :] = (own_ref[...] + x_ref[0:n, :].astype(f32)).astype(bf16)
    out_ref[n : 2 * n, :] = (y_ref[0:n, :].astype(f32) + d_ref[0:n, :].astype(f32)).astype(bf16)
    out_ref[2 * n : 2 * n + GEO, :] = geo_ref[...]
    for i, r in enumerate((x_ref, y_ref, d_ref)):
        out_ref[2 * n + GEO * (i + 1) : 2 * n + GEO * (i + 2), :] = r[n:, :]


def amplitude_sum(own, geo, x, y, d):
    n = own.shape[0]
    return pl.pallas_call(
        amplitude_sum_kernel,
        out_shape=jax.ShapeDtypeStruct((2 * n + 4 * GEO, 128), bf16),
        name="amplitude_sum",
    )(own, geo, x, y, d)


def velocity_kernel(width, blocks, where, cpl, near_ref, far_ref, m0, m1, m2, m3, out_ref, picked):
    _, y, c, z = (where[1 + i] for i in range(4))
    count = m0.shape[1] // 128
    secs = near_ref.shape[0]
    for j, m_ref in enumerate((m0, m1, m2, m3)):
        for k in range(count):
            b = cpl[j, k]
            h = b % blocks
            owner = b // blocks
            t, s = owner // secs, owner % secs
            row = pl.multiple_of((((t // 2) ^ y) * blocks + h) * width, width)
            zr = s ^ z

            @pl.when((t % 2) == c)
            def _():
                picked[:, k * 128 : (k + 1) * 128] = near_ref[zr, pl.ds(row, width), :]

            @pl.when((t % 2) != c)
            def _():
                picked[:, k * 128 : (k + 1) * 128] = far_ref[zr, pl.ds(row, width), :]

        vel = lax.dot_general(picked[...], m_ref[...], (((1,), (1,)), ((), ())), preferred_element_type=f32)
        out_ref[j] = vel.astype(bf16)


def velocities(where, cpl, near, far, modes, width, blocks):
    vmem = pl.BlockSpec(memory_space=pltpu.VMEM)
    smem = pl.BlockSpec(memory_space=pltpu.SMEM)
    panels, depth = modes[0].shape
    return pl.pallas_call(
        functools.partial(velocity_kernel, width, blocks),
        in_specs=[smem, smem] + [vmem] * 6,
        out_specs=vmem,
        out_shape=jax.ShapeDtypeStruct((4, width, panels), bf16),
        scratch_shapes=[pltpu.VMEM((width, depth), bf16)],
        compiler_params=pltpu.CompilerParams(vmem_limit_bytes=32 << 20),
        name="velocities",
    )(where, cpl, near, far, *modes)


def helmholtz_kernel(panels, tgt_ref, src_ref, re_ref, im_ref, tgt_mat, dist):
    groups = tgt_ref.shape[0] // GEO
    lanes = 128
    scale = turns / math.sqrt(panels)

    @pl.when(pl.program_id(0) == 0)
    def _():
        ones = jnp.ones((3, lanes), f32)
        for j in range(groups):
            g = tgt_ref[j * GEO : (j + 1) * GEO, :].astype(f32)
            area = g[12:13] + g[13:14] + g[14:15]
            norm = g[9:10] + g[10:11] + g[11:12] - area * (turns * turns / panels)
            col = slice(j * lanes, (j + 1) * lanes)
            tgt_mat[:, col] = jnp.zeros((tgt_mat.shape[0], lanes), f32)
            for a in range(3):
                for b in range(3):
                    tgt_mat[16 * a + 3 * b : 16 * a + 3 * b + 3, col] = -2.0 * g[3 * a : 3 * a + 3]
            tgt_mat[9:12, col] = ones
            for i, part in enumerate(three_parts(norm)):
                tgt_mat[48 + i : 49 + i, col] = part

    src = [src_ref[0, j * GEO : (j + 1) * GEO, :] for j in range(groups)]
    wide = jnp.concatenate(src, axis=1)
    stack = jnp.concatenate([wide, wide, wide, jnp.ones_like(wide)], axis=0)
    dist[...] = lax.dot_general(
        tgt_mat[...].astype(bf16), stack, (((0,), (0,)), ((), ())), preferred_element_type=f32
    )
    area = wide[12:15, :].astype(f32)
    weight = (area[0:1] + area[1:2] + area[2:3]) * scale
    strip = 16

    def step(i, _):
        r0 = pl.multiple_of(i * strip, strip)
        for c0 in range(0, groups * lanes, 256):
            cols = slice(c0, c0 + 256)
            square = dist[pl.ds(r0, strip), cols]
            inverse = lax.rsqrt(square)
            t = square * inverse
            f = t - ((t + round_shift) - round_shift)
            u = f * f
            s = (((sin_terms[3] * u + sin_terms[2]) * u + sin_terms[1]) * u + sin_terms[0]) * f
            c = ((cos_terms[3] * u + cos_terms[2]) * u + cos_terms[1]) * u + cos_terms[0]
            w = weight[:, cols] * inverse
            re_ref[pl.ds(r0, strip), cols] = (w - (s * s) * w).astype(bf16)
            im_ref[pl.ds(r0, strip), cols] = ((s * c) * w).astype(bf16)
        return 0

    lax.fori_loop(0, dist.shape[0] // strip, step, 0, unroll=2)


def helmholtz(panels, targets, payload):
    secs, rows, lanes = payload.shape
    geo = targets.shape[0]
    side = geo // GEO * lanes
    at = rows // geo - 1
    return pl.pallas_call(
        functools.partial(helmholtz_kernel, panels),
        grid=(secs,),
        in_specs=[
            pl.BlockSpec(targets.shape, lambda i: (0, 0)),
            pl.BlockSpec((1, geo, lanes), lambda i: (i, at, 0)),
        ],
        out_specs=[pl.BlockSpec((side, side), lambda i: (0, i))] * 2,
        out_shape=[jax.ShapeDtypeStruct((side, secs * side), bf16)] * 2,
        scratch_shapes=[pltpu.VMEM((64, side), f32), pltpu.VMEM((side, side), f32)],
        compiler_params=pltpu.CompilerParams(vmem_limit_bytes=40 << 20),
        cost_estimate=pl.CostEstimate(flops=30 * side * side * secs, bytes_accessed=4 * side * side * secs, transcendentals=side * side * secs),
        name="helmholtz",
    )(targets, payload)


def pressure_kernel(blocks_of, where, cpl, va_ref, vb_ref, ar_ref, ai_ref, br_ref, bi_ref, geo_ref, m0, m1, m2, m3, pt_ref, near_ref, far_ref, acc, lead, turned, total):
    step = pl.program_id(0)
    secs = pl.num_programs(0)
    groups, width, lanes = va_ref.shape[1:]
    half = width // 2

    def product(v_ref, gr_ref, gi_ref):
        for j in range(groups):
            v = v_ref[0, j]
            col = slice(j * lanes, (j + 1) * lanes)
            lead[:, col] = v
            turned[0:half, col] = -v[half:]
            turned[half:, col] = v[0:half]
        dims = (((1,), (1,)), ((), ()))
        return lax.dot_general(gr_ref[...], lead[...], dims, preferred_element_type=f32) + lax.dot_general(
            gi_ref[...], turned[...], dims, preferred_element_type=f32
        )

    term = product(va_ref, ar_ref, ai_ref) + product(vb_ref, br_ref, bi_ref)

    @pl.when(step == 0)
    def _():
        acc[...] = term

    @pl.when(step > 0)
    def _():
        acc[...] += term

    @pl.when(step == secs - 1)
    def _():
        x, y, c, z = (where[1 + i] for i in range(4))
        p = acc[...].T.astype(bf16)
        total[...] = jnp.zeros_like(total)
        count = m0.shape[1] // lanes
        sec_n, tgt_n = blocks_of
        for j, m_ref in enumerate((m0, m1, m2, m3)):
            pj = p[:, j * lanes : (j + 1) * lanes]
            pt_ref[j] = pj
            g = geo_ref[j * GEO + 12 : j * GEO + 15, :].astype(f32)
            area = g[0:1] + g[1:2] + g[2:3]
            weighted = (pj.astype(f32) * area).astype(bf16)
            terms = jnp.dot(weighted, m_ref[...], preferred_element_type=f32)
            for k in range(count):
                b = cpl[j, k]
                s = b % sec_n
                t = (b // sec_n) % tgt_n
                xb = b // (sec_n * tgt_n)
                at = (((t % 2) ^ c) * sec_n + (s ^ z)) * groups + (xb ^ x) + 2 * ((t // 2) ^ y)
                total[at] += terms[:, k * lanes : (k + 1) * lanes]
        n = near_ref.shape[0]
        near_ref[...] = total[0:n]
        far_ref[...] = total[n:].astype(bf16)


def pressures(where, cpl, va, vb, ga, gb, geo, modes, tgt_n):
    secs, groups, width, lanes = va.shape
    side = groups * lanes
    smem = pl.BlockSpec(memory_space=pltpu.SMEM)
    whole = lambda shape: pl.BlockSpec(shape, lambda i: (0,) * len(shape))
    vel = pl.BlockSpec((1, groups, width, lanes), lambda i: (i, 0, 0, 0))
    mat = pl.BlockSpec((side, side), lambda i: (0, i))
    n = secs * groups
    return pl.pallas_call(
        functools.partial(pressure_kernel, (secs, tgt_n)),
        grid=(secs,),
        in_specs=[smem, smem, vel, vel, mat, mat, mat, mat, whole(geo.shape)] + [whole(modes[0].shape)] * 4,
        out_specs=[whole((groups, width, lanes)), whole((n, width, lanes)), whole((n, width, lanes))],
        out_shape=[
            jax.ShapeDtypeStruct((groups, width, lanes), bf16),
            jax.ShapeDtypeStruct((n, width, lanes), f32),
            jax.ShapeDtypeStruct((n, width, lanes), bf16),
        ],
        scratch_shapes=[
            pltpu.VMEM((side, width), f32),
            pltpu.VMEM((width, side), bf16),
            pltpu.VMEM((width, side), bf16),
            pltpu.VMEM((2 * n, width, lanes), f32),
        ],
        compiler_params=pltpu.CompilerParams(vmem_limit_bytes=48 << 20),
        name="pressures",
    )(where, cpl, va, vb, *ga, *gb, geo, *modes)


def core_sum_kernel(near_ref, got_ref, own_ref, *send):
    groups = own_ref.shape[0]
    own_ref[...] = near_ref[0:groups] + got_ref[0:groups].astype(f32)
    for i, s in enumerate(send):
        r = slice((i + 1) * groups, (i + 2) * groups)
        s[...] = (near_ref[r] + got_ref[r].astype(f32)).astype(bf16)


def core_sum(near, got, secs):
    groups = near.shape[0] // secs
    shape = (groups,) + near.shape[1:]
    return pl.pallas_call(
        core_sum_kernel,
        out_shape=[jax.ShapeDtypeStruct(shape, f32)] + [jax.ShapeDtypeStruct(shape, bf16)] * (secs - 1),
        name="core_sum",
    )(near, got)


def sec_sum_kernel(count, *refs):
    own, got, pt, outs = refs[0], refs[1 : 1 + count], refs[1 + count], refs[2 + count :]
    for j, out in enumerate(outs):
        value = own[j]
        for g in got:
            value = value + g[j].astype(f32)
        out[0] = value.astype(out.dtype)
        out[1] = pt[j].astype(out.dtype)


def sec_sum(own, got, pt):
    shape = (2,) + own.shape[1:]
    return pl.pallas_call(
        functools.partial(sec_sum_kernel, len(got)),
        out_shape=[jax.ShapeDtypeStruct(shape, f32)] + [jax.ShapeDtypeStruct(shape, bf16)] * 3,
        name="sec_sum",
    )(own, *got, pt)


def output_kernel(where, r0, r1, r2, r3, loads_ref, press_ref, loads_t, press_t):
    half = loads_t.shape[0] // 2
    quarter = half // 4
    for mask, r in enumerate((r0, r1, r2, r3)):
        at = pl.multiple_of((where[0] ^ mask) * quarter, quarter)
        for part in range(2):
            rows = pl.ds(part * half + at, quarter)
            loads_t[rows, :] = r[0, part * quarter : (part + 1) * quarter, :].astype(f32)
            press_t[rows, :] = r[1, part * quarter : (part + 1) * quarter, :].astype(f32)
    loads_ref[...] = loads_t[...].T
    press_ref[...] = press_t[...].T.astype(bf16)


def outputs(where, parts):
    _, width, lanes = parts[0].shape
    cols = 4 * width
    vmem = pl.BlockSpec(memory_space=pltpu.VMEM)
    return pl.pallas_call(
        output_kernel,
        in_specs=[pl.BlockSpec(memory_space=pltpu.SMEM)] + [vmem] * 4,
        out_specs=[vmem, vmem],
        out_shape=[jax.ShapeDtypeStruct((lanes, cols), f32), jax.ShapeDtypeStruct((lanes, cols), bf16)],
        scratch_shapes=[pltpu.VMEM((cols, lanes), f32)] * 2,
        name="outputs",
    )(where, *parts)


def on_device_fast(modal_loads, receptance, shapes, coupling, panel_coords, panel_areas):
    secs, tgts = lax.axis_size("sec"), lax.axis_size("tgt")
    device_count = lax.axis_size("blk") * tgts * secs
    pan_dev = panel_coords.shape[1]
    panels = float(pan_dev * device_count)
    width = modal_loads.shape[1] // 4
    blocks = receptance.shape[1] // shapes.shape[2]
    x, y, c, z = place()
    where = jnp.stack([x + 2 * y, x, y, c, z]).astype(jnp.int32)

    own, s1, s2, s3, geo = amplitude_parts(
        panels, where, receptance, modal_loads, panel_coords, panel_areas[None, :], coupling
    )
    got = [exchange_plane(s, m) for m, s in ((1, s1), (2, s2), (3, s3))]
    flat = shapes.reshape(pan_dev, -1)
    modes = [flat] + [exchange_plane(flat, m) for m in (1, 2, 3)]
    count = coupling.shape[1]
    cpl = jnp.concatenate(
        [coupling] + [g[-1:, :count].astype(jnp.int32) for g in got], axis=0
    )
    payload = amplitude_sum(own, geo, *got)
    near = jnp.stack([payload] + [exchange_sec(payload, m) for m in range(1, secs)])
    far = exchange_core(near)
    targets = payload[-4 * GEO :, :]
    g_near = helmholtz(panels, targets, near)
    g_far = helmholtz(panels, targets, far)
    vel = velocities(where, cpl, near, far, modes, width, blocks)
    v_near = jnp.stack([vel] + [exchange_sec(vel, m) for m in range(1, secs)])
    v_far = exchange_core(v_near)
    pt, n_near, n_far = pressures(where, cpl, v_near, v_far, g_near, g_far, targets, modes, tgts)
    n_got = exchange_core(n_far)
    parts = core_sum(n_near, n_got, secs)
    sec_got = [exchange_sec(p, m) for m, p in zip(range(1, secs), parts[1:])]
    finals = sec_sum(parts[0], sec_got, pt)
    mine = [finals[0]] + [exchange_plane(f, m) for m, f in zip((1, 2, 3), finals[1:])]
    return outputs(where, mine)


def rotate_combine(leading, second):
    half_width = leading.shape[1] // 2
    return jnp.concatenate(
        [
            leading[:, :half_width] - second[:, half_width:],
            leading[:, half_width:] + second[:, :half_width],
        ],
        axis=1,
    )


def pressure_block(target_geometry, source_geometry, source_vel, total_panels):
    delta_x = target_geometry[0][:, None] - source_geometry[0][None, :]
    delta_y = target_geometry[1][:, None] - source_geometry[1][None, :]
    delta_z = target_geometry[2][:, None] - source_geometry[2][None, :]
    source_area = source_geometry[3][None, :]
    distance = jnp.sqrt(
        delta_x * delta_x + delta_y * delta_y + delta_z * delta_z + source_area / total_panels
    )
    weight = source_area / (distance * math.sqrt(total_panels))
    phase_angle = wave_number * distance
    kernel = jnp.concatenate(
        [
            (jnp.cos(phase_angle) * weight).astype(jnp.bfloat16),
            (jnp.sin(phase_angle) * weight).astype(jnp.bfloat16),
        ],
        axis=0,
    )
    products = lax.dot_general(
        kernel, source_vel, (((1,), (1,)), ((), ())), preferred_element_type=jnp.float32
    )
    target_count = target_geometry.shape[1]
    return rotate_combine(products[:target_count], products[target_count:])


def on_device_general(modal_loads, receptance, shapes, coupling, panel_coords, panel_areas):
    pan_dev = panel_coords.shape[1]
    case_width = modal_loads.shape[1]
    device_count = lax.axis_size("blk") * lax.axis_size("tgt") * lax.axis_size("sec")
    total_panels = float(pan_dev * device_count)
    row_share = receptance.shape[1]
    stacked = jnp.dot(
        receptance.reshape(2 * row_share, receptance.shape[2]),
        modal_loads,
        preferred_element_type=jnp.float32,
    )
    modal_sum = rotate_combine(stacked[:row_share], stacked[row_share:])
    modal_sum = lax.psum(modal_sum, "blk")
    amplitudes = lax.all_gather(modal_sum.astype(jnp.bfloat16), ("tgt", "sec"), axis=0, tiled=True)
    mode_block = shapes.shape[2]
    blocks = amplitudes.reshape(-1, mode_block, case_width)
    chosen = blocks[coupling]
    block_count = coupling.shape[0]
    shaped = shapes.reshape(block_count, -1, shapes.shape[1], mode_block)
    vel_t = (
        jnp.einsum("bpkm,bkmc->cbp", shaped, chosen, preferred_element_type=jnp.float32)
        .reshape(case_width, pan_dev)
        .astype(jnp.bfloat16)
    )
    geometry = jnp.concatenate([panel_coords, panel_areas[None, :]], axis=0)
    source_vel, source_geometry = (
        lax.all_gather(vel_t.astype(jnp.float32), ("tgt", "sec"), axis=1, tiled=True).astype(
            vel_t.dtype
        ),
        lax.all_gather(geometry, ("tgt", "sec"), axis=1, tiled=True),
    )
    target_geometry = lax.all_gather(geometry, "blk", axis=1, tiled=True)
    target_groups = pan_dev * lax.axis_size("blk") // pan_dev

    def single_block(block_index):
        target_block = lax.dynamic_slice_in_dim(target_geometry, block_index * pan_dev, pan_dev, 1)
        return pressure_block(target_block, source_geometry, source_vel, total_panels)

    stacked_terms = lax.map(single_block, jnp.arange(target_groups, dtype=jnp.int32))
    pressure_f = lax.psum_scatter(
        stacked_terms.reshape(pan_dev * lax.axis_size("blk"), case_width).astype(jnp.bfloat16),
        "blk",
        scatter_dimension=0,
        tiled=True,
    )
    weighted = (panel_areas[:, None] * pressure_f.astype(jnp.float32)).astype(jnp.bfloat16)
    contrib = jnp.einsum(
        "bpkm,bpc->bkmc",
        shaped,
        weighted.reshape(block_count, -1, case_width),
        preferred_element_type=jnp.float32,
    )
    onehot = (
        coupling[:, :, None] == jnp.arange(blocks.shape[0], dtype=jnp.int32)[None, None, :]
    ).astype(jnp.float32)
    partial_loads = jnp.einsum(
        "bkj,bkmc->jmc", onehot, contrib, precision=lax.Precision.HIGHEST
    ).reshape(-1, case_width)
    new_loads = lax.psum_scatter(
        partial_loads, ("blk", "tgt", "sec"), scatter_dimension=0, tiled=True
    )
    return (new_loads, pressure_f)


def on_device(modal_loads, receptance, shapes, coupling, panel_coords, panel_areas):
    lanes = 128
    secs = lax.axis_size("sec")
    mine = modal_loads.shape[0] * lax.axis_size("blk") // (lax.axis_size("blk") * lax.axis_size("tgt") * secs)
    fits = (
        lax.axis_size("blk") == 2
        and lax.axis_size("tgt") == 4
        and secs & (secs - 1) == 0
        and coupling.shape[0] == 1
        and shapes.shape[2] == lanes
        and panel_coords.shape[1] == lanes
        and modal_loads.shape[1] == lanes
        and mine == lanes
    )
    body = on_device_fast if fits else on_device_general
    return body(modal_loads, receptance, shapes, coupling, panel_coords, panel_areas)


def solution(mesh):
    in_specs = (
        P("blk", None),
        P(None, ("tgt", "sec"), "blk"),
        P(("blk", "tgt", "sec"), None, None),
        P(("blk", "tgt", "sec"), None),
        P(None, ("blk", "tgt", "sec")),
        P(("blk", "tgt", "sec")),
    )
    out_specs = (P(("blk", "tgt", "sec"), None), P(("blk", "tgt", "sec"), None))
    return jax.shard_map(
        on_device, mesh=mesh, in_specs=in_specs, out_specs=out_specs, check_vma=False
    )
```

```python
import functools
import math

import jax
import jax.numpy as jnp
import numpy as np
from jax import lax
from jax.experimental import pallas as pl
from jax.experimental.pallas import tpu as pltpu
from jax.sharding import PartitionSpec as P

wave_number = 40.0
turns = wave_number / (2.0 * math.pi)
bf16 = jnp.bfloat16
f32 = jnp.float32
AXES = ("blk", "tgt", "sec")
GEO = 16


def fit(values, terms):
    nodes = 0.125 + 0.125 * np.cos(np.pi * (np.arange(400) + 0.5) / 400)
    matrix = np.vander(nodes, terms, increasing=True)
    return [float(c) for c in np.linalg.lstsq(matrix, values(nodes), rcond=None)[0]]


sin_terms = fit(lambda u: math.sqrt(2.0) * np.sin(np.pi * np.sqrt(u)) / np.sqrt(u), 4)
cos_terms = fit(lambda u: math.sqrt(2.0) * np.cos(np.pi * np.sqrt(u)), 4)


def exchange_plane(x, mask):
    nb, nt = lax.axis_size("blk"), lax.axis_size("tgt")
    pairs = [
        (b * nt + t, (b ^ (mask & 1)) * nt + (t ^ (2 * (mask >> 1))))
        for b in range(nb)
        for t in range(nt)
    ]
    return lax.ppermute(x, ("blk", "tgt"), pairs)


def exchange_sec(x, mask):
    return lax.ppermute(x, "sec", [(s, s ^ mask) for s in range(lax.axis_size("sec"))])


def exchange_core(x):
    return lax.ppermute(x, "tgt", [(t, t ^ 1) for t in range(lax.axis_size("tgt"))])


VMEM = pl.BlockSpec(memory_space=pltpu.VMEM)
SMEM = pl.BlockSpec(memory_space=pltpu.SMEM)
HBM = pl.BlockSpec(memory_space=pltpu.HBM)


def place():
    t = lax.axis_index("tgt")
    return lax.axis_index("blk"), t >> 1, t & 1, lax.axis_index("sec")


def limit(mib):
    return pltpu.CompilerParams(vmem_limit_bytes=mib << 20)


def bits_of(n):
    return n.bit_length() - 1


def three_parts(x):
    first = x.astype(bf16).astype(f32)
    rest = x - first
    second = rest.astype(bf16).astype(f32)
    return first, second, rest - second


def amplitude_kernel(panels, r_hbm, l_hbm, xyz_hbm, area_hbm, cpl_hbm, own_ref, s1_ref, s2_ref, s3_ref, geo_ref, r_buf, l_buf, xyz, areas, cpl, amp_t, geo, sems):
    rows, lanes = r_buf.shape[1], 128
    blocks = rows // lanes
    small = [
        pltpu.make_async_copy(s, d, sems.at[i])
        for i, (s, d) in enumerate(((xyz_hbm, xyz), (area_hbm, areas), (cpl_hbm, cpl)))
    ]
    fetch_loads = pltpu.make_async_copy(l_hbm, l_buf, sems.at[3])
    fetch = [
        pltpu.make_async_copy(r_hbm.at[:, b * lanes : (b + 1) * lanes, :], r_buf.at[:, b * lanes : (b + 1) * lanes, :], sems.at[4 + b])
        for b in range(blocks)
    ]
    for copy in [fetch_loads] + fetch + small:
        copy.start()
    for copy in small:
        copy.wait()
    scaled = (xyz[...] - 0.5) * turns
    area = areas[...]
    norm = jnp.sum(scaled * scaled, axis=0, keepdims=True) + area * (turns * turns / panels)
    geo[...] = jnp.zeros_like(geo)
    for i, part in enumerate(three_parts(scaled)):
        geo[3 * i : 3 * i + 3, :] = part
    for i, part in enumerate(three_parts(norm)):
        geo[9 + i : 10 + i, :] = part
    for i, part in enumerate(three_parts(area)):
        geo[12 + i : 13 + i, :] = part
    geo[15:16, 0 : cpl.shape[1]] = cpl[...].astype(f32)
    packed = geo[...].astype(bf16)
    geo_ref[...] = packed
    for out in (s1_ref, s2_ref, s3_ref):
        out[out.shape[0] - GEO :, :] = packed

    width = l_buf.shape[1]
    half = width // 2
    quarter = half // 4
    x, y, _, _ = place()
    mine = x + 2 * y
    fetch_loads.wait()
    for b in range(blocks):
        fetch[b].wait()
        span = slice(b * lanes, (b + 1) * lanes)
        both = jnp.dot(r_buf[:, span, :].reshape(2 * lanes, r_buf.shape[2]), l_buf[...], preferred_element_type=f32)
        turned = pltpu.roll(both[lanes:], half, 1)
        lane = lax.broadcasted_iota(jnp.int32, turned.shape, 1)
        amp_t[...] = (both[:lanes] + jnp.where(lane < half, -turned, turned)).T
        for mask, out in enumerate((own_ref, s1_ref, s2_ref, s3_ref)):
            at = pl.multiple_of((mine ^ mask) * quarter, quarter)
            for part in range(2):
                r0 = (2 * b + part) * quarter
                out[r0 : r0 + quarter, :] = amp_t[pl.ds(part * half + at, quarter), :].astype(out.dtype)


def amplitude_parts(panels, receptance, loads, xyz, area, coupling):
    _, rows, depth = receptance.shape
    width = loads.shape[1]
    blocks = rows // 128
    chunk = blocks * (width // 4)
    outs = [((chunk, 128), f32)] + [((chunk + GEO, 128), bf16)] * 3 + [((GEO, 128), bf16)]
    return pl.pallas_call(
        functools.partial(amplitude_kernel, panels),
        in_specs=[HBM] * 5,
        out_specs=[VMEM] * len(outs),
        out_shape=[jax.ShapeDtypeStruct(s, d) for s, d in outs],
        scratch_shapes=[
            pltpu.VMEM(receptance.shape, bf16),
            pltpu.VMEM(loads.shape, bf16),
            pltpu.VMEM(xyz.shape, f32),
            pltpu.VMEM(area.shape, f32),
            pltpu.VMEM(coupling.shape, jnp.int32),
            pltpu.VMEM((width, 128), f32),
            pltpu.VMEM((GEO, 128), f32),
            pltpu.SemaphoreType.DMA((4 + blocks,)),
        ],
        compiler_params=limit(12),
        cost_estimate=pl.CostEstimate(flops=4 * rows * depth * width, bytes_accessed=4 * rows * depth, transcendentals=0),
        name="amplitude_parts",
    )(receptance, loads, xyz, area, coupling)


def amplitude_sum_kernel(own_ref, geo_ref, x_ref, y_ref, d_ref, out_ref, cpl_ref):
    n = own_ref.shape[0]
    out_ref[0:n, :] = (own_ref[...] + x_ref[0:n, :].astype(f32)).astype(bf16)
    out_ref[n : 2 * n, :] = (y_ref[0:n, :].astype(f32) + d_ref[0:n, :].astype(f32)).astype(bf16)
    geos = [geo_ref[...]] + [r[n:, :] for r in (x_ref, y_ref, d_ref)]
    for i, g in enumerate(geos):
        out_ref[2 * n + GEO * i : 2 * n + GEO * (i + 1), :] = g
        cpl_ref[i : i + 1, :] = g.astype(f32)[GEO - 1 :, :].astype(jnp.int32)


def amplitude_sum(own, geo, x, y, d):
    n = own.shape[0]
    return pl.pallas_call(
        amplitude_sum_kernel,
        in_specs=[VMEM] * 5,
        out_specs=[VMEM] * 2,
        out_shape=[jax.ShapeDtypeStruct((2 * n + 4 * GEO, 128), bf16), jax.ShapeDtypeStruct((4, 128), jnp.int32)],
        compiler_params=limit(4),
        name="amplitude_sum",
    )(own, geo, x, y, d)


def stack_kernel(*refs):
    for i, r in enumerate(refs[:-1]):
        refs[-1][i] = r[...]


def stack(parts):
    return pl.pallas_call(
        stack_kernel,
        in_specs=[VMEM] * len(parts),
        out_specs=VMEM,
        out_shape=jax.ShapeDtypeStruct((len(parts),) + parts[0].shape, parts[0].dtype),
        compiler_params=limit(4),
        name="stack",
    )(*parts)


def velocity_kernel(width, blocks, scale, secs, cpl, *refs):
    near, far_ref = refs[0:secs], refs[secs]
    modes, out_ref, table, picked = refs[secs + 1 : secs + 5], refs[-3], refs[-2], refs[-1]
    _, y, c, z = place()
    used = 2 * blocks * width
    for i in range(secs):
        table[0, i] = near[i][0:used, :]
        table[1, i] = far_ref[i, 0:used, :]
    sec_bits, block_bits = bits_of(secs), bits_of(blocks)
    count = modes[0].shape[1] // 128
    for j, m_ref in enumerate(modes):
        for k in range(count):
            b = cpl[j, k]
            h = b & (blocks - 1)
            s = (b >> block_bits) & (secs - 1)
            t = b >> (block_bits + sec_bits)
            row = pl.multiple_of((((((t >> 1) ^ y) << block_bits) + h) * width), width)
            picked[j, :, k * 128 : (k + 1) * 128] = table[(t & 1) ^ c, s ^ z, pl.ds(row, width), :]
    for j, m_ref in enumerate(modes):
        vel = lax.dot_general(picked[j], m_ref[...], (((1,), (1,)), ((), ())), preferred_element_type=f32)
        g = near[0][used + GEO * j : used + GEO * (j + 1), :].astype(f32)
        area = (g[12:13] + g[13:14] + g[14:15]) * scale
        out_ref[j] = (vel * area).astype(bf16)


def velocities(panels, cpl, near, far, modes, width, blocks):
    count, depth = modes[0].shape
    secs = len(near)
    return pl.pallas_call(
        functools.partial(velocity_kernel, width, blocks, turns / math.sqrt(panels), secs),
        in_specs=[SMEM] + [VMEM] * (secs + 5),
        out_specs=VMEM,
        out_shape=jax.ShapeDtypeStruct((4, width, count), bf16),
        scratch_shapes=[
            pltpu.VMEM((2, secs, 2 * blocks * width, 128), bf16),
            pltpu.VMEM((4, width, depth), bf16),
        ],
        compiler_params=limit(6),
        name="velocities",
    )(cpl, *near, far, *modes)


def target_kernel(panels, tgt_ref, out_ref, mat):
    lanes = tgt_ref.shape[1]
    mat[...] = jnp.zeros_like(mat)
    for j in range(tgt_ref.shape[0] // GEO):
        g = tgt_ref[j * GEO : (j + 1) * GEO, :].astype(f32)
        area = g[12:13] + g[13:14] + g[14:15]
        norm = g[9:10] + g[10:11] + g[11:12] - area * (turns * turns / panels)
        col = slice(j * lanes, (j + 1) * lanes)
        for a in range(3):
            for b in range(3):
                mat[GEO * a + 3 * b : GEO * a + 3 * b + 3, col] = -2.0 * g[3 * a : 3 * a + 3]
        mat[9:12, col] = jnp.ones((3, lanes), f32)
        for i, part in enumerate(three_parts(norm)):
            mat[3 * GEO + i : 3 * GEO + i + 1, col] = part
    out_ref[...] = mat[...].T.astype(bf16)


def target_matrix(panels, geo):
    side = geo.shape[0] // GEO * geo.shape[1]
    return pl.pallas_call(
        functools.partial(target_kernel, panels),
        in_specs=[VMEM],
        out_specs=VMEM,
        out_shape=jax.ShapeDtypeStruct((side, 4 * GEO), bf16),
        scratch_shapes=[pltpu.VMEM((4 * GEO, side), f32)],
        compiler_params=limit(4),
        name="target_matrix",
    )(geo)


def helmholtz_kernel(at, tgt_ref, src_ref, re_ref, im_ref, dist):
    src = src_ref if at is None else src_ref.at[at]
    side = tgt_ref.shape[0]
    first = src.shape[0] - side // 128 * GEO
    wide = jnp.concatenate([src[first + j * GEO : first + (j + 1) * GEO, :] for j in range(side // 128)], axis=1)
    full = jnp.concatenate([wide, wide, wide, jnp.ones_like(wide)], axis=0)
    dist[...] = jnp.dot(tgt_ref[...], full, preferred_element_type=f32)
    strip, span = 16, 256
    c0, c1, c2 = (c / cos_terms[3] for c in cos_terms[:3])

    def step(i, _):
        rows = pl.ds(pl.multiple_of(i * strip, strip), strip)
        for n in range(side // span):
            cols = slice(n * span, (n + 1) * span)
            square = dist[rows, cols]
            inverse = lax.rsqrt(square)
            t = square * inverse
            f = t - jnp.round(t)
            u = f * f
            s = (((sin_terms[3] * u + sin_terms[2]) * u + sin_terms[1]) * u + sin_terms[0]) * f
            c = ((u + c2) * u + c1) * u + c0
            part = s * inverse
            re_ref[rows, cols] = (inverse - s * part).astype(bf16)
            im_ref[rows, cols] = (c * part).astype(bf16)
        return 0

    lax.fori_loop(0, side // strip, step, 0, unroll=4)


def helmholtz(targets, payload, at=None):
    side = targets.shape[0]
    return pl.pallas_call(
        functools.partial(helmholtz_kernel, at),
        in_specs=[VMEM] * 2,
        out_specs=[VMEM] * 2,
        out_shape=[jax.ShapeDtypeStruct((side, side), bf16)] * 2,
        scratch_shapes=[pltpu.VMEM((side, side), f32)],
        compiler_params=limit(4),
        cost_estimate=pl.CostEstimate(flops=4096 * side * side, bytes_accessed=4 * side * side, transcendentals=side * side),
        name="helmholtz",
    )(targets, payload)


def pressure_kernel(secs, tgt_n, cpl, *refs):
    v_near, v_far = refs[0:secs], refs[secs]
    mats = refs[secs + 1 : 5 * secs + 1]
    geo_ref, modes = refs[5 * secs + 1], refs[5 * secs + 2 : 5 * secs + 6]
    pt_ref, near_ref, far_ref, lead, turned, total = refs[5 * secs + 6 :]
    groups, width, lanes = v_near[0].shape
    half = width // 2
    side = groups * lanes
    for i in range(2 * secs):
        for j in range(groups):
            v = v_near[i][j] if i < secs else v_far[i - secs, j]
            col = slice(i * side + j * lanes, i * side + (j + 1) * lanes)
            lead[:, col] = v
            turned[0:half, col] = -v[half:]
            turned[half:, col] = v[0:half]
    dims = (((1,), (1,)), ((), ()))
    re = im = 0.0
    for i in range(2 * secs):
        col = slice(i * side, (i + 1) * side)
        re += lax.dot_general(mats[2 * i][...], lead[:, col], dims, preferred_element_type=f32)
        im += lax.dot_general(mats[2 * i + 1][...], turned[:, col], dims, preferred_element_type=f32)
    p = (re + im * cos_terms[3]).T.astype(bf16)
    total[...] = jnp.zeros_like(total)
    x, y, c, z = place()
    sec_bits, tgt_bits = bits_of(secs), bits_of(tgt_n)
    for j, m_ref in enumerate(modes):
        pj = p[:, j * lanes : (j + 1) * lanes]
        pt_ref[j] = pj
        g = geo_ref[j * GEO : (j + 1) * GEO, :].astype(f32)
        weighted = (pj.astype(f32) * (g[12:13] + g[13:14] + g[14:15])).astype(bf16)
        terms = jnp.dot(weighted, m_ref[...], preferred_element_type=f32)
        for k in range(m_ref.shape[1] // lanes):
            b = cpl[j, k]
            s = b & (secs - 1)
            t = (b >> sec_bits) & (tgt_n - 1)
            xb = b >> (sec_bits + tgt_bits)
            at = ((((t & 1) ^ c) * secs + (s ^ z)) * groups) + (xb ^ x) + 2 * ((t >> 1) ^ y)
            total[at] += terms[:, k * lanes : (k + 1) * lanes]
    n = near_ref.shape[0]
    near_ref[...] = total[0:n]
    far_ref[...] = total[n:].astype(bf16)


def pressures(cpl, v_near, v_far, mats, geo, modes, tgt_n):
    secs = len(v_near)
    groups, width, lanes = v_near[0].shape
    side = groups * lanes
    n = secs * groups
    args = [*v_near, v_far, *mats, geo, *modes]
    return pl.pallas_call(
        functools.partial(pressure_kernel, secs, tgt_n),
        in_specs=[SMEM] + [VMEM] * len(args),
        out_specs=[VMEM] * 3,
        out_shape=[
            jax.ShapeDtypeStruct((groups, width, lanes), bf16),
            jax.ShapeDtypeStruct((n, width, lanes), f32),
            jax.ShapeDtypeStruct((n, width, lanes), bf16),
        ],
        scratch_shapes=[
            pltpu.VMEM((width, 2 * secs * side), bf16),
            pltpu.VMEM((width, 2 * secs * side), bf16),
            pltpu.VMEM((2 * n, width, lanes), f32),
        ],
        compiler_params=limit(8),
        name="pressures",
    )(cpl, *args)


def core_sum_kernel(near_ref, got_ref, own_ref, *send):
    groups = own_ref.shape[0]
    own_ref[...] = near_ref[0:groups] + got_ref[0:groups].astype(f32)
    for i, s in enumerate(send):
        r = slice((i + 1) * groups, (i + 2) * groups)
        s[...] = (near_ref[r] + got_ref[r].astype(f32)).astype(bf16)


def core_sum(near, got, secs):
    groups = near.shape[0] // secs
    shape = (groups,) + near.shape[1:]
    return pl.pallas_call(
        core_sum_kernel,
        in_specs=[VMEM] * 2,
        out_specs=[VMEM] * secs,
        out_shape=[jax.ShapeDtypeStruct(shape, f32)] + [jax.ShapeDtypeStruct(shape, bf16)] * (secs - 1),
        compiler_params=limit(4),
        name="core_sum",
    )(near, got)


def sec_sum_kernel(count, *refs):
    own, got, pt, outs = refs[0], refs[1 : 1 + count], refs[1 + count], refs[2 + count :]
    for j, out in enumerate(outs):
        value = own[j]
        for g in got:
            value = value + g[j].astype(f32)
        out[0] = value.astype(out.dtype)
        out[1] = pt[j].astype(out.dtype)


def sec_sum(own, got, pt):
    shape = (2,) + own.shape[1:]
    return pl.pallas_call(
        functools.partial(sec_sum_kernel, len(got)),
        in_specs=[VMEM] * (2 + len(got)),
        out_specs=[VMEM] * 4,
        out_shape=[jax.ShapeDtypeStruct(shape, f32)] + [jax.ShapeDtypeStruct(shape, bf16)] * 3,
        compiler_params=limit(4),
        name="sec_sum",
    )(own, *got, pt)


def output_kernel(r0, r1, r2, r3, loads_ref, press_ref, loads_t, press_t):
    half = loads_t.shape[0] // 2
    quarter = half // 4
    x, y, _, _ = place()
    for mask, r in enumerate((r0, r1, r2, r3)):
        at = pl.multiple_of(((x + 2 * y) ^ mask) * quarter, quarter)
        for part in range(2):
            rows = pl.ds(part * half + at, quarter)
            loads_t[rows, :] = r[0, part * quarter : (part + 1) * quarter, :].astype(f32)
            press_t[rows, :] = r[1, part * quarter : (part + 1) * quarter, :].astype(f32)
    loads_ref[...] = loads_t[...].T
    press_ref[...] = press_t[...].T.astype(bf16)


def outputs(parts):
    _, width, lanes = parts[0].shape
    cols = 4 * width
    return pl.pallas_call(
        output_kernel,
        in_specs=[VMEM] * 4,
        out_shape=[jax.ShapeDtypeStruct((lanes, cols), f32), jax.ShapeDtypeStruct((lanes, cols), bf16)],
        scratch_shapes=[pltpu.VMEM((cols, lanes), f32)] * 2,
        compiler_params=limit(4),
        name="outputs",
    )(*parts)


def on_device_fast(modal_loads, receptance, shapes, coupling, panel_coords, panel_areas):
    secs, tgts = lax.axis_size("sec"), lax.axis_size("tgt")
    device_count = lax.axis_size("blk") * tgts * secs
    pan_dev = panel_coords.shape[1]
    panels = float(pan_dev * device_count)
    width = modal_loads.shape[1] // 4
    blocks = receptance.shape[1] // shapes.shape[2]

    own, s1, s2, s3, geo = amplitude_parts(
        panels, receptance, modal_loads, panel_coords, panel_areas[None, :], coupling
    )
    got = [exchange_plane(s, m) for m, s in ((1, s1), (2, s2), (3, s3))]
    flat = shapes.reshape(pan_dev, -1)
    modes = [flat] + [exchange_plane(flat, m) for m in (1, 2, 3)]
    payload, cpl = amplitude_sum(own, geo, *got)
    near = [payload] + [exchange_sec(payload, m) for m in range(1, secs)]
    far = exchange_core(stack(near))
    targets = payload[-4 * GEO :, :]
    across = target_matrix(panels, targets)
    mats = [helmholtz(across, n) for n in near] + [helmholtz(across, far, i) for i in range(secs)]
    mats = [m for pair in mats for m in pair]
    vel = velocities(panels, cpl, near, far, modes, width, blocks)
    v_near = [vel] + [exchange_sec(vel, m) for m in range(1, secs)]
    v_far = exchange_core(stack(v_near))
    pt, n_near, n_far = pressures(cpl, v_near, v_far, mats, targets, modes, tgts)
    parts = core_sum(n_near, exchange_core(n_far), secs)
    sec_got = [exchange_sec(p, m) for m, p in zip(range(1, secs), parts[1:])]
    finals = sec_sum(parts[0], sec_got, pt)
    mine = [finals[0]] + [exchange_plane(f, m) for m, f in zip((1, 2, 3), finals[1:])]
    return outputs(mine)


def rotate_combine(leading, second):
    half_width = leading.shape[1] // 2
    return jnp.concatenate(
        [
            leading[:, :half_width] - second[:, half_width:],
            leading[:, half_width:] + second[:, :half_width],
        ],
        axis=1,
    )


def pressure_block(target_geometry, source_geometry, source_vel, total_panels):
    delta_x = target_geometry[0][:, None] - source_geometry[0][None, :]
    delta_y = target_geometry[1][:, None] - source_geometry[1][None, :]
    delta_z = target_geometry[2][:, None] - source_geometry[2][None, :]
    source_area = source_geometry[3][None, :]
    distance = jnp.sqrt(
        delta_x * delta_x + delta_y * delta_y + delta_z * delta_z + source_area / total_panels
    )
    weight = source_area / (distance * math.sqrt(total_panels))
    phase_angle = wave_number * distance
    kernel = jnp.concatenate(
        [
            (jnp.cos(phase_angle) * weight).astype(jnp.bfloat16),
            (jnp.sin(phase_angle) * weight).astype(jnp.bfloat16),
        ],
        axis=0,
    )
    products = lax.dot_general(
        kernel, source_vel, (((1,), (1,)), ((), ())), preferred_element_type=jnp.float32
    )
    target_count = target_geometry.shape[1]
    return rotate_combine(products[:target_count], products[target_count:])


def on_device_general(modal_loads, receptance, shapes, coupling, panel_coords, panel_areas):
    pan_dev = panel_coords.shape[1]
    case_width = modal_loads.shape[1]
    device_count = lax.axis_size("blk") * lax.axis_size("tgt") * lax.axis_size("sec")
    total_panels = float(pan_dev * device_count)
    row_share = receptance.shape[1]
    stacked = jnp.dot(
        receptance.reshape(2 * row_share, receptance.shape[2]),
        modal_loads,
        preferred_element_type=jnp.float32,
    )
    modal_sum = rotate_combine(stacked[:row_share], stacked[row_share:])
    modal_sum = lax.psum(modal_sum, "blk")
    amplitudes = lax.all_gather(modal_sum.astype(jnp.bfloat16), ("tgt", "sec"), axis=0, tiled=True)
    mode_block = shapes.shape[2]
    blocks = amplitudes.reshape(-1, mode_block, case_width)
    chosen = blocks[coupling]
    block_count = coupling.shape[0]
    shaped = shapes.reshape(block_count, -1, shapes.shape[1], mode_block)
    vel_t = (
        jnp.einsum("bpkm,bkmc->cbp", shaped, chosen, preferred_element_type=jnp.float32)
        .reshape(case_width, pan_dev)
        .astype(jnp.bfloat16)
    )
    geometry = jnp.concatenate([panel_coords, panel_areas[None, :]], axis=0)
    source_vel, source_geometry = (
        lax.all_gather(vel_t.astype(jnp.float32), ("tgt", "sec"), axis=1, tiled=True).astype(
            vel_t.dtype
        ),
        lax.all_gather(geometry, ("tgt", "sec"), axis=1, tiled=True),
    )
    target_geometry = lax.all_gather(geometry, "blk", axis=1, tiled=True)
    target_groups = pan_dev * lax.axis_size("blk") // pan_dev

    def single_block(block_index):
        target_block = lax.dynamic_slice_in_dim(target_geometry, block_index * pan_dev, pan_dev, 1)
        return pressure_block(target_block, source_geometry, source_vel, total_panels)

    stacked_terms = lax.map(single_block, jnp.arange(target_groups, dtype=jnp.int32))
    pressure_f = lax.psum_scatter(
        stacked_terms.reshape(pan_dev * lax.axis_size("blk"), case_width).astype(jnp.bfloat16),
        "blk",
        scatter_dimension=0,
        tiled=True,
    )
    weighted = (panel_areas[:, None] * pressure_f.astype(jnp.float32)).astype(jnp.bfloat16)
    contrib = jnp.einsum(
        "bpkm,bpc->bkmc",
        shaped,
        weighted.reshape(block_count, -1, case_width),
        preferred_element_type=jnp.float32,
    )
    onehot = (
        coupling[:, :, None] == jnp.arange(blocks.shape[0], dtype=jnp.int32)[None, None, :]
    ).astype(jnp.float32)
    partial_loads = jnp.einsum(
        "bkj,bkmc->jmc", onehot, contrib, precision=lax.Precision.HIGHEST
    ).reshape(-1, case_width)
    new_loads = lax.psum_scatter(
        partial_loads, ("blk", "tgt", "sec"), scatter_dimension=0, tiled=True
    )
    return (new_loads, pressure_f)


def on_device(modal_loads, receptance, shapes, coupling, panel_coords, panel_areas):
    lanes = 128
    secs = lax.axis_size("sec")
    mine = modal_loads.shape[0] * lax.axis_size("blk") // (lax.axis_size("blk") * lax.axis_size("tgt") * secs)
    fits = (
        lax.axis_size("blk") == 2
        and lax.axis_size("tgt") == 4
        and secs & (secs - 1) == 0
        and coupling.shape[0] == 1
        and shapes.shape[2] == lanes
        and panel_coords.shape[1] == lanes
        and modal_loads.shape[1] == lanes
        and mine == lanes
    )
    body = on_device_fast if fits else on_device_general
    return body(modal_loads, receptance, shapes, coupling, panel_coords, panel_areas)


def solution(mesh):
    in_specs = (
        P("blk", None),
        P(None, ("tgt", "sec"), "blk"),
        P(("blk", "tgt", "sec"), None, None),
        P(("blk", "tgt", "sec"), None),
        P(None, ("blk", "tgt", "sec")),
        P(("blk", "tgt", "sec")),
    )
    out_specs = (P(("blk", "tgt", "sec"), None), P(("blk", "tgt", "sec"), None))
    return jax.shard_map(
        on_device, mesh=mesh, in_specs=in_specs, out_specs=out_specs, check_vma=False
    )
```

```python
import functools
import math

import jax
import jax.numpy as jnp
import numpy as np
from jax import lax
from jax.experimental import pallas as pl
from jax.experimental.pallas import tpu as pltpu
from jax.sharding import PartitionSpec as P

wave_number = 40.0
turns = wave_number / (2.0 * math.pi)
bf16 = jnp.bfloat16
f32 = jnp.float32
AXES = ("blk", "tgt", "sec")
GEO = 16


def fit(values, terms):
    nodes = 0.125 + 0.125 * np.cos(np.pi * (np.arange(400) + 0.5) / 400)
    matrix = np.vander(nodes, terms, increasing=True)
    return [float(c) for c in np.linalg.lstsq(matrix, values(nodes), rcond=None)[0]]


sin_terms = fit(lambda u: math.sqrt(2.0) * np.sin(np.pi * np.sqrt(u)) / np.sqrt(u), 4)
cos_terms = fit(lambda u: math.sqrt(2.0) * np.cos(np.pi * np.sqrt(u)), 4)


def exchange_plane(x, mask):
    nb, nt = lax.axis_size("blk"), lax.axis_size("tgt")
    pairs = [
        (b * nt + t, (b ^ (mask & 1)) * nt + (t ^ (2 * (mask >> 1))))
        for b in range(nb)
        for t in range(nt)
    ]
    return lax.ppermute(x, ("blk", "tgt"), pairs)


def exchange_sec(x, mask):
    return lax.ppermute(x, "sec", [(s, s ^ mask) for s in range(lax.axis_size("sec"))])


def exchange_core(x):
    return lax.ppermute(x, "tgt", [(t, t ^ 1) for t in range(lax.axis_size("tgt"))])


VMEM = pl.BlockSpec(memory_space=pltpu.VMEM)
SMEM = pl.BlockSpec(memory_space=pltpu.SMEM)
HBM = pl.BlockSpec(memory_space=pltpu.HBM)


def place():
    t = lax.axis_index("tgt")
    return lax.axis_index("blk"), t >> 1, t & 1, lax.axis_index("sec")


def limit(mib):
    return pltpu.CompilerParams(vmem_limit_bytes=mib << 20)


def bits_of(n):
    return n.bit_length() - 1


def three_parts(x):
    first = x.astype(bf16).astype(f32)
    rest = x - first
    second = rest.astype(bf16).astype(f32)
    return first, second, rest - second


def amplitude_kernel(panels, r_hbm, l_hbm, xyz_hbm, area_hbm, cpl_hbm, own_ref, s1_ref, s2_ref, s3_ref, geo_ref, r_buf, l_buf, xyz, areas, cpl, amp_t, geo, sems):
    rows, lanes = r_buf.shape[1], 128
    blocks = rows // lanes
    small = [
        pltpu.make_async_copy(s, d, sems.at[i])
        for i, (s, d) in enumerate(((xyz_hbm, xyz), (area_hbm, areas), (cpl_hbm, cpl)))
    ]
    fetch_loads = pltpu.make_async_copy(l_hbm, l_buf, sems.at[3])
    fetch = [
        pltpu.make_async_copy(r_hbm.at[:, b * lanes : (b + 1) * lanes, :], r_buf.at[:, b * lanes : (b + 1) * lanes, :], sems.at[4 + b])
        for b in range(blocks)
    ]
    for copy in [fetch_loads] + fetch + small:
        copy.start()
    for copy in small:
        copy.wait()
    scaled = (xyz[...] - 0.5) * turns
    area = areas[...]
    norm = jnp.sum(scaled * scaled, axis=0, keepdims=True) + area * (turns * turns / panels)
    geo[...] = jnp.zeros_like(geo)
    for i, part in enumerate(three_parts(scaled)):
        geo[3 * i : 3 * i + 3, :] = part
    for i, part in enumerate(three_parts(norm)):
        geo[9 + i : 10 + i, :] = part
    for i, part in enumerate(three_parts(area)):
        geo[12 + i : 13 + i, :] = part
    geo[15:16, 0 : cpl.shape[1]] = cpl[...].astype(f32)
    packed = geo[...].astype(bf16)
    geo_ref[...] = packed
    for out in (s1_ref, s2_ref, s3_ref):
        out[out.shape[0] - GEO :, :] = packed

    width = l_buf.shape[1]
    half = width // 2
    quarter = half // 4
    x, y, _, _ = place()
    mine = x + 2 * y
    fetch_loads.wait()
    for b in range(blocks):
        fetch[b].wait()
        span = slice(b * lanes, (b + 1) * lanes)
        both = jnp.dot(r_buf[:, span, :].reshape(2 * lanes, r_buf.shape[2]), l_buf[...], preferred_element_type=f32)
        turned = pltpu.roll(both[lanes:], half, 1)
        lane = lax.broadcasted_iota(jnp.int32, turned.shape, 1)
        amp_t[...] = (both[:lanes] + jnp.where(lane < half, -turned, turned)).T
        for mask, out in enumerate((own_ref, s1_ref, s2_ref, s3_ref)):
            at = pl.multiple_of((mine ^ mask) * quarter, quarter)
            for part in range(2):
                r0 = (2 * b + part) * quarter
                out[r0 : r0 + quarter, :] = amp_t[pl.ds(part * half + at, quarter), :].astype(out.dtype)


def amplitude_parts(panels, receptance, loads, xyz, area, coupling):
    _, rows, depth = receptance.shape
    width = loads.shape[1]
    blocks = rows // 128
    chunk = blocks * (width // 4)
    outs = [((chunk, 128), f32)] + [((chunk + GEO, 128), bf16)] * 3 + [((GEO, 128), bf16)]
    return pl.pallas_call(
        functools.partial(amplitude_kernel, panels),
        in_specs=[HBM] * 5,
        out_specs=[VMEM] * len(outs),
        out_shape=[jax.ShapeDtypeStruct(s, d) for s, d in outs],
        scratch_shapes=[
            pltpu.VMEM(receptance.shape, bf16),
            pltpu.VMEM(loads.shape, bf16),
            pltpu.VMEM(xyz.shape, f32),
            pltpu.VMEM(area.shape, f32),
            pltpu.VMEM(coupling.shape, jnp.int32),
            pltpu.VMEM((width, 128), f32),
            pltpu.VMEM((GEO, 128), f32),
            pltpu.SemaphoreType.DMA((4 + blocks,)),
        ],
        compiler_params=limit(12),
        cost_estimate=pl.CostEstimate(flops=4 * rows * depth * width, bytes_accessed=4 * rows * depth, transcendentals=0),
        name="amplitude_parts",
    )(receptance, loads, xyz, area, coupling)


def amplitude_sum_kernel(own_ref, geo_ref, x_ref, y_ref, d_ref, out_ref, cpl_ref):
    n = own_ref.shape[0]
    out_ref[0:n, :] = (own_ref[...] + x_ref[0:n, :].astype(f32)).astype(bf16)
    out_ref[n : 2 * n, :] = (y_ref[0:n, :].astype(f32) + d_ref[0:n, :].astype(f32)).astype(bf16)
    geos = [geo_ref[...]] + [r[n:, :] for r in (x_ref, y_ref, d_ref)]
    for i, g in enumerate(geos):
        out_ref[2 * n + GEO * i : 2 * n + GEO * (i + 1), :] = g
        cpl_ref[i : i + 1, :] = g.astype(f32)[GEO - 1 :, :].astype(jnp.int32)


def amplitude_sum(own, geo, x, y, d):
    n = own.shape[0]
    return pl.pallas_call(
        amplitude_sum_kernel,
        in_specs=[VMEM] * 5,
        out_specs=[VMEM] * 2,
        out_shape=[jax.ShapeDtypeStruct((2 * n + 4 * GEO, 128), bf16), jax.ShapeDtypeStruct((4, 128), jnp.int32)],
        compiler_params=limit(4),
        name="amplitude_sum",
    )(own, geo, x, y, d)


def stack_kernel(*refs):
    for i, r in enumerate(refs[:-1]):
        refs[-1][i] = r[...]


def stack(parts):
    return pl.pallas_call(
        stack_kernel,
        in_specs=[VMEM] * len(parts),
        out_specs=VMEM,
        out_shape=jax.ShapeDtypeStruct((len(parts),) + parts[0].shape, parts[0].dtype),
        compiler_params=limit(4),
        name="stack",
    )(*parts)


def velocity_kernel(width, blocks, scale, secs, cpl, *refs):
    near, far_ref = refs[0:secs], refs[secs]
    modes, out_ref, table, picked = refs[secs + 1 : secs + 5], refs[-3], refs[-2], refs[-1]
    _, y, c, z = place()
    used = 2 * blocks * width
    for i in range(secs):
        table[0, i] = near[i][0:used, :]
        table[1, i] = far_ref[i, 0:used, :]
    sec_bits, block_bits = bits_of(secs), bits_of(blocks)
    count = modes[0].shape[1] // 128
    for j, m_ref in enumerate(modes):
        for k in range(count):
            b = cpl[j, k]
            h = b & (blocks - 1)
            s = (b >> block_bits) & (secs - 1)
            t = b >> (block_bits + sec_bits)
            row = pl.multiple_of((((((t >> 1) ^ y) << block_bits) + h) * width), width)
            picked[j, :, k * 128 : (k + 1) * 128] = table[(t & 1) ^ c, s ^ z, pl.ds(row, width), :]
    for j, m_ref in enumerate(modes):
        vel = lax.dot_general(picked[j], m_ref[...], (((1,), (1,)), ((), ())), preferred_element_type=f32)
        g = near[0][used + GEO * j : used + GEO * (j + 1), :].astype(f32)
        area = (g[12:13] + g[13:14] + g[14:15]) * scale
        out_ref[j] = (vel * area).astype(bf16)


def velocities(panels, cpl, near, far, modes, width, blocks):
    count, depth = modes[0].shape
    secs = len(near)
    return pl.pallas_call(
        functools.partial(velocity_kernel, width, blocks, turns / math.sqrt(panels), secs),
        in_specs=[SMEM] + [VMEM] * (secs + 5),
        out_specs=VMEM,
        out_shape=jax.ShapeDtypeStruct((4, width, count), bf16),
        scratch_shapes=[
            pltpu.VMEM((2, secs, 2 * blocks * width, 128), bf16),
            pltpu.VMEM((4, width, depth), bf16),
        ],
        compiler_params=limit(6),
        name="velocities",
    )(cpl, *near, far, *modes)


def target_kernel(panels, tgt_ref, out_ref, mat):
    lanes = tgt_ref.shape[1]
    mat[...] = jnp.zeros_like(mat)
    for j in range(tgt_ref.shape[0] // GEO):
        g = tgt_ref[j * GEO : (j + 1) * GEO, :].astype(f32)
        area = g[12:13] + g[13:14] + g[14:15]
        norm = g[9:10] + g[10:11] + g[11:12] - area * (turns * turns / panels)
        col = slice(j * lanes, (j + 1) * lanes)
        for a in range(3):
            for b in range(3):
                mat[GEO * a + 3 * b : GEO * a + 3 * b + 3, col] = -2.0 * g[3 * a : 3 * a + 3]
        mat[9:12, col] = jnp.ones((3, lanes), f32)
        for i, part in enumerate(three_parts(norm)):
            mat[3 * GEO + i : 3 * GEO + i + 1, col] = part
    out_ref[...] = mat[...].T.astype(bf16)


def target_matrix(panels, geo):
    side = geo.shape[0] // GEO * geo.shape[1]
    return pl.pallas_call(
        functools.partial(target_kernel, panels),
        in_specs=[VMEM],
        out_specs=VMEM,
        out_shape=jax.ShapeDtypeStruct((side, 4 * GEO), bf16),
        scratch_shapes=[pltpu.VMEM((4 * GEO, side), f32)],
        compiler_params=limit(4),
        name="target_matrix",
    )(geo)


def helmholtz_kernel(at, tgt_ref, src_ref, re_ref, im_ref, dist):
    src = src_ref if at is None else src_ref.at[at]
    side = tgt_ref.shape[0]
    first = src.shape[0] - side // 128 * GEO
    wide = jnp.concatenate([src[first + j * GEO : first + (j + 1) * GEO, :] for j in range(side // 128)], axis=1)
    full = jnp.concatenate([wide, wide, wide, jnp.ones_like(wide)], axis=0)
    dist[...] = jnp.dot(tgt_ref[...], full, preferred_element_type=f32)
    strip, span = 16, 256
    c0, c1, c2 = (c / cos_terms[3] for c in cos_terms[:3])

    def step(i, _):
        rows = pl.ds(pl.multiple_of(i * strip, strip), strip)
        for n in range(side // span):
            cols = slice(n * span, (n + 1) * span)
            square = dist[rows, cols]
            inverse = lax.rsqrt(square)
            t = square * inverse
            f = t - jnp.round(t)
            u = f * f
            s = (((sin_terms[3] * u + sin_terms[2]) * u + sin_terms[1]) * u + sin_terms[0]) * f
            c = ((u + c2) * u + c1) * u + c0
            part = s * inverse
            re_ref[rows, cols] = (inverse - s * part).astype(bf16)
            im_ref[rows, cols] = (c * part).astype(bf16)
        return 0

    lax.fori_loop(0, side // strip, step, 0, unroll=4)


def helmholtz(targets, payload, at=None):
    side = targets.shape[0]
    return pl.pallas_call(
        functools.partial(helmholtz_kernel, at),
        in_specs=[VMEM] * 2,
        out_specs=[VMEM] * 2,
        out_shape=[jax.ShapeDtypeStruct((side, side), bf16)] * 2,
        scratch_shapes=[pltpu.VMEM((side, side), f32)],
        compiler_params=limit(4),
        cost_estimate=pl.CostEstimate(flops=4096 * side * side, bytes_accessed=4 * side * side, transcendentals=side * side),
        name="helmholtz",
    )(targets, payload)


def pressure_kernel(secs, tgt_n, cpl, *refs):
    v_near, v_far = refs[0:secs], refs[secs]
    mats = refs[secs + 1 : 5 * secs + 1]
    geo_ref, modes = refs[5 * secs + 1], refs[5 * secs + 2 : 5 * secs + 6]
    pt_ref, near_ref, far_ref, lead, turned, total = refs[5 * secs + 6 :]
    groups, width, lanes = v_near[0].shape
    half = width // 2
    side = groups * lanes
    for i in range(2 * secs):
        for j in range(groups):
            v = v_near[i][j] if i < secs else v_far[i - secs, j]
            col = slice(i * side + j * lanes, i * side + (j + 1) * lanes)
            lead[:, col] = v
            turned[0:half, col] = -v[half:]
            turned[half:, col] = v[0:half]
    dims = (((1,), (1,)), ((), ()))
    re = im = 0.0
    for i in range(2 * secs):
        col = slice(i * side, (i + 1) * side)
        re += lax.dot_general(mats[2 * i][...], lead[:, col], dims, preferred_element_type=f32)
        im += lax.dot_general(mats[2 * i + 1][...], turned[:, col], dims, preferred_element_type=f32)
    p = (re + im * cos_terms[3]).T.astype(bf16)
    total[...] = jnp.zeros_like(total)
    x, y, c, z = place()
    sec_bits, tgt_bits = bits_of(secs), bits_of(tgt_n)
    for j, m_ref in enumerate(modes):
        pj = p[:, j * lanes : (j + 1) * lanes]
        pt_ref[j] = pj
        g = geo_ref[j * GEO : (j + 1) * GEO, :].astype(f32)
        weighted = (pj.astype(f32) * (g[12:13] + g[13:14] + g[14:15])).astype(bf16)
        terms = jnp.dot(weighted, m_ref[...], preferred_element_type=f32)
        for k in range(m_ref.shape[1] // lanes):
            b = cpl[j, k]
            s = b & (secs - 1)
            t = (b >> sec_bits) & (tgt_n - 1)
            xb = b >> (sec_bits + tgt_bits)
            at = ((((t & 1) ^ c) * secs + (s ^ z)) * groups) + (xb ^ x) + 2 * ((t >> 1) ^ y)
            total[at] += terms[:, k * lanes : (k + 1) * lanes]
    n = near_ref.shape[0]
    near_ref[...] = total[0:n]
    far_ref[...] = total[n:].astype(bf16)


def pressures(cpl, v_near, v_far, mats, geo, modes, tgt_n):
    secs = len(v_near)
    groups, width, lanes = v_near[0].shape
    side = groups * lanes
    n = secs * groups
    args = [*v_near, v_far, *mats, geo, *modes]
    return pl.pallas_call(
        functools.partial(pressure_kernel, secs, tgt_n),
        in_specs=[SMEM] + [VMEM] * len(args),
        out_specs=[VMEM] * 3,
        out_shape=[
            jax.ShapeDtypeStruct((groups, width, lanes), bf16),
            jax.ShapeDtypeStruct((n, width, lanes), f32),
            jax.ShapeDtypeStruct((n, width, lanes), bf16),
        ],
        scratch_shapes=[
            pltpu.VMEM((width, 2 * secs * side), bf16),
            pltpu.VMEM((width, 2 * secs * side), bf16),
            pltpu.VMEM((2 * n, width, lanes), f32),
        ],
        compiler_params=limit(8),
        name="pressures",
    )(cpl, *args)


def core_sum_kernel(near_ref, got_ref, own_ref, *send):
    groups = own_ref.shape[0]
    own_ref[...] = near_ref[0:groups] + got_ref[0:groups].astype(f32)
    for i, s in enumerate(send):
        r = slice((i + 1) * groups, (i + 2) * groups)
        s[...] = (near_ref[r] + got_ref[r].astype(f32)).astype(bf16)


def core_sum(near, got, secs):
    groups = near.shape[0] // secs
    shape = (groups,) + near.shape[1:]
    return pl.pallas_call(
        core_sum_kernel,
        in_specs=[VMEM] * 2,
        out_specs=[VMEM] * secs,
        out_shape=[jax.ShapeDtypeStruct(shape, f32)] + [jax.ShapeDtypeStruct(shape, bf16)] * (secs - 1),
        compiler_params=limit(4),
        name="core_sum",
    )(near, got)


def sec_sum_kernel(count, *refs):
    own, got, pt, outs = refs[0], refs[1 : 1 + count], refs[1 + count], refs[2 + count :]
    for j, out in enumerate(outs):
        value = own[j]
        for g in got:
            value = value + g[j].astype(f32)
        out[0] = value.astype(out.dtype)
        out[1] = pt[j].astype(out.dtype)


def sec_sum(own, got, pt):
    shape = (2,) + own.shape[1:]
    return pl.pallas_call(
        functools.partial(sec_sum_kernel, len(got)),
        in_specs=[VMEM] * (2 + len(got)),
        out_specs=[VMEM] * 4,
        out_shape=[jax.ShapeDtypeStruct(shape, f32)] + [jax.ShapeDtypeStruct(shape, bf16)] * 3,
        compiler_params=limit(4),
        name="sec_sum",
    )(own, *got, pt)


def output_kernel(r0, r1, r2, r3, loads_ref, press_ref, loads_t, press_t):
    half = loads_t.shape[0] // 2
    quarter = half // 4
    x, y, _, _ = place()
    for mask, r in enumerate((r0, r1, r2, r3)):
        at = pl.multiple_of(((x + 2 * y) ^ mask) * quarter, quarter)
        for part in range(2):
            rows = pl.ds(part * half + at, quarter)
            loads_t[rows, :] = r[0, part * quarter : (part + 1) * quarter, :].astype(f32)
            press_t[rows, :] = r[1, part * quarter : (part + 1) * quarter, :].astype(f32)
    loads_ref[...] = loads_t[...].T
    press_ref[...] = press_t[...].T.astype(bf16)


def outputs(parts):
    _, width, lanes = parts[0].shape
    cols = 4 * width
    return pl.pallas_call(
        output_kernel,
        in_specs=[VMEM] * 4,
        out_shape=[jax.ShapeDtypeStruct((lanes, cols), f32), jax.ShapeDtypeStruct((lanes, cols), bf16)],
        scratch_shapes=[pltpu.VMEM((cols, lanes), f32)] * 2,
        compiler_params=limit(4),
        name="outputs",
    )(*parts)


def on_device_fast(modal_loads, receptance, shapes, coupling, panel_coords, panel_areas):
    secs, tgts = lax.axis_size("sec"), lax.axis_size("tgt")
    device_count = lax.axis_size("blk") * tgts * secs
    pan_dev = panel_coords.shape[1]
    panels = float(pan_dev * device_count)
    width = modal_loads.shape[1] // 4
    blocks = receptance.shape[1] // shapes.shape[2]

    held = [
        pltpu.with_memory_space_constraint(a, pltpu.HBM)
        for a in (receptance, modal_loads, panel_coords, panel_areas[None, :], coupling)
    ]
    own, s1, s2, s3, geo = amplitude_parts(panels, *held)
    got = [exchange_plane(s, m) for m, s in ((1, s1), (2, s2), (3, s3))]
    flat = shapes.reshape(pan_dev, -1)
    modes = [flat] + [exchange_plane(flat, m) for m in (1, 2, 3)]
    payload, cpl = amplitude_sum(own, geo, *got)
    near = [payload] + [exchange_sec(payload, m) for m in range(1, secs)]
    far = exchange_core(stack(near))
    targets = payload[-4 * GEO :, :]
    across = target_matrix(panels, targets)
    mats = [helmholtz(across, n) for n in near] + [helmholtz(across, far, i) for i in range(secs)]
    mats = [m for pair in mats for m in pair]
    vel = velocities(panels, cpl, near, far, modes, width, blocks)
    v_near = [vel] + [exchange_sec(vel, m) for m in range(1, secs)]
    v_far = exchange_core(stack(v_near))
    pt, n_near, n_far = pressures(cpl, v_near, v_far, mats, targets, modes, tgts)
    parts = core_sum(n_near, exchange_core(n_far), secs)
    sec_got = [exchange_sec(p, m) for m, p in zip(range(1, secs), parts[1:])]
    finals = sec_sum(parts[0], sec_got, pt)
    mine = [finals[0]] + [exchange_plane(f, m) for m, f in zip((1, 2, 3), finals[1:])]
    return outputs(mine)


def rotate_combine(leading, second):
    half_width = leading.shape[1] // 2
    return jnp.concatenate(
        [
            leading[:, :half_width] - second[:, half_width:],
            leading[:, half_width:] + second[:, :half_width],
        ],
        axis=1,
    )


def pressure_block(target_geometry, source_geometry, source_vel, total_panels):
    delta_x = target_geometry[0][:, None] - source_geometry[0][None, :]
    delta_y = target_geometry[1][:, None] - source_geometry[1][None, :]
    delta_z = target_geometry[2][:, None] - source_geometry[2][None, :]
    source_area = source_geometry[3][None, :]
    distance = jnp.sqrt(
        delta_x * delta_x + delta_y * delta_y + delta_z * delta_z + source_area / total_panels
    )
    weight = source_area / (distance * math.sqrt(total_panels))
    phase_angle = wave_number * distance
    kernel = jnp.concatenate(
        [
            (jnp.cos(phase_angle) * weight).astype(jnp.bfloat16),
            (jnp.sin(phase_angle) * weight).astype(jnp.bfloat16),
        ],
        axis=0,
    )
    products = lax.dot_general(
        kernel, source_vel, (((1,), (1,)), ((), ())), preferred_element_type=jnp.float32
    )
    target_count = target_geometry.shape[1]
    return rotate_combine(products[:target_count], products[target_count:])


def on_device_general(modal_loads, receptance, shapes, coupling, panel_coords, panel_areas):
    pan_dev = panel_coords.shape[1]
    case_width = modal_loads.shape[1]
    device_count = lax.axis_size("blk") * lax.axis_size("tgt") * lax.axis_size("sec")
    total_panels = float(pan_dev * device_count)
    row_share = receptance.shape[1]
    stacked = jnp.dot(
        receptance.reshape(2 * row_share, receptance.shape[2]),
        modal_loads,
        preferred_element_type=jnp.float32,
    )
    modal_sum = rotate_combine(stacked[:row_share], stacked[row_share:])
    modal_sum = lax.psum(modal_sum, "blk")
    amplitudes = lax.all_gather(modal_sum.astype(jnp.bfloat16), ("tgt", "sec"), axis=0, tiled=True)
    mode_block = shapes.shape[2]
    blocks = amplitudes.reshape(-1, mode_block, case_width)
    chosen = blocks[coupling]
    block_count = coupling.shape[0]
    shaped = shapes.reshape(block_count, -1, shapes.shape[1], mode_block)
    vel_t = (
        jnp.einsum("bpkm,bkmc->cbp", shaped, chosen, preferred_element_type=jnp.float32)
        .reshape(case_width, pan_dev)
        .astype(jnp.bfloat16)
    )
    geometry = jnp.concatenate([panel_coords, panel_areas[None, :]], axis=0)
    source_vel, source_geometry = (
        lax.all_gather(vel_t.astype(jnp.float32), ("tgt", "sec"), axis=1, tiled=True).astype(
            vel_t.dtype
        ),
        lax.all_gather(geometry, ("tgt", "sec"), axis=1, tiled=True),
    )
    target_geometry = lax.all_gather(geometry, "blk", axis=1, tiled=True)
    target_groups = pan_dev * lax.axis_size("blk") // pan_dev

    def single_block(block_index):
        target_block = lax.dynamic_slice_in_dim(target_geometry, block_index * pan_dev, pan_dev, 1)
        return pressure_block(target_block, source_geometry, source_vel, total_panels)

    stacked_terms = lax.map(single_block, jnp.arange(target_groups, dtype=jnp.int32))
    pressure_f = lax.psum_scatter(
        stacked_terms.reshape(pan_dev * lax.axis_size("blk"), case_width).astype(jnp.bfloat16),
        "blk",
        scatter_dimension=0,
        tiled=True,
    )
    weighted = (panel_areas[:, None] * pressure_f.astype(jnp.float32)).astype(jnp.bfloat16)
    contrib = jnp.einsum(
        "bpkm,bpc->bkmc",
        shaped,
        weighted.reshape(block_count, -1, case_width),
        preferred_element_type=jnp.float32,
    )
    onehot = (
        coupling[:, :, None] == jnp.arange(blocks.shape[0], dtype=jnp.int32)[None, None, :]
    ).astype(jnp.float32)
    partial_loads = jnp.einsum(
        "bkj,bkmc->jmc", onehot, contrib, precision=lax.Precision.HIGHEST
    ).reshape(-1, case_width)
    new_loads = lax.psum_scatter(
        partial_loads, ("blk", "tgt", "sec"), scatter_dimension=0, tiled=True
    )
    return (new_loads, pressure_f)


def on_device(modal_loads, receptance, shapes, coupling, panel_coords, panel_areas):
    lanes = 128
    secs = lax.axis_size("sec")
    mine = modal_loads.shape[0] * lax.axis_size("blk") // (lax.axis_size("blk") * lax.axis_size("tgt") * secs)
    fits = (
        lax.axis_size("blk") == 2
        and lax.axis_size("tgt") == 4
        and secs & (secs - 1) == 0
        and coupling.shape[0] == 1
        and shapes.shape[2] == lanes
        and panel_coords.shape[1] == lanes
        and modal_loads.shape[1] == lanes
        and mine == lanes
    )
    body = on_device_fast if fits else on_device_general
    return body(modal_loads, receptance, shapes, coupling, panel_coords, panel_areas)


def solution(mesh):
    in_specs = (
        P("blk", None),
        P(None, ("tgt", "sec"), "blk"),
        P(("blk", "tgt", "sec"), None, None),
        P(("blk", "tgt", "sec"), None),
        P(None, ("blk", "tgt", "sec")),
        P(("blk", "tgt", "sec")),
    )
    out_specs = (P(("blk", "tgt", "sec"), None), P(("blk", "tgt", "sec"), None))
    return jax.shard_map(
        on_device, mesh=mesh, in_specs=in_specs, out_specs=out_specs, check_vma=False
    )
```

```python
import functools
import math

import jax
import jax.numpy as jnp
import numpy as np
from jax import lax
from jax.experimental import pallas as pl
from jax.experimental.pallas import tpu as pltpu
from jax.sharding import PartitionSpec as P

wave_number = 40.0
turns = wave_number / (2.0 * math.pi)
bf16 = jnp.bfloat16
f32 = jnp.float32
AXES = ("blk", "tgt", "sec")
GEO = 16


def fit(values, terms):
    nodes = 0.125 + 0.125 * np.cos(np.pi * (np.arange(400) + 0.5) / 400)
    matrix = np.vander(nodes, terms, increasing=True)
    return [float(c) for c in np.linalg.lstsq(matrix, values(nodes), rcond=None)[0]]


sin_terms = fit(lambda u: math.sqrt(2.0) * np.sin(np.pi * np.sqrt(u)) / np.sqrt(u), 4)
cos_terms = fit(lambda u: math.sqrt(2.0) * np.cos(np.pi * np.sqrt(u)), 4)


def exchange_plane(x, mask):
    nb, nt = lax.axis_size("blk"), lax.axis_size("tgt")
    pairs = [
        (b * nt + t, (b ^ (mask & 1)) * nt + (t ^ (2 * (mask >> 1))))
        for b in range(nb)
        for t in range(nt)
    ]
    return lax.ppermute(x, ("blk", "tgt"), pairs)


def exchange_sec(x, mask):
    return lax.ppermute(x, "sec", [(s, s ^ mask) for s in range(lax.axis_size("sec"))])


def exchange_core(x):
    return lax.ppermute(x, "tgt", [(t, t ^ 1) for t in range(lax.axis_size("tgt"))])


VMEM = pl.BlockSpec(memory_space=pltpu.VMEM)
SMEM = pl.BlockSpec(memory_space=pltpu.SMEM)
HBM = pl.BlockSpec(memory_space=pltpu.HBM)


def place():
    t = lax.axis_index("tgt")
    return lax.axis_index("blk"), t >> 1, t & 1, lax.axis_index("sec")


def limit(mib):
    return pltpu.CompilerParams(vmem_limit_bytes=mib << 20)


def bits_of(n):
    return n.bit_length() - 1


def three_parts(x):
    first = x.astype(bf16).astype(f32)
    rest = x - first
    second = rest.astype(bf16).astype(f32)
    return first, second, rest - second


def amplitude_kernel(panels, r_hbm, l_hbm, xyz_hbm, area_hbm, cpl_hbm, own_ref, s1_ref, s2_ref, s3_ref, geo_ref, r_buf, l_buf, xyz, areas, cpl, amp_t, geo, sems):
    rows, lanes = r_buf.shape[1], 128
    blocks = rows // lanes
    small = [
        pltpu.make_async_copy(s, d, sems.at[i])
        for i, (s, d) in enumerate(((xyz_hbm, xyz), (area_hbm, areas), (cpl_hbm, cpl)))
    ]
    fetch_loads = pltpu.make_async_copy(l_hbm, l_buf, sems.at[3])
    fetch = [
        pltpu.make_async_copy(r_hbm.at[:, b * lanes : (b + 1) * lanes, :], r_buf.at[:, b * lanes : (b + 1) * lanes, :], sems.at[4 + b])
        for b in range(blocks)
    ]
    for copy in [fetch_loads] + fetch + small:
        copy.start()
    for copy in small:
        copy.wait()
    scaled = (xyz[...] - 0.5) * turns
    area = areas[...]
    norm = jnp.sum(scaled * scaled, axis=0, keepdims=True) + area * (turns * turns / panels)
    geo[...] = jnp.zeros_like(geo)
    for i, part in enumerate(three_parts(scaled)):
        geo[3 * i : 3 * i + 3, :] = part
    for i, part in enumerate(three_parts(norm)):
        geo[9 + i : 10 + i, :] = part
    for i, part in enumerate(three_parts(area)):
        geo[12 + i : 13 + i, :] = part
    geo[15:16, 0 : cpl.shape[1]] = cpl[...].astype(f32)
    packed = geo[...].astype(bf16)
    geo_ref[...] = packed
    for out in (s1_ref, s2_ref, s3_ref):
        out[out.shape[0] - GEO :, :] = packed

    width = l_buf.shape[1]
    half = width // 2
    quarter = half // 4
    x, y, _, _ = place()
    mine = x + 2 * y
    fetch_loads.wait()
    for b in range(blocks):
        fetch[b].wait()
        span = slice(b * lanes, (b + 1) * lanes)
        both = jnp.dot(r_buf[:, span, :].reshape(2 * lanes, r_buf.shape[2]), l_buf[...], preferred_element_type=f32)
        turned = pltpu.roll(both[lanes:], half, 1)
        lane = lax.broadcasted_iota(jnp.int32, turned.shape, 1)
        amp_t[...] = (both[:lanes] + jnp.where(lane < half, -turned, turned)).T
        for mask, out in enumerate((own_ref, s1_ref, s2_ref, s3_ref)):
            at = pl.multiple_of((mine ^ mask) * quarter, quarter)
            for part in range(2):
                r0 = (2 * b + part) * quarter
                out[r0 : r0 + quarter, :] = amp_t[pl.ds(part * half + at, quarter), :].astype(out.dtype)


def amplitude_parts(panels, receptance, loads, xyz, area, coupling):
    _, rows, depth = receptance.shape
    width = loads.shape[1]
    blocks = rows // 128
    chunk = blocks * (width // 4)
    outs = [((chunk, 128), f32)] + [((chunk + GEO, 128), bf16)] * 3 + [((GEO, 128), bf16)]
    return pl.pallas_call(
        functools.partial(amplitude_kernel, panels),
        in_specs=[HBM] * 5,
        out_specs=[VMEM] * len(outs),
        out_shape=[jax.ShapeDtypeStruct(s, d) for s, d in outs],
        scratch_shapes=[
            pltpu.VMEM(receptance.shape, bf16),
            pltpu.VMEM(loads.shape, bf16),
            pltpu.VMEM(xyz.shape, f32),
            pltpu.VMEM(area.shape, f32),
            pltpu.VMEM(coupling.shape, jnp.int32),
            pltpu.VMEM((width, 128), f32),
            pltpu.VMEM((GEO, 128), f32),
            pltpu.SemaphoreType.DMA((4 + blocks,)),
        ],
        compiler_params=limit(12),
        cost_estimate=pl.CostEstimate(flops=4 * rows * depth * width, bytes_accessed=1, transcendentals=0),
        name="amplitude_parts",
    )(receptance, loads, xyz, area, coupling)


def amplitude_sum_kernel(count, *refs):
    own_ref, geo_ref, d_ref, x_ref, y_ref, out_ref, cpl_ref = refs[count:]
    n = own_ref.shape[0]
    out_ref[0:n, :] = (own_ref[...] + x_ref[0:n, :].astype(f32)).astype(bf16)
    out_ref[n : 2 * n, :] = (y_ref[0:n, :].astype(f32) + d_ref[0:n, :].astype(f32)).astype(bf16)
    geos = [geo_ref[...]] + [r[n:, :] for r in (x_ref, y_ref, d_ref)]
    for i, g in enumerate(geos):
        out_ref[2 * n + GEO * i : 2 * n + GEO * (i + 1), :] = g
        cpl_ref[i : i + 1, :] = g.astype(f32)[GEO - 1 :, :].astype(jnp.int32)


def amplitude_sum(early, own, geo, x, y, d):
    n = own.shape[0]
    return pl.pallas_call(
        functools.partial(amplitude_sum_kernel, len(early)),
        in_specs=[pl.BlockSpec(memory_space=pl.ANY)] * len(early) + [VMEM] * 5,
        out_specs=[VMEM] * 2,
        out_shape=[jax.ShapeDtypeStruct((2 * n + 4 * GEO, 128), bf16), jax.ShapeDtypeStruct((4, 128), jnp.int32)],
        compiler_params=limit(4),
        name="amplitude_sum",
    )(*early, own, geo, d, x, y)


def stack_kernel(*refs):
    for i, r in enumerate(refs[:-1]):
        refs[-1][i] = r[...]


def stack(parts):
    return pl.pallas_call(
        stack_kernel,
        in_specs=[VMEM] * len(parts),
        out_specs=VMEM,
        out_shape=jax.ShapeDtypeStruct((len(parts),) + parts[0].shape, parts[0].dtype),
        compiler_params=limit(4),
        name="stack",
    )(*parts)


def velocity_kernel(width, blocks, scale, secs, cpl, *refs):
    near, far_ref = refs[0:secs], refs[secs]
    modes, out_ref, table, picked = refs[secs + 1 : secs + 5], refs[-3], refs[-2], refs[-1]
    _, y, c, z = place()
    used = 2 * blocks * width
    for i in range(secs):
        table[0, i] = near[i][0:used, :]
        table[1, i] = far_ref[i, 0:used, :]
    sec_bits, block_bits = bits_of(secs), bits_of(blocks)
    count = modes[0].shape[1] // 128
    for j, m_ref in enumerate(modes):
        for k in range(count):
            b = cpl[j, k]
            h = b & (blocks - 1)
            s = (b >> block_bits) & (secs - 1)
            t = b >> (block_bits + sec_bits)
            row = pl.multiple_of((((((t >> 1) ^ y) << block_bits) + h) * width), width)
            picked[j, :, k * 128 : (k + 1) * 128] = table[(t & 1) ^ c, s ^ z, pl.ds(row, width), :]
    for j, m_ref in enumerate(modes):
        vel = lax.dot_general(picked[j], m_ref[...], (((1,), (1,)), ((), ())), preferred_element_type=f32)
        g = near[0][used + GEO * j : used + GEO * (j + 1), :].astype(f32)
        area = (g[12:13] + g[13:14] + g[14:15]) * scale
        out_ref[j] = (vel * area).astype(bf16)


def velocities(panels, cpl, near, far, modes, width, blocks):
    count, depth = modes[0].shape
    secs = len(near)
    return pl.pallas_call(
        functools.partial(velocity_kernel, width, blocks, turns / math.sqrt(panels), secs),
        in_specs=[SMEM] + [VMEM] * (secs + 5),
        out_specs=VMEM,
        out_shape=jax.ShapeDtypeStruct((4, width, count), bf16),
        scratch_shapes=[
            pltpu.VMEM((2, secs, 2 * blocks * width, 128), bf16),
            pltpu.VMEM((4, width, depth), bf16),
        ],
        compiler_params=limit(6),
        name="velocities",
    )(cpl, *near, far, *modes)


def target_kernel(panels, tgt_ref, out_ref, mat):
    lanes = tgt_ref.shape[1]
    mat[...] = jnp.zeros_like(mat)
    for j in range(tgt_ref.shape[0] // GEO):
        g = tgt_ref[j * GEO : (j + 1) * GEO, :].astype(f32)
        area = g[12:13] + g[13:14] + g[14:15]
        norm = g[9:10] + g[10:11] + g[11:12] - area * (turns * turns / panels)
        col = slice(j * lanes, (j + 1) * lanes)
        for a in range(3):
            for b in range(3):
                mat[GEO * a + 3 * b : GEO * a + 3 * b + 3, col] = -2.0 * g[3 * a : 3 * a + 3]
        mat[9:12, col] = jnp.ones((3, lanes), f32)
        for i, part in enumerate(three_parts(norm)):
            mat[3 * GEO + i : 3 * GEO + i + 1, col] = part
    out_ref[...] = mat[...].astype(bf16)


def target_matrix(panels, geo):
    side = geo.shape[0] // GEO * geo.shape[1]
    return pl.pallas_call(
        functools.partial(target_kernel, panels),
        in_specs=[VMEM],
        out_specs=VMEM,
        out_shape=jax.ShapeDtypeStruct((4 * GEO, side), bf16),
        scratch_shapes=[pltpu.VMEM((4 * GEO, side), f32)],
        compiler_params=limit(4),
        name="target_matrix",
    )(geo)


def helmholtz_kernel(at, tgt_ref, src_ref, *refs):
    re_ref, im_ref = refs[-2:]
    src = src_ref if at is None else src_ref.at[at]
    side = tgt_ref.shape[1]
    first = src.shape[0] - side // 128 * GEO
    c0, c1, c2 = (c / cos_terms[3] for c in cos_terms[:3])
    strip = 128
    for r in range(0, side, strip):
        at_row = first + r // 128 * GEO
        one = src[at_row : at_row + GEO, :]
        full = jnp.concatenate([one, one, one, jnp.ones_like(one)], axis=0)
        square = lax.dot_general(full, tgt_ref[...], (((0,), (0,)), ((), ())), preferred_element_type=f32)
        inverse = lax.rsqrt(square)
        t = square * inverse
        f = t - jnp.round(t)
        u = f * f
        s = (((sin_terms[3] * u + sin_terms[2]) * u + sin_terms[1]) * u + sin_terms[0]) * f
        c = ((u + c2) * u + c1) * u + c0
        part = s * inverse
        re_ref[r : r + strip, :] = (inverse - s * part).astype(bf16)
        im_ref[r : r + strip, :] = (c * part).astype(bf16)


def helmholtz(targets, payload, at=None, after=(), cost=1.0):
    side = targets.shape[1]
    return pl.pallas_call(
        functools.partial(helmholtz_kernel, at),
        in_specs=[VMEM] * 2 + [pl.BlockSpec(memory_space=pl.ANY)] * len(after),
        out_specs=[VMEM] * 2,
        out_shape=[jax.ShapeDtypeStruct((side, side), bf16)] * 2,
        compiler_params=limit(4),
        cost_estimate=pl.CostEstimate(flops=int(cost * 4000 * side * side), bytes_accessed=1, transcendentals=0),
        name="helmholtz",
    )(targets, payload, *after)


def pressure_kernel(secs, tgt_n, cpl, *refs):
    v_near, v_far = refs[0:secs], refs[secs]
    mats = refs[secs + 1 : 5 * secs + 1]
    geo_ref, modes = refs[5 * secs + 1], refs[5 * secs + 2 : 5 * secs + 6]
    pt_ref, near_ref, far_ref, lead, turned, total = refs[5 * secs + 6 :]
    groups, width, lanes = v_near[0].shape
    half = width // 2
    side = groups * lanes
    for i in range(2 * secs):
        for j in range(groups):
            v = v_near[i][j] if i < secs else v_far[i - secs, j]
            col = slice(i * side + j * lanes, i * side + (j + 1) * lanes)
            lead[:, col] = v
            turned[0:half, col] = -v[half:]
            turned[half:, col] = v[0:half]
    re = im = 0.0
    for i in range(2 * secs):
        col = slice(i * side, (i + 1) * side)
        re += jnp.dot(lead[:, col], mats[2 * i][...], preferred_element_type=f32)
        im += jnp.dot(turned[:, col], mats[2 * i + 1][...], preferred_element_type=f32)
    p = (re + im * cos_terms[3]).astype(bf16)
    total[...] = jnp.zeros_like(total)
    x, y, c, z = place()
    sec_bits, tgt_bits = bits_of(secs), bits_of(tgt_n)
    for j, m_ref in enumerate(modes):
        pj = p[:, j * lanes : (j + 1) * lanes]
        pt_ref[j] = pj
        g = geo_ref[j * GEO : (j + 1) * GEO, :].astype(f32)
        weighted = (pj.astype(f32) * (g[12:13] + g[13:14] + g[14:15])).astype(bf16)
        terms = jnp.dot(weighted, m_ref[...], preferred_element_type=f32)
        for k in range(m_ref.shape[1] // lanes):
            b = cpl[j, k]
            s = b & (secs - 1)
            t = (b >> sec_bits) & (tgt_n - 1)
            xb = b >> (sec_bits + tgt_bits)
            at = ((((t & 1) ^ c) * secs + (s ^ z)) * groups) + (xb ^ x) + 2 * ((t >> 1) ^ y)
            total[at] += terms[:, k * lanes : (k + 1) * lanes]
    n = near_ref.shape[0]
    near_ref[...] = total[0:n]
    far_ref[...] = total[n:].astype(bf16)


def pressures(cpl, v_near, v_far, mats, geo, modes, tgt_n):
    secs = len(v_near)
    groups, width, lanes = v_near[0].shape
    side = groups * lanes
    n = secs * groups
    args = [*v_near, v_far, *mats, geo, *modes]
    return pl.pallas_call(
        functools.partial(pressure_kernel, secs, tgt_n),
        in_specs=[SMEM] + [VMEM] * len(args),
        out_specs=[VMEM] * 3,
        out_shape=[
            jax.ShapeDtypeStruct((groups, width, lanes), bf16),
            jax.ShapeDtypeStruct((n, width, lanes), f32),
            jax.ShapeDtypeStruct((n, width, lanes), bf16),
        ],
        scratch_shapes=[
            pltpu.VMEM((width, 2 * secs * side), bf16),
            pltpu.VMEM((width, 2 * secs * side), bf16),
            pltpu.VMEM((2 * n, width, lanes), f32),
        ],
        compiler_params=limit(8),
        name="pressures",
    )(cpl, *args)


def core_sum_kernel(near_ref, got_ref, own_ref, *send):
    groups = own_ref.shape[0]
    own_ref[...] = near_ref[0:groups] + got_ref[0:groups].astype(f32)
    for i, s in enumerate(send):
        r = slice((i + 1) * groups, (i + 2) * groups)
        s[...] = (near_ref[r] + got_ref[r].astype(f32)).astype(bf16)


def core_sum(near, got, secs):
    groups = near.shape[0] // secs
    shape = (groups,) + near.shape[1:]
    return pl.pallas_call(
        core_sum_kernel,
        in_specs=[VMEM] * 2,
        out_specs=[VMEM] * secs,
        out_shape=[jax.ShapeDtypeStruct(shape, f32)] + [jax.ShapeDtypeStruct(shape, bf16)] * (secs - 1),
        compiler_params=limit(4),
        name="core_sum",
    )(near, got)


def sec_sum_kernel(count, *refs):
    own, got, pt, outs = refs[0], refs[count:0:-1], refs[1 + count], refs[2 + count :]
    for j, out in enumerate(outs):
        value = own[j]
        for g in got:
            value = value + g[j].astype(f32)
        out[0] = value.astype(out.dtype)
        out[1] = pt[j].astype(out.dtype)


def sec_sum(own, got, pt):
    shape = (2,) + own.shape[1:]
    return pl.pallas_call(
        functools.partial(sec_sum_kernel, len(got)),
        in_specs=[VMEM] * (2 + len(got)),
        out_specs=[VMEM] * 4,
        out_shape=[jax.ShapeDtypeStruct(shape, f32)] + [jax.ShapeDtypeStruct(shape, bf16)] * 3,
        compiler_params=limit(4),
        name="sec_sum",
    )(own, *got[::-1], pt)


def output_kernel(r0, r3, r1, r2, loads_ref, press_ref, loads_t, press_t):
    half = loads_t.shape[0] // 2
    quarter = half // 4
    x, y, _, _ = place()
    for mask, r in enumerate((r0, r1, r2, r3)):
        at = pl.multiple_of(((x + 2 * y) ^ mask) * quarter, quarter)
        for part in range(2):
            rows = pl.ds(part * half + at, quarter)
            loads_t[rows, :] = r[0, part * quarter : (part + 1) * quarter, :].astype(f32)
            press_t[rows, :] = r[1, part * quarter : (part + 1) * quarter, :].astype(f32)
    loads_ref[...] = loads_t[...].T
    press_ref[...] = press_t[...].T.astype(bf16)


def outputs(parts):
    _, width, lanes = parts[0].shape
    cols = 4 * width
    return pl.pallas_call(
        output_kernel,
        in_specs=[VMEM] * 4,
        out_shape=[jax.ShapeDtypeStruct((lanes, cols), f32), jax.ShapeDtypeStruct((lanes, cols), bf16)],
        scratch_shapes=[pltpu.VMEM((cols, lanes), f32)] * 2,
        compiler_params=limit(4),
        name="outputs",
    )(parts[0], parts[3], parts[1], parts[2])


def on_device_fast(modal_loads, receptance, shapes, coupling, panel_coords, panel_areas):
    secs, tgts = lax.axis_size("sec"), lax.axis_size("tgt")
    device_count = lax.axis_size("blk") * tgts * secs
    pan_dev = panel_coords.shape[1]
    panels = float(pan_dev * device_count)
    width = modal_loads.shape[1] // 4
    blocks = receptance.shape[1] // shapes.shape[2]

    held = [
        pltpu.with_memory_space_constraint(a, pltpu.HBM)
        for a in (receptance, modal_loads, panel_coords, panel_areas[None, :], coupling)
    ]
    own, s1, s2, s3, geo = amplitude_parts(panels, *held)
    got = [exchange_plane(s, m) for m, s in ((1, s1), (2, s2), (3, s3))]
    modes = [shapes] + [exchange_plane(shapes, m) for m in (1, 2)]
    modes.append(exchange_plane(modes[1], 2))
    early = modes[1:3]
    modes = [m.reshape(pan_dev, -1) for m in modes]
    payload, cpl = amplitude_sum(early, own, geo, *got)
    near = [payload] + [exchange_sec(payload, m) for m in range(1, secs)]
    far = exchange_core(stack(near))
    targets = payload[-4 * GEO :, :]
    across = target_matrix(panels, targets)
    vel = velocities(panels, cpl, near, far, modes, width, blocks)
    mats = [helmholtz(across, n) for n in near] + [helmholtz(across, far, i, (vel,), 1.4) for i in range(secs)]
    mats = [m for pair in mats for m in pair]
    v_near = [vel] + [exchange_sec(vel, m) for m in range(1, secs)]
    v_far = exchange_core(stack(v_near))
    pt, n_near, n_far = pressures(cpl, v_near, v_far, mats, targets, modes, tgts)
    parts = core_sum(n_near, exchange_core(n_far), secs)
    sec_got = [exchange_sec(p, m) for m, p in zip(range(1, secs), parts[1:])]
    finals = sec_sum(parts[0], sec_got, pt)
    mine = [finals[0]] + [exchange_plane(f, m) for m, f in zip((1, 2, 3), finals[1:])]
    return outputs(mine)


def rotate_combine(leading, second):
    half_width = leading.shape[1] // 2
    return jnp.concatenate(
        [
            leading[:, :half_width] - second[:, half_width:],
            leading[:, half_width:] + second[:, :half_width],
        ],
        axis=1,
    )


def pressure_block(target_geometry, source_geometry, source_vel, total_panels):
    delta_x = target_geometry[0][:, None] - source_geometry[0][None, :]
    delta_y = target_geometry[1][:, None] - source_geometry[1][None, :]
    delta_z = target_geometry[2][:, None] - source_geometry[2][None, :]
    source_area = source_geometry[3][None, :]
    distance = jnp.sqrt(
        delta_x * delta_x + delta_y * delta_y + delta_z * delta_z + source_area / total_panels
    )
    weight = source_area / (distance * math.sqrt(total_panels))
    phase_angle = wave_number * distance
    kernel = jnp.concatenate(
        [
            (jnp.cos(phase_angle) * weight).astype(jnp.bfloat16),
            (jnp.sin(phase_angle) * weight).astype(jnp.bfloat16),
        ],
        axis=0,
    )
    products = lax.dot_general(
        kernel, source_vel, (((1,), (1,)), ((), ())), preferred_element_type=jnp.float32
    )
    target_count = target_geometry.shape[1]
    return rotate_combine(products[:target_count], products[target_count:])


def on_device_general(modal_loads, receptance, shapes, coupling, panel_coords, panel_areas):
    pan_dev = panel_coords.shape[1]
    case_width = modal_loads.shape[1]
    device_count = lax.axis_size("blk") * lax.axis_size("tgt") * lax.axis_size("sec")
    total_panels = float(pan_dev * device_count)
    row_share = receptance.shape[1]
    stacked = jnp.dot(
        receptance.reshape(2 * row_share, receptance.shape[2]),
        modal_loads,
        preferred_element_type=jnp.float32,
    )
    modal_sum = rotate_combine(stacked[:row_share], stacked[row_share:])
    modal_sum = lax.psum(modal_sum, "blk")
    amplitudes = lax.all_gather(modal_sum.astype(jnp.bfloat16), ("tgt", "sec"), axis=0, tiled=True)
    mode_block = shapes.shape[2]
    blocks = amplitudes.reshape(-1, mode_block, case_width)
    chosen = blocks[coupling]
    block_count = coupling.shape[0]
    shaped = shapes.reshape(block_count, -1, shapes.shape[1], mode_block)
    vel_t = (
        jnp.einsum("bpkm,bkmc->cbp", shaped, chosen, preferred_element_type=jnp.float32)
        .reshape(case_width, pan_dev)
        .astype(jnp.bfloat16)
    )
    geometry = jnp.concatenate([panel_coords, panel_areas[None, :]], axis=0)
    source_vel, source_geometry = (
        lax.all_gather(vel_t.astype(jnp.float32), ("tgt", "sec"), axis=1, tiled=True).astype(
            vel_t.dtype
        ),
        lax.all_gather(geometry, ("tgt", "sec"), axis=1, tiled=True),
    )
    target_geometry = lax.all_gather(geometry, "blk", axis=1, tiled=True)
    target_groups = pan_dev * lax.axis_size("blk") // pan_dev

    def single_block(block_index):
        target_block = lax.dynamic_slice_in_dim(target_geometry, block_index * pan_dev, pan_dev, 1)
        return pressure_block(target_block, source_geometry, source_vel, total_panels)

    stacked_terms = lax.map(single_block, jnp.arange(target_groups, dtype=jnp.int32))
    pressure_f = lax.psum_scatter(
        stacked_terms.reshape(pan_dev * lax.axis_size("blk"), case_width).astype(jnp.bfloat16),
        "blk",
        scatter_dimension=0,
        tiled=True,
    )
    weighted = (panel_areas[:, None] * pressure_f.astype(jnp.float32)).astype(jnp.bfloat16)
    contrib = jnp.einsum(
        "bpkm,bpc->bkmc",
        shaped,
        weighted.reshape(block_count, -1, case_width),
        preferred_element_type=jnp.float32,
    )
    onehot = (
        coupling[:, :, None] == jnp.arange(blocks.shape[0], dtype=jnp.int32)[None, None, :]
    ).astype(jnp.float32)
    partial_loads = jnp.einsum(
        "bkj,bkmc->jmc", onehot, contrib, precision=lax.Precision.HIGHEST
    ).reshape(-1, case_width)
    new_loads = lax.psum_scatter(
        partial_loads, ("blk", "tgt", "sec"), scatter_dimension=0, tiled=True
    )
    return (new_loads, pressure_f)


def on_device(modal_loads, receptance, shapes, coupling, panel_coords, panel_areas):
    lanes = 128
    secs = lax.axis_size("sec")
    mine = modal_loads.shape[0] * lax.axis_size("blk") // (lax.axis_size("blk") * lax.axis_size("tgt") * secs)
    fits = (
        lax.axis_size("blk") == 2
        and lax.axis_size("tgt") == 4
        and secs & (secs - 1) == 0
        and coupling.shape[0] == 1
        and shapes.shape[2] == lanes
        and panel_coords.shape[1] == lanes
        and modal_loads.shape[1] == lanes
        and mine == lanes
    )
    body = on_device_fast if fits else on_device_general
    return body(modal_loads, receptance, shapes, coupling, panel_coords, panel_areas)


def solution(mesh):
    in_specs = (
        P("blk", None),
        P(None, ("tgt", "sec"), "blk"),
        P(("blk", "tgt", "sec"), None, None),
        P(("blk", "tgt", "sec"), None),
        P(None, ("blk", "tgt", "sec")),
        P(("blk", "tgt", "sec")),
    )
    out_specs = (P(("blk", "tgt", "sec"), None), P(("blk", "tgt", "sec"), None))
    return jax.shard_map(
        on_device, mesh=mesh, in_specs=in_specs, out_specs=out_specs, check_vma=False
    )
```

```python
import functools
import math

import jax
import jax.numpy as jnp
import numpy as np
from jax import lax
from jax.experimental import pallas as pl
from jax.experimental.pallas import tpu as pltpu
from jax.sharding import PartitionSpec as P

wave_number = 40.0
turns = wave_number / (2.0 * math.pi)
bf16 = jnp.bfloat16
f32 = jnp.float32
AXES = ("blk", "tgt", "sec")
GEO = 16


def fit(values, terms):
    nodes = 0.125 + 0.125 * np.cos(np.pi * (np.arange(400) + 0.5) / 400)
    matrix = np.vander(nodes, terms, increasing=True)
    return [float(c) for c in np.linalg.lstsq(matrix, values(nodes), rcond=None)[0]]


sin_terms = fit(lambda u: math.sqrt(2.0) * np.sin(np.pi * np.sqrt(u)) / np.sqrt(u), 4)
cos_terms = fit(lambda u: math.sqrt(2.0) * np.cos(np.pi * np.sqrt(u)), 4)


def exchange_plane(x, mask):
    nb, nt = lax.axis_size("blk"), lax.axis_size("tgt")
    pairs = [
        (b * nt + t, (b ^ (mask & 1)) * nt + (t ^ (2 * (mask >> 1))))
        for b in range(nb)
        for t in range(nt)
    ]
    return lax.ppermute(x, ("blk", "tgt"), pairs)


def exchange_sec(x, mask):
    return lax.ppermute(x, "sec", [(s, s ^ mask) for s in range(lax.axis_size("sec"))])


def exchange_core(x):
    return lax.ppermute(x, "tgt", [(t, t ^ 1) for t in range(lax.axis_size("tgt"))])


VMEM = pl.BlockSpec(memory_space=pltpu.VMEM)
SMEM = pl.BlockSpec(memory_space=pltpu.SMEM)
HBM = pl.BlockSpec(memory_space=pltpu.HBM)


def place():
    t = lax.axis_index("tgt")
    return lax.axis_index("blk"), t >> 1, t & 1, lax.axis_index("sec")


def limit(mib):
    return pltpu.CompilerParams(vmem_limit_bytes=mib << 20)


def bits_of(n):
    return n.bit_length() - 1


def three_parts(x):
    first = x.astype(bf16).astype(f32)
    rest = x - first
    second = rest.astype(bf16).astype(f32)
    return first, second, rest - second


def amplitude_kernel(panels, r_hbm, l_hbm, xyz_hbm, area_hbm, cpl_hbm, own_ref, s1_ref, s2_ref, s3_ref, geo_ref, r_buf, l_buf, xyz, areas, cpl, amp_t, geo, sems):
    rows, lanes = r_buf.shape[1], 128
    blocks = rows // lanes
    small = [
        pltpu.make_async_copy(s, d, sems.at[i])
        for i, (s, d) in enumerate(((xyz_hbm, xyz), (area_hbm, areas), (cpl_hbm, cpl)))
    ]
    fetch_loads = pltpu.make_async_copy(l_hbm, l_buf, sems.at[3])
    fetch = [
        pltpu.make_async_copy(
            r_hbm.at[part, b * lanes : (b + 1) * lanes, :], r_buf.at[part, b * lanes : (b + 1) * lanes, :], sems.at[4 + 2 * b + part]
        )
        for b in range(blocks)
        for part in range(2)
    ]
    for copy in [fetch_loads] + small + fetch:
        copy.start()
    width = l_buf.shape[1]
    half = width // 2
    quarter = half // 4
    x, y, _, _ = place()
    mine = x + 2 * y
    fetch_loads.wait()
    for b in range(blocks):
        span = slice(b * lanes, (b + 1) * lanes)
        fetch[2 * b].wait()
        lead = jnp.dot(r_buf[0, span, :], l_buf[...], preferred_element_type=f32)
        fetch[2 * b + 1].wait()
        turned = pltpu.roll(jnp.dot(r_buf[1, span, :], l_buf[...], preferred_element_type=f32), half, 1)
        lane = lax.broadcasted_iota(jnp.int32, turned.shape, 1)
        amp_t[...] = (lead + jnp.where(lane < half, -turned, turned)).T
        for mask, out in enumerate((own_ref, s1_ref, s2_ref, s3_ref)):
            at = pl.multiple_of((mine ^ mask) * quarter, quarter)
            for part in range(2):
                r0 = (2 * b + part) * quarter
                out[r0 : r0 + quarter, :] = amp_t[pl.ds(part * half + at, quarter), :].astype(out.dtype)

    for copy in small:
        copy.wait()
    scaled = (xyz[...] - 0.5) * turns
    area = areas[...]
    norm = jnp.sum(scaled * scaled, axis=0, keepdims=True) + area * (turns * turns / panels)
    geo[...] = jnp.zeros_like(geo)
    for i, part in enumerate(three_parts(scaled)):
        geo[3 * i : 3 * i + 3, :] = part
    for i, part in enumerate(three_parts(norm)):
        geo[9 + i : 10 + i, :] = part
    for i, part in enumerate(three_parts(area)):
        geo[12 + i : 13 + i, :] = part
    geo[15:16, 0 : cpl.shape[1]] = cpl[...].astype(f32)
    packed = geo[...].astype(bf16)
    geo_ref[...] = packed
    for out in (s1_ref, s2_ref, s3_ref):
        out[out.shape[0] - GEO :, :] = packed


def amplitude_parts(panels, receptance, loads, xyz, area, coupling):
    _, rows, depth = receptance.shape
    width = loads.shape[1]
    blocks = rows // 128
    chunk = blocks * (width // 4)
    outs = [((chunk, 128), f32)] + [((chunk + GEO, 128), bf16)] * 3 + [((GEO, 128), bf16)]
    return pl.pallas_call(
        functools.partial(amplitude_kernel, panels),
        in_specs=[HBM] * 5,
        out_specs=[VMEM] * len(outs),
        out_shape=[jax.ShapeDtypeStruct(s, d) for s, d in outs],
        scratch_shapes=[
            pltpu.VMEM(receptance.shape, bf16),
            pltpu.VMEM(loads.shape, bf16),
            pltpu.VMEM(xyz.shape, f32),
            pltpu.VMEM(area.shape, f32),
            pltpu.VMEM(coupling.shape, jnp.int32),
            pltpu.VMEM((width, 128), f32),
            pltpu.VMEM((GEO, 128), f32),
            pltpu.SemaphoreType.DMA((4 + 2 * blocks,)),
        ],
        compiler_params=limit(12),
        cost_estimate=pl.CostEstimate(flops=4 * rows * depth * width, bytes_accessed=1, transcendentals=0),
        name="amplitude_parts",
    )(receptance, loads, xyz, area, coupling)


def amplitude_sum_kernel(count, *refs):
    own_ref, geo_ref, d_ref, x_ref, y_ref, out_ref, cpl_ref = refs[count:]
    n = own_ref.shape[0]
    out_ref[0:n, :] = (own_ref[...] + x_ref[0:n, :].astype(f32)).astype(bf16)
    out_ref[n : 2 * n, :] = (y_ref[0:n, :].astype(f32) + d_ref[0:n, :].astype(f32)).astype(bf16)
    geos = [geo_ref[...]] + [r[n:, :] for r in (x_ref, y_ref, d_ref)]
    for i, g in enumerate(geos):
        out_ref[2 * n + GEO * i : 2 * n + GEO * (i + 1), :] = g
        cpl_ref[i : i + 1, :] = g.astype(f32)[GEO - 1 :, :].astype(jnp.int32)


def amplitude_sum(early, own, geo, x, y, d):
    n = own.shape[0]
    return pl.pallas_call(
        functools.partial(amplitude_sum_kernel, len(early)),
        in_specs=[pl.BlockSpec(memory_space=pl.ANY)] * len(early) + [VMEM] * 5,
        out_specs=[VMEM] * 2,
        out_shape=[jax.ShapeDtypeStruct((2 * n + 4 * GEO, 128), bf16), jax.ShapeDtypeStruct((4, 128), jnp.int32)],
        compiler_params=limit(4),
        name="amplitude_sum",
    )(*early, own, geo, d, x, y)


def stack_kernel(*refs):
    for i, r in enumerate(refs[:-1]):
        refs[-1][i] = r[...]


def stack(parts):
    return pl.pallas_call(
        stack_kernel,
        in_specs=[VMEM] * len(parts),
        out_specs=VMEM,
        out_shape=jax.ShapeDtypeStruct((len(parts),) + parts[0].shape, parts[0].dtype),
        compiler_params=limit(4),
        name="stack",
    )(*parts)


def velocity_kernel(width, blocks, scale, secs, cpl, *refs):
    near, far_ref = refs[0:secs], refs[secs]
    modes, out_ref, table, picked = refs[secs + 1 : secs + 5], *refs[-3:]
    _, y, c, z = place()
    used = 2 * blocks * width
    for i in range(secs):
        table[0, i] = near[i][0:used, :]
        table[1, i] = far_ref[i, 0:used, :]
    sec_bits, block_bits = bits_of(secs), bits_of(blocks)
    count = modes[0].shape[1] // 128
    for j, m_ref in enumerate(modes):
        for k in range(count):
            b = cpl[j, k]
            h = b & (blocks - 1)
            s = (b >> block_bits) & (secs - 1)
            t = b >> (block_bits + sec_bits)
            row = pl.multiple_of((((((t >> 1) ^ y) << block_bits) + h) * width), width)
            picked[j, :, k * 128 : (k + 1) * 128] = table[(t & 1) ^ c, s ^ z, pl.ds(row, width), :]
    for j, m_ref in enumerate(modes):
        vel = lax.dot_general(picked[j], m_ref[...], (((1,), (1,)), ((), ())), preferred_element_type=f32)
        g = near[0][used + GEO * j : used + GEO * (j + 1), :].astype(f32)
        area = (g[12:13] + g[13:14] + g[14:15]) * scale
        out_ref[j] = (vel * area).astype(bf16)


def velocities(panels, cpl, near, far, modes, width, blocks):
    count, depth = modes[0].shape
    secs = len(near)
    return pl.pallas_call(
        functools.partial(velocity_kernel, width, blocks, turns / math.sqrt(panels), secs),
        in_specs=[VMEM] * (secs + 6),
        out_specs=VMEM,
        out_shape=jax.ShapeDtypeStruct((4, width, count), bf16),
        scratch_shapes=[
            pltpu.VMEM((2, secs, 2 * blocks * width, 128), bf16),
            pltpu.VMEM((4, width, depth), bf16),
        ],
        compiler_params=limit(6),
        name="velocities",
    )(cpl, *near, far, *modes)


def target_kernel(panels, tgt_ref, out_ref, mat):
    lanes = tgt_ref.shape[1]
    mat[...] = jnp.zeros_like(mat)
    for j in range(tgt_ref.shape[0] // GEO):
        g = tgt_ref[j * GEO : (j + 1) * GEO, :].astype(f32)
        area = g[12:13] + g[13:14] + g[14:15]
        norm = g[9:10] + g[10:11] + g[11:12] - area * (turns * turns / panels)
        col = slice(j * lanes, (j + 1) * lanes)
        for a in range(3):
            for b in range(3):
                mat[GEO * a + 3 * b : GEO * a + 3 * b + 3, col] = -2.0 * g[3 * a : 3 * a + 3]
        mat[9:12, col] = jnp.ones((3, lanes), f32)
        for i, part in enumerate(three_parts(norm)):
            mat[3 * GEO + i : 3 * GEO + i + 1, col] = part
    out_ref[...] = mat[...].astype(bf16)


def target_matrix(panels, geo):
    side = geo.shape[0] // GEO * geo.shape[1]
    return pl.pallas_call(
        functools.partial(target_kernel, panels),
        in_specs=[VMEM],
        out_specs=VMEM,
        out_shape=jax.ShapeDtypeStruct((4 * GEO, side), bf16),
        scratch_shapes=[pltpu.VMEM((4 * GEO, side), f32)],
        compiler_params=limit(4),
        name="target_matrix",
    )(geo)


def helmholtz_kernel(at, tgt_ref, src_ref, *refs):
    re_ref, im_ref = refs[-2:]
    src = src_ref if at is None else src_ref.at[at]
    side = tgt_ref.shape[1]
    first = src.shape[0] - side // 128 * GEO
    c0, c1, c2 = (c / cos_terms[3] for c in cos_terms[:3])
    strip = 128
    for r in range(0, side, strip):
        at_row = first + r // 128 * GEO
        one = src[at_row : at_row + GEO, :]
        full = jnp.concatenate([one, one, one, jnp.ones_like(one)], axis=0)
        square = lax.dot_general(full, tgt_ref[...], (((0,), (0,)), ((), ())), preferred_element_type=f32)
        inverse = lax.rsqrt(square)
        t = square * inverse
        f = t - jnp.round(t)
        u = f * f
        s = (((sin_terms[3] * u + sin_terms[2]) * u + sin_terms[1]) * u + sin_terms[0]) * f
        c = ((u + c2) * u + c1) * u + c0
        part = s * inverse
        re_ref[r : r + strip, :] = (inverse - s * part).astype(bf16)
        im_ref[r : r + strip, :] = (c * part).astype(bf16)


def helmholtz(targets, payload, at=None, after=(), cost=1.0):
    side = targets.shape[1]
    return pl.pallas_call(
        functools.partial(helmholtz_kernel, at),
        in_specs=[VMEM] * 2 + [pl.BlockSpec(memory_space=pl.ANY)] * len(after),
        out_specs=[VMEM] * 2,
        out_shape=[jax.ShapeDtypeStruct((side, side), bf16)] * 2,
        compiler_params=limit(4),
        cost_estimate=pl.CostEstimate(flops=int(cost * 3900 * side * side), bytes_accessed=1, transcendentals=0),
        name="helmholtz",
    )(targets, payload, *after)


def pressure_kernel(secs, tgt_n, cpl, *refs):
    v_near, v_far = refs[0:secs], refs[secs]
    mats = refs[secs + 1 : 5 * secs + 1]
    geo_ref, modes = refs[5 * secs + 1], refs[5 * secs + 2 : 5 * secs + 6]
    pt_ref, near_ref, far_ref, lead, turned, total = refs[5 * secs + 6 :]
    groups, width, lanes = v_near[0].shape
    half = width // 2
    side = groups * lanes
    for i in range(2 * secs):
        for j in range(groups):
            v = v_near[i][j] if i < secs else v_far[i - secs, j]
            col = slice(i * side + j * lanes, i * side + (j + 1) * lanes)
            lead[:, col] = v
            turned[0:half, col] = -v[half:]
            turned[half:, col] = v[0:half]
    re = im = 0.0
    for i in range(2 * secs):
        col = slice(i * side, (i + 1) * side)
        re += jnp.dot(lead[:, col], mats[2 * i][...], preferred_element_type=f32)
        im += jnp.dot(turned[:, col], mats[2 * i + 1][...], preferred_element_type=f32)
    p = (re + im * cos_terms[3]).astype(bf16)
    total[...] = jnp.zeros_like(total)
    x, y, c, z = place()
    sec_bits, tgt_bits = bits_of(secs), bits_of(tgt_n)
    for j, m_ref in enumerate(modes):
        pj = p[:, j * lanes : (j + 1) * lanes]
        pt_ref[j] = pj
        g = geo_ref[j * GEO : (j + 1) * GEO, :].astype(f32)
        weighted = (pj.astype(f32) * (g[12:13] + g[13:14] + g[14:15])).astype(bf16)
        terms = jnp.dot(weighted, m_ref[...], preferred_element_type=f32)
        for k in range(m_ref.shape[1] // lanes):
            b = cpl[j, k]
            s = b & (secs - 1)
            t = (b >> sec_bits) & (tgt_n - 1)
            xb = b >> (sec_bits + tgt_bits)
            at = ((((t & 1) ^ c) * secs + (s ^ z)) * groups) + (xb ^ x) + 2 * ((t >> 1) ^ y)
            total[at] += terms[:, k * lanes : (k + 1) * lanes]
    n = near_ref.shape[0]
    near_ref[...] = total[0:n]
    far_ref[...] = total[n:].astype(bf16)


def pressures(cpl, v_near, v_far, mats, geo, modes, tgt_n):
    secs = len(v_near)
    groups, width, lanes = v_near[0].shape
    side = groups * lanes
    n = secs * groups
    args = [*v_near, v_far, *mats, geo, *modes]
    return pl.pallas_call(
        functools.partial(pressure_kernel, secs, tgt_n),
        in_specs=[VMEM] * (1 + len(args)),
        out_specs=[VMEM] * 3,
        out_shape=[
            jax.ShapeDtypeStruct((groups, width, lanes), bf16),
            jax.ShapeDtypeStruct((n, width, lanes), f32),
            jax.ShapeDtypeStruct((n, width, lanes), bf16),
        ],
        scratch_shapes=[
            pltpu.VMEM((width, 2 * secs * side), bf16),
            pltpu.VMEM((width, 2 * secs * side), bf16),
            pltpu.VMEM((2 * n, width, lanes), f32),
        ],
        compiler_params=limit(8),
        name="pressures",
    )(cpl, *args)


def core_sum_kernel(near_ref, got_ref, own_ref, *send):
    groups = own_ref.shape[0]
    own_ref[...] = near_ref[0:groups] + got_ref[0:groups].astype(f32)
    for i, s in enumerate(send):
        r = slice((i + 1) * groups, (i + 2) * groups)
        s[...] = (near_ref[r] + got_ref[r].astype(f32)).astype(bf16)


def core_sum(near, got, secs):
    groups = near.shape[0] // secs
    shape = (groups,) + near.shape[1:]
    return pl.pallas_call(
        core_sum_kernel,
        in_specs=[VMEM] * 2,
        out_specs=[VMEM] * secs,
        out_shape=[jax.ShapeDtypeStruct(shape, f32)] + [jax.ShapeDtypeStruct(shape, bf16)] * (secs - 1),
        compiler_params=limit(4),
        name="core_sum",
    )(near, got)


def sec_sum_kernel(count, *refs):
    own, got, pt, outs = refs[0], refs[count:0:-1], refs[1 + count], refs[2 + count :]
    for j, out in enumerate(outs):
        value = own[j]
        for g in got:
            value = value + g[j].astype(f32)
        out[0] = value.astype(out.dtype)
        out[1] = pt[j].astype(out.dtype)


def sec_sum(own, got, pt):
    shape = (2,) + own.shape[1:]
    return pl.pallas_call(
        functools.partial(sec_sum_kernel, len(got)),
        in_specs=[VMEM] * (2 + len(got)),
        out_specs=[VMEM] * 4,
        out_shape=[jax.ShapeDtypeStruct(shape, f32)] + [jax.ShapeDtypeStruct(shape, bf16)] * 3,
        compiler_params=limit(4),
        name="sec_sum",
    )(own, *got[::-1], pt)


def output_kernel(r0, r3, r1, r2, loads_ref, press_ref, loads_t, press_t):
    half = loads_t.shape[0] // 2
    quarter = half // 4
    x, y, _, _ = place()
    for mask, r in enumerate((r0, r1, r2, r3)):
        at = pl.multiple_of(((x + 2 * y) ^ mask) * quarter, quarter)
        for part in range(2):
            rows = pl.ds(part * half + at, quarter)
            loads_t[rows, :] = r[0, part * quarter : (part + 1) * quarter, :].astype(f32)
            press_t[rows, :] = r[1, part * quarter : (part + 1) * quarter, :].astype(f32)
    loads_ref[...] = loads_t[...].T
    press_ref[...] = press_t[...].T.astype(bf16)


def outputs(parts):
    _, width, lanes = parts[0].shape
    cols = 4 * width
    return pl.pallas_call(
        output_kernel,
        in_specs=[VMEM] * 4,
        out_shape=[jax.ShapeDtypeStruct((lanes, cols), f32), jax.ShapeDtypeStruct((lanes, cols), bf16)],
        scratch_shapes=[pltpu.VMEM((cols, lanes), f32)] * 2,
        compiler_params=limit(4),
        name="outputs",
    )(parts[0], parts[3], parts[1], parts[2])


def on_device_fast(modal_loads, receptance, shapes, coupling, panel_coords, panel_areas):
    secs, tgts = lax.axis_size("sec"), lax.axis_size("tgt")
    device_count = lax.axis_size("blk") * tgts * secs
    pan_dev = panel_coords.shape[1]
    panels = float(pan_dev * device_count)
    width = modal_loads.shape[1] // 4
    blocks = receptance.shape[1] // shapes.shape[2]

    held = [
        pltpu.with_memory_space_constraint(a, pltpu.HBM)
        for a in (receptance, modal_loads, panel_coords, panel_areas[None, :], coupling)
    ]
    own, s1, s2, s3, geo = amplitude_parts(panels, *held)
    got = [exchange_plane(s, m) for m, s in ((1, s1), (2, s2), (3, s3))]
    modes = [shapes] + [exchange_plane(shapes, m) for m in (1, 2)]
    modes.append(exchange_plane(modes[1], 2))
    early = modes[1:3]
    modes = [m.reshape(pan_dev, -1) for m in modes]
    payload, cpl = amplitude_sum(early, own, geo, *got)
    near = [payload] + [exchange_sec(payload, m) for m in range(1, secs)]
    far = exchange_core(stack(near))
    targets = payload[-4 * GEO :, :]
    across = target_matrix(panels, targets)
    vel = velocities(panels, cpl, near, far, modes, width, blocks)
    mats = [helmholtz(across, n) for n in near] + [helmholtz(across, far, i, (vel,), 1.4) for i in range(secs)]
    mats = [m for pair in mats for m in pair]
    v_near = [vel] + [exchange_sec(vel, m) for m in range(1, secs)]
    v_far = exchange_core(stack(v_near))
    pt, n_near, n_far = pressures(cpl, v_near, v_far, mats, targets, modes, tgts)
    parts = core_sum(n_near, exchange_core(n_far), secs)
    sec_got = [exchange_sec(p, m) for m, p in zip(range(1, secs), parts[1:])]
    finals = sec_sum(parts[0], sec_got, pt)
    mine = [finals[0]] + [exchange_plane(f, m) for m, f in zip((1, 2, 3), finals[1:])]
    return outputs(mine)


def rotate_combine(leading, second):
    half_width = leading.shape[1] // 2
    return jnp.concatenate(
        [
            leading[:, :half_width] - second[:, half_width:],
            leading[:, half_width:] + second[:, :half_width],
        ],
        axis=1,
    )


def pressure_block(target_geometry, source_geometry, source_vel, total_panels):
    delta_x = target_geometry[0][:, None] - source_geometry[0][None, :]
    delta_y = target_geometry[1][:, None] - source_geometry[1][None, :]
    delta_z = target_geometry[2][:, None] - source_geometry[2][None, :]
    source_area = source_geometry[3][None, :]
    distance = jnp.sqrt(
        delta_x * delta_x + delta_y * delta_y + delta_z * delta_z + source_area / total_panels
    )
    weight = source_area / (distance * math.sqrt(total_panels))
    phase_angle = wave_number * distance
    kernel = jnp.concatenate(
        [
            (jnp.cos(phase_angle) * weight).astype(jnp.bfloat16),
            (jnp.sin(phase_angle) * weight).astype(jnp.bfloat16),
        ],
        axis=0,
    )
    products = lax.dot_general(
        kernel, source_vel, (((1,), (1,)), ((), ())), preferred_element_type=jnp.float32
    )
    target_count = target_geometry.shape[1]
    return rotate_combine(products[:target_count], products[target_count:])


def on_device_general(modal_loads, receptance, shapes, coupling, panel_coords, panel_areas):
    pan_dev = panel_coords.shape[1]
    case_width = modal_loads.shape[1]
    device_count = lax.axis_size("blk") * lax.axis_size("tgt") * lax.axis_size("sec")
    total_panels = float(pan_dev * device_count)
    row_share = receptance.shape[1]
    stacked = jnp.dot(
        receptance.reshape(2 * row_share, receptance.shape[2]),
        modal_loads,
        preferred_element_type=jnp.float32,
    )
    modal_sum = rotate_combine(stacked[:row_share], stacked[row_share:])
    modal_sum = lax.psum(modal_sum, "blk")
    amplitudes = lax.all_gather(modal_sum.astype(jnp.bfloat16), ("tgt", "sec"), axis=0, tiled=True)
    mode_block = shapes.shape[2]
    blocks = amplitudes.reshape(-1, mode_block, case_width)
    chosen = blocks[coupling]
    block_count = coupling.shape[0]
    shaped = shapes.reshape(block_count, -1, shapes.shape[1], mode_block)
    vel_t = (
        jnp.einsum("bpkm,bkmc->cbp", shaped, chosen, preferred_element_type=jnp.float32)
        .reshape(case_width, pan_dev)
        .astype(jnp.bfloat16)
    )
    geometry = jnp.concatenate([panel_coords, panel_areas[None, :]], axis=0)
    source_vel, source_geometry = (
        lax.all_gather(vel_t.astype(jnp.float32), ("tgt", "sec"), axis=1, tiled=True).astype(
            vel_t.dtype
        ),
        lax.all_gather(geometry, ("tgt", "sec"), axis=1, tiled=True),
    )
    target_geometry = lax.all_gather(geometry, "blk", axis=1, tiled=True)
    target_groups = pan_dev * lax.axis_size("blk") // pan_dev

    def single_block(block_index):
        target_block = lax.dynamic_slice_in_dim(target_geometry, block_index * pan_dev, pan_dev, 1)
        return pressure_block(target_block, source_geometry, source_vel, total_panels)

    stacked_terms = lax.map(single_block, jnp.arange(target_groups, dtype=jnp.int32))
    pressure_f = lax.psum_scatter(
        stacked_terms.reshape(pan_dev * lax.axis_size("blk"), case_width).astype(jnp.bfloat16),
        "blk",
        scatter_dimension=0,
        tiled=True,
    )
    weighted = (panel_areas[:, None] * pressure_f.astype(jnp.float32)).astype(jnp.bfloat16)
    contrib = jnp.einsum(
        "bpkm,bpc->bkmc",
        shaped,
        weighted.reshape(block_count, -1, case_width),
        preferred_element_type=jnp.float32,
    )
    onehot = (
        coupling[:, :, None] == jnp.arange(blocks.shape[0], dtype=jnp.int32)[None, None, :]
    ).astype(jnp.float32)
    partial_loads = jnp.einsum(
        "bkj,bkmc->jmc", onehot, contrib, precision=lax.Precision.HIGHEST
    ).reshape(-1, case_width)
    new_loads = lax.psum_scatter(
        partial_loads, ("blk", "tgt", "sec"), scatter_dimension=0, tiled=True
    )
    return (new_loads, pressure_f)


def on_device(modal_loads, receptance, shapes, coupling, panel_coords, panel_areas):
    lanes = 128
    secs = lax.axis_size("sec")
    mine = modal_loads.shape[0] * lax.axis_size("blk") // (lax.axis_size("blk") * lax.axis_size("tgt") * secs)
    fits = (
        lax.axis_size("blk") == 2
        and lax.axis_size("tgt") == 4
        and secs & (secs - 1) == 0
        and coupling.shape[0] == 1
        and shapes.shape[2] == lanes
        and panel_coords.shape[1] == lanes
        and modal_loads.shape[1] == lanes
        and mine == lanes
    )
    body = on_device_fast if fits else on_device_general
    return body(modal_loads, receptance, shapes, coupling, panel_coords, panel_areas)


def solution(mesh):
    in_specs = (
        P("blk", None),
        P(None, ("tgt", "sec"), "blk"),
        P(("blk", "tgt", "sec"), None, None),
        P(("blk", "tgt", "sec"), None),
        P(None, ("blk", "tgt", "sec")),
        P(("blk", "tgt", "sec")),
    )
    out_specs = (P(("blk", "tgt", "sec"), None), P(("blk", "tgt", "sec"), None))
    return jax.shard_map(
        on_device, mesh=mesh, in_specs=in_specs, out_specs=out_specs, check_vma=False
    )
```

```python
import functools
import math

import jax
import jax.numpy as jnp
import numpy as np
from jax import lax
from jax.experimental import pallas as pl
from jax.experimental.pallas import tpu as pltpu
from jax.sharding import PartitionSpec as P

wave_number = 40.0
turns = wave_number / (2.0 * math.pi)
bf16 = jnp.bfloat16
f32 = jnp.float32
AXES = ("blk", "tgt", "sec")
GEO = 16


def fit(values, terms):
    nodes = 0.125 + 0.125 * np.cos(np.pi * (np.arange(400) + 0.5) / 400)
    matrix = np.vander(nodes, terms, increasing=True)
    return [float(c) for c in np.linalg.lstsq(matrix, values(nodes), rcond=None)[0]]


sin_terms = fit(lambda u: math.sqrt(2.0) * np.sin(np.pi * np.sqrt(u)) / np.sqrt(u), 4)
cos_terms = fit(lambda u: math.sqrt(2.0) * np.cos(np.pi * np.sqrt(u)), 4)


def exchange_plane(x, mask):
    nb, nt = lax.axis_size("blk"), lax.axis_size("tgt")
    pairs = [
        (b * nt + t, (b ^ (mask & 1)) * nt + (t ^ (2 * (mask >> 1))))
        for b in range(nb)
        for t in range(nt)
    ]
    return lax.ppermute(x, ("blk", "tgt"), pairs)


def exchange_sec(x, mask):
    return lax.ppermute(x, "sec", [(s, s ^ mask) for s in range(lax.axis_size("sec"))])


def exchange_core(x):
    return lax.ppermute(x, "tgt", [(t, t ^ 1) for t in range(lax.axis_size("tgt"))])


VMEM = pl.BlockSpec(memory_space=pltpu.VMEM)
SMEM = pl.BlockSpec(memory_space=pltpu.SMEM)
HBM = pl.BlockSpec(memory_space=pltpu.HBM)


def place():
    t = lax.axis_index("tgt")
    return lax.axis_index("blk"), t >> 1, t & 1, lax.axis_index("sec")


def limit(mib):
    return pltpu.CompilerParams(vmem_limit_bytes=mib << 20)


def bits_of(n):
    return n.bit_length() - 1


def three_parts(x):
    first = x.astype(bf16).astype(f32)
    rest = x - first
    second = rest.astype(bf16).astype(f32)
    return first, second, rest - second


def amplitude_kernel(panels, r_hbm, l_hbm, xyz_hbm, area_hbm, cpl_hbm, own_ref, s1_ref, s2_ref, s3_ref, geo_ref, r_buf, l_buf, xyz, areas, cpl, amp_t, geo, sems):
    rows, lanes = r_buf.shape[1], 128
    blocks = rows // lanes
    small = [
        pltpu.make_async_copy(s, d, sems.at[i])
        for i, (s, d) in enumerate(((xyz_hbm, xyz), (area_hbm, areas), (cpl_hbm, cpl)))
    ]
    fetch_loads = pltpu.make_async_copy(l_hbm, l_buf, sems.at[3])
    fetch = [
        pltpu.make_async_copy(
            r_hbm.at[part, b * lanes : (b + 1) * lanes, :], r_buf.at[part, b * lanes : (b + 1) * lanes, :], sems.at[4 + 2 * b + part]
        )
        for b in range(blocks)
        for part in range(2)
    ]
    for copy in [fetch_loads] + small + fetch:
        copy.start()
    width = l_buf.shape[1]
    half = width // 2
    quarter = half // 4
    x, y, _, _ = place()
    mine = x + 2 * y
    fetch_loads.wait()
    for b in range(blocks):
        span = slice(b * lanes, (b + 1) * lanes)
        fetch[2 * b].wait()
        lead = jnp.dot(r_buf[0, span, :], l_buf[...], preferred_element_type=f32)
        fetch[2 * b + 1].wait()
        turned = pltpu.roll(jnp.dot(r_buf[1, span, :], l_buf[...], preferred_element_type=f32), half, 1)
        lane = lax.broadcasted_iota(jnp.int32, turned.shape, 1)
        amp_t[...] = (lead + jnp.where(lane < half, -turned, turned)).T
        for mask, out in enumerate((own_ref, s1_ref, s2_ref, s3_ref)):
            at = pl.multiple_of((mine ^ mask) * quarter, quarter)
            for part in range(2):
                r0 = (2 * b + part) * quarter
                out[r0 : r0 + quarter, :] = amp_t[pl.ds(part * half + at, quarter), :].astype(out.dtype)

    for copy in small:
        copy.wait()
    scaled = (xyz[...] - 0.5) * turns
    area = areas[...]
    norm = jnp.sum(scaled * scaled, axis=0, keepdims=True) + area * (turns * turns / panels)
    geo[...] = jnp.zeros_like(geo)
    for i, part in enumerate(three_parts(scaled)):
        geo[3 * i : 3 * i + 3, :] = part
    for i, part in enumerate(three_parts(norm)):
        geo[9 + i : 10 + i, :] = part
    for i, part in enumerate(three_parts(area)):
        geo[12 + i : 13 + i, :] = part
    geo[15:16, 0 : cpl.shape[1]] = cpl[...].astype(f32)
    packed = geo[...].astype(bf16)
    geo_ref[...] = packed
    for out in (s1_ref, s2_ref, s3_ref):
        out[out.shape[0] - GEO :, :] = packed


def amplitude_parts(panels, receptance, loads, xyz, area, coupling):
    _, rows, depth = receptance.shape
    width = loads.shape[1]
    blocks = rows // 128
    chunk = blocks * (width // 4)
    outs = [((chunk, 128), f32)] + [((chunk + GEO, 128), bf16)] * 3 + [((GEO, 128), bf16)]
    return pl.pallas_call(
        functools.partial(amplitude_kernel, panels),
        in_specs=[HBM] * 5,
        out_specs=[VMEM] * len(outs),
        out_shape=[jax.ShapeDtypeStruct(s, d) for s, d in outs],
        scratch_shapes=[
            pltpu.VMEM(receptance.shape, bf16),
            pltpu.VMEM(loads.shape, bf16),
            pltpu.VMEM(xyz.shape, f32),
            pltpu.VMEM(area.shape, f32),
            pltpu.VMEM(coupling.shape, jnp.int32),
            pltpu.VMEM((width, 128), f32),
            pltpu.VMEM((GEO, 128), f32),
            pltpu.SemaphoreType.DMA((4 + 2 * blocks,)),
        ],
        compiler_params=limit(12),
        cost_estimate=pl.CostEstimate(flops=4 * rows * depth * width, bytes_accessed=1, transcendentals=0),
        name="amplitude_parts",
    )(receptance, loads, xyz, area, coupling)


def amplitude_sum_kernel(count, *refs):
    own_ref, geo_ref, x_ref, y_ref, d_ref, out_ref, cpl_ref = refs[count:]
    n = own_ref.shape[0]
    out_ref[0:n, :] = (own_ref[...] + x_ref[0:n, :].astype(f32)).astype(bf16)
    out_ref[n : 2 * n, :] = (y_ref[0:n, :].astype(f32) + d_ref[0:n, :].astype(f32)).astype(bf16)
    geos = [geo_ref[...]] + [r[n:, :] for r in (x_ref, y_ref, d_ref)]
    for i, g in enumerate(geos):
        out_ref[2 * n + GEO * i : 2 * n + GEO * (i + 1), :] = g
        cpl_ref[i : i + 1, :] = g.astype(f32)[GEO - 1 :, :].astype(jnp.int32)


def amplitude_sum(early, own, geo, x, y, d):
    n = own.shape[0]
    return pl.pallas_call(
        functools.partial(amplitude_sum_kernel, 0),
        in_specs=[pl.BlockSpec(memory_space=pl.ANY)] * len(early) + [VMEM] * 5,
        out_specs=[VMEM] * 2,
        out_shape=[jax.ShapeDtypeStruct((2 * n + 4 * GEO, 128), bf16), jax.ShapeDtypeStruct((4, 128), jnp.int32)],
        compiler_params=limit(4),
        name="amplitude_sum",
    )(own, geo, x, y, d)


def stack_kernel(*refs):
    for i, r in enumerate(refs[:-1]):
        refs[-1][i] = r[...]


def stack(parts):
    return pl.pallas_call(
        stack_kernel,
        in_specs=[VMEM] * len(parts),
        out_specs=VMEM,
        out_shape=jax.ShapeDtypeStruct((len(parts),) + parts[0].shape, parts[0].dtype),
        compiler_params=limit(4),
        name="stack",
    )(*parts)


def velocity_kernel(width, blocks, scale, secs, cpl, *refs):
    near, far_ref = refs[0:secs], refs[secs]
    modes, out_ref, table, picked = refs[secs + 1 : secs + 5], *refs[-3:]
    _, y, c, z = place()
    used = 2 * blocks * width
    for i in range(secs):
        table[0, i] = near[i][0:used, :]
        table[1, i] = far_ref[i, 0:used, :]
    sec_bits, block_bits = bits_of(secs), bits_of(blocks)
    count = modes[0].shape[1] // 128
    for j, m_ref in enumerate(modes):
        for k in range(count):
            b = cpl[j, k]
            h = b & (blocks - 1)
            s = (b >> block_bits) & (secs - 1)
            t = b >> (block_bits + sec_bits)
            row = pl.multiple_of((((((t >> 1) ^ y) << block_bits) + h) * width), width)
            picked[j, :, k * 128 : (k + 1) * 128] = table[(t & 1) ^ c, s ^ z, pl.ds(row, width), :]
    for j, m_ref in enumerate(modes):
        vel = lax.dot_general(picked[j], m_ref[...], (((1,), (1,)), ((), ())), preferred_element_type=f32)
        g = near[0][used + GEO * j : used + GEO * (j + 1), :].astype(f32)
        area = (g[12:13] + g[13:14] + g[14:15]) * scale
        out_ref[j] = (vel * area).astype(bf16)


def velocities(panels, cpl, near, far, modes, width, blocks):
    count, depth = modes[0].shape
    secs = len(near)
    return pl.pallas_call(
        functools.partial(velocity_kernel, width, blocks, turns / math.sqrt(panels), secs),
        in_specs=[VMEM] * (secs + 6),
        out_specs=VMEM,
        out_shape=jax.ShapeDtypeStruct((4, width, count), bf16),
        scratch_shapes=[
            pltpu.VMEM((2, secs, 2 * blocks * width, 128), bf16),
            pltpu.VMEM((4, width, depth), bf16),
        ],
        compiler_params=limit(6),
        name="velocities",
    )(cpl, *near, far, *modes)


def target_kernel(panels, tgt_ref, out_ref, mat):
    lanes = tgt_ref.shape[1]
    mat[...] = jnp.zeros_like(mat)
    for j in range(tgt_ref.shape[0] // GEO):
        g = tgt_ref[j * GEO : (j + 1) * GEO, :].astype(f32)
        area = g[12:13] + g[13:14] + g[14:15]
        norm = g[9:10] + g[10:11] + g[11:12] - area * (turns * turns / panels)
        col = slice(j * lanes, (j + 1) * lanes)
        for a in range(3):
            for b in range(3):
                mat[GEO * a + 3 * b : GEO * a + 3 * b + 3, col] = -2.0 * g[3 * a : 3 * a + 3]
        mat[9:12, col] = jnp.ones((3, lanes), f32)
        for i, part in enumerate(three_parts(norm)):
            mat[3 * GEO + i : 3 * GEO + i + 1, col] = part
    out_ref[...] = mat[...].astype(bf16)


def target_matrix(panels, geo):
    side = geo.shape[0] // GEO * geo.shape[1]
    return pl.pallas_call(
        functools.partial(target_kernel, panels),
        in_specs=[VMEM],
        out_specs=VMEM,
        out_shape=jax.ShapeDtypeStruct((4 * GEO, side), bf16),
        scratch_shapes=[pltpu.VMEM((4 * GEO, side), f32)],
        compiler_params=limit(4),
        name="target_matrix",
    )(geo)


def helmholtz_kernel(at, tgt_ref, src_ref, *refs):
    re_ref, im_ref = refs[-2:]
    src = src_ref if at is None else src_ref.at[at]
    side = tgt_ref.shape[1]
    first = src.shape[0] - side // 128 * GEO
    c0, c1, c2 = (c / cos_terms[3] for c in cos_terms[:3])
    strip = 128
    for r in range(0, side, strip):
        at_row = first + r // 128 * GEO
        one = src[at_row : at_row + GEO, :]
        full = jnp.concatenate([one, one, one, jnp.ones_like(one)], axis=0)
        square = lax.dot_general(full, tgt_ref[...], (((0,), (0,)), ((), ())), preferred_element_type=f32)
        inverse = lax.rsqrt(square)
        t = square * inverse
        f = t - jnp.round(t)
        u = f * f
        s = (((sin_terms[3] * u + sin_terms[2]) * u + sin_terms[1]) * u + sin_terms[0]) * f
        c = ((u + c2) * u + c1) * u + c0
        part = s * inverse
        re_ref[r : r + strip, :] = (inverse - s * part).astype(bf16)
        im_ref[r : r + strip, :] = (c * part).astype(bf16)


def helmholtz(targets, payload, at=None, after=(), cost=1.0):
    side = targets.shape[1]
    return pl.pallas_call(
        functools.partial(helmholtz_kernel, at),
        in_specs=[VMEM] * 2 + [pl.BlockSpec(memory_space=pl.ANY)] * len(after),
        out_specs=[VMEM] * 2,
        out_shape=[jax.ShapeDtypeStruct((side, side), bf16)] * 2,
        compiler_params=limit(4),
        cost_estimate=pl.CostEstimate(flops=int(cost * 3900 * side * side), bytes_accessed=1, transcendentals=0),
        name="helmholtz",
    )(targets, payload, *after)


def pressure_kernel(secs, tgt_n, cpl, *refs):
    v_near, v_far = refs[0:secs], refs[secs]
    mats = refs[secs + 1 : 5 * secs + 1]
    geo_ref, modes = refs[5 * secs + 1], refs[5 * secs + 2 : 5 * secs + 6]
    pt_ref, near_ref, far_ref, lead, turned, total = refs[5 * secs + 6 :]
    groups, width, lanes = v_near[0].shape
    half = width // 2
    side = groups * lanes
    for i in range(2 * secs):
        for j in range(groups):
            v = v_near[i][j] if i < secs else v_far[i - secs, j]
            col = slice(i * side + j * lanes, i * side + (j + 1) * lanes)
            lead[:, col] = v
            turned[0:half, col] = -v[half:]
            turned[half:, col] = v[0:half]
    re = im = 0.0
    for i in range(2 * secs):
        col = slice(i * side, (i + 1) * side)
        re += jnp.dot(lead[:, col], mats[2 * i][...], preferred_element_type=f32)
        im += jnp.dot(turned[:, col], mats[2 * i + 1][...], preferred_element_type=f32)
    p = (re + im * cos_terms[3]).astype(bf16)
    total[...] = jnp.zeros_like(total)
    x, y, c, z = place()
    sec_bits, tgt_bits = bits_of(secs), bits_of(tgt_n)
    for j, m_ref in enumerate(modes):
        pj = p[:, j * lanes : (j + 1) * lanes]
        pt_ref[j] = pj
        g = geo_ref[j * GEO : (j + 1) * GEO, :].astype(f32)
        weighted = (pj.astype(f32) * (g[12:13] + g[13:14] + g[14:15])).astype(bf16)
        terms = jnp.dot(weighted, m_ref[...], preferred_element_type=f32)
        for k in range(m_ref.shape[1] // lanes):
            b = cpl[j, k]
            s = b & (secs - 1)
            t = (b >> sec_bits) & (tgt_n - 1)
            xb = b >> (sec_bits + tgt_bits)
            at = ((((t & 1) ^ c) * secs + (s ^ z)) * groups) + (xb ^ x) + 2 * ((t >> 1) ^ y)
            total[at] += terms[:, k * lanes : (k + 1) * lanes]
    n = near_ref.shape[0]
    near_ref[...] = total[0:n]
    far_ref[...] = total[n:].astype(bf16)


def pressures(cpl, v_near, v_far, mats, geo, modes, tgt_n):
    secs = len(v_near)
    groups, width, lanes = v_near[0].shape
    side = groups * lanes
    n = secs * groups
    args = [*v_near, v_far, *mats, geo, *modes]
    return pl.pallas_call(
        functools.partial(pressure_kernel, secs, tgt_n),
        in_specs=[VMEM] * (1 + len(args)),
        out_specs=[VMEM] * 3,
        out_shape=[
            jax.ShapeDtypeStruct((groups, width, lanes), bf16),
            jax.ShapeDtypeStruct((n, width, lanes), f32),
            jax.ShapeDtypeStruct((n, width, lanes), bf16),
        ],
        scratch_shapes=[
            pltpu.VMEM((width, 2 * secs * side), bf16),
            pltpu.VMEM((width, 2 * secs * side), bf16),
            pltpu.VMEM((2 * n, width, lanes), f32),
        ],
        compiler_params=limit(8),
        name="pressures",
    )(cpl, *args)


def core_sum_kernel(near_ref, got_ref, own_ref, *send):
    groups = own_ref.shape[0]
    own_ref[...] = near_ref[0:groups] + got_ref[0:groups].astype(f32)
    for i, s in enumerate(send):
        r = slice((i + 1) * groups, (i + 2) * groups)
        s[...] = (near_ref[r] + got_ref[r].astype(f32)).astype(bf16)


def core_sum(near, got, secs):
    groups = near.shape[0] // secs
    shape = (groups,) + near.shape[1:]
    return pl.pallas_call(
        core_sum_kernel,
        in_specs=[VMEM] * 2,
        out_specs=[VMEM] * secs,
        out_shape=[jax.ShapeDtypeStruct(shape, f32)] + [jax.ShapeDtypeStruct(shape, bf16)] * (secs - 1),
        compiler_params=limit(4),
        name="core_sum",
    )(near, got)


def sec_sum_kernel(count, *refs):
    own, got, pt, outs = refs[0], refs[count:0:-1], refs[1 + count], refs[2 + count :]
    for j, out in enumerate(outs):
        value = own[j]
        for g in got:
            value = value + g[j].astype(f32)
        out[0] = value.astype(out.dtype)
        out[1] = pt[j].astype(out.dtype)


def sec_sum(own, got, pt):
    shape = (2,) + own.shape[1:]
    return pl.pallas_call(
        functools.partial(sec_sum_kernel, len(got)),
        in_specs=[VMEM] * (2 + len(got)),
        out_specs=[VMEM] * 4,
        out_shape=[jax.ShapeDtypeStruct(shape, f32)] + [jax.ShapeDtypeStruct(shape, bf16)] * 3,
        compiler_params=limit(4),
        name="sec_sum",
    )(own, *got[::-1], pt)


def output_kernel(r0, r3, r1, r2, loads_ref, press_ref, loads_t, press_t):
    half = loads_t.shape[0] // 2
    quarter = half // 4
    x, y, _, _ = place()
    for mask, r in enumerate((r0, r1, r2, r3)):
        at = pl.multiple_of(((x + 2 * y) ^ mask) * quarter, quarter)
        for part in range(2):
            rows = pl.ds(part * half + at, quarter)
            loads_t[rows, :] = r[0, part * quarter : (part + 1) * quarter, :].astype(f32)
            press_t[rows, :] = r[1, part * quarter : (part + 1) * quarter, :].astype(f32)
    loads_ref[...] = loads_t[...].T
    press_ref[...] = press_t[...].T.astype(bf16)


def outputs(parts):
    _, width, lanes = parts[0].shape
    cols = 4 * width
    return pl.pallas_call(
        output_kernel,
        in_specs=[VMEM] * 4,
        out_shape=[jax.ShapeDtypeStruct((lanes, cols), f32), jax.ShapeDtypeStruct((lanes, cols), bf16)],
        scratch_shapes=[pltpu.VMEM((cols, lanes), f32)] * 2,
        compiler_params=limit(4),
        name="outputs",
    )(parts[0], parts[3], parts[1], parts[2])


def on_device_fast(modal_loads, receptance, shapes, coupling, panel_coords, panel_areas):
    secs, tgts = lax.axis_size("sec"), lax.axis_size("tgt")
    device_count = lax.axis_size("blk") * tgts * secs
    pan_dev = panel_coords.shape[1]
    panels = float(pan_dev * device_count)
    width = modal_loads.shape[1] // 4
    blocks = receptance.shape[1] // shapes.shape[2]

    held = [
        pltpu.with_memory_space_constraint(a, pltpu.HBM)
        for a in (receptance, modal_loads, panel_coords, panel_areas[None, :], coupling)
    ]
    own, s1, s2, s3, geo = amplitude_parts(panels, *held)
    got = [exchange_plane(s, m) for m, s in ((1, s1), (2, s2), (3, s3))]
    flat = shapes.reshape(pan_dev, -1)
    modes = [flat] + [exchange_plane(flat, m) for m in (1, 2, 3)]
    payload, cpl = amplitude_sum([], own, geo, *got)
    near = [payload] + [exchange_sec(payload, m) for m in range(1, secs)]
    far = exchange_core(stack(near))
    targets = payload[-4 * GEO :, :]
    across = target_matrix(panels, targets)
    vel = velocities(panels, cpl, near, far, modes, width, blocks)
    mats = [helmholtz(across, n) for n in near] + [helmholtz(across, far, i, (vel,), 1.4) for i in range(secs)]
    mats = [m for pair in mats for m in pair]
    v_near = [vel] + [exchange_sec(vel, m) for m in range(1, secs)]
    v_far = exchange_core(stack(v_near))
    pt, n_near, n_far = pressures(cpl, v_near, v_far, mats, targets, modes, tgts)
    parts = core_sum(n_near, exchange_core(n_far), secs)
    sec_got = [exchange_sec(p, m) for m, p in zip(range(1, secs), parts[1:])]
    finals = sec_sum(parts[0], sec_got, pt)
    mine = [finals[0]] + [exchange_plane(f, m) for m, f in zip((1, 2, 3), finals[1:])]
    return outputs(mine)


def rotate_combine(leading, second):
    half_width = leading.shape[1] // 2
    return jnp.concatenate(
        [
            leading[:, :half_width] - second[:, half_width:],
            leading[:, half_width:] + second[:, :half_width],
        ],
        axis=1,
    )


def pressure_block(target_geometry, source_geometry, source_vel, total_panels):
    delta_x = target_geometry[0][:, None] - source_geometry[0][None, :]
    delta_y = target_geometry[1][:, None] - source_geometry[1][None, :]
    delta_z = target_geometry[2][:, None] - source_geometry[2][None, :]
    source_area = source_geometry[3][None, :]
    distance = jnp.sqrt(
        delta_x * delta_x + delta_y * delta_y + delta_z * delta_z + source_area / total_panels
    )
    weight = source_area / (distance * math.sqrt(total_panels))
    phase_angle = wave_number * distance
    kernel = jnp.concatenate(
        [
            (jnp.cos(phase_angle) * weight).astype(jnp.bfloat16),
            (jnp.sin(phase_angle) * weight).astype(jnp.bfloat16),
        ],
        axis=0,
    )
    products = lax.dot_general(
        kernel, source_vel, (((1,), (1,)), ((), ())), preferred_element_type=jnp.float32
    )
    target_count = target_geometry.shape[1]
    return rotate_combine(products[:target_count], products[target_count:])


def on_device_general(modal_loads, receptance, shapes, coupling, panel_coords, panel_areas):
    pan_dev = panel_coords.shape[1]
    case_width = modal_loads.shape[1]
    device_count = lax.axis_size("blk") * lax.axis_size("tgt") * lax.axis_size("sec")
    total_panels = float(pan_dev * device_count)
    row_share = receptance.shape[1]
    stacked = jnp.dot(
        receptance.reshape(2 * row_share, receptance.shape[2]),
        modal_loads,
        preferred_element_type=jnp.float32,
    )
    modal_sum = rotate_combine(stacked[:row_share], stacked[row_share:])
    modal_sum = lax.psum(modal_sum, "blk")
    amplitudes = lax.all_gather(modal_sum.astype(jnp.bfloat16), ("tgt", "sec"), axis=0, tiled=True)
    mode_block = shapes.shape[2]
    blocks = amplitudes.reshape(-1, mode_block, case_width)
    chosen = blocks[coupling]
    block_count = coupling.shape[0]
    shaped = shapes.reshape(block_count, -1, shapes.shape[1], mode_block)
    vel_t = (
        jnp.einsum("bpkm,bkmc->cbp", shaped, chosen, preferred_element_type=jnp.float32)
        .reshape(case_width, pan_dev)
        .astype(jnp.bfloat16)
    )
    geometry = jnp.concatenate([panel_coords, panel_areas[None, :]], axis=0)
    source_vel, source_geometry = (
        lax.all_gather(vel_t.astype(jnp.float32), ("tgt", "sec"), axis=1, tiled=True).astype(
            vel_t.dtype
        ),
        lax.all_gather(geometry, ("tgt", "sec"), axis=1, tiled=True),
    )
    target_geometry = lax.all_gather(geometry, "blk", axis=1, tiled=True)
    target_groups = pan_dev * lax.axis_size("blk") // pan_dev

    def single_block(block_index):
        target_block = lax.dynamic_slice_in_dim(target_geometry, block_index * pan_dev, pan_dev, 1)
        return pressure_block(target_block, source_geometry, source_vel, total_panels)

    stacked_terms = lax.map(single_block, jnp.arange(target_groups, dtype=jnp.int32))
    pressure_f = lax.psum_scatter(
        stacked_terms.reshape(pan_dev * lax.axis_size("blk"), case_width).astype(jnp.bfloat16),
        "blk",
        scatter_dimension=0,
        tiled=True,
    )
    weighted = (panel_areas[:, None] * pressure_f.astype(jnp.float32)).astype(jnp.bfloat16)
    contrib = jnp.einsum(
        "bpkm,bpc->bkmc",
        shaped,
        weighted.reshape(block_count, -1, case_width),
        preferred_element_type=jnp.float32,
    )
    onehot = (
        coupling[:, :, None] == jnp.arange(blocks.shape[0], dtype=jnp.int32)[None, None, :]
    ).astype(jnp.float32)
    partial_loads = jnp.einsum(
        "bkj,bkmc->jmc", onehot, contrib, precision=lax.Precision.HIGHEST
    ).reshape(-1, case_width)
    new_loads = lax.psum_scatter(
        partial_loads, ("blk", "tgt", "sec"), scatter_dimension=0, tiled=True
    )
    return (new_loads, pressure_f)


def on_device(modal_loads, receptance, shapes, coupling, panel_coords, panel_areas):
    lanes = 128
    secs = lax.axis_size("sec")
    mine = modal_loads.shape[0] * lax.axis_size("blk") // (lax.axis_size("blk") * lax.axis_size("tgt") * secs)
    fits = (
        lax.axis_size("blk") == 2
        and lax.axis_size("tgt") == 4
        and secs & (secs - 1) == 0
        and coupling.shape[0] == 1
        and shapes.shape[2] == lanes
        and panel_coords.shape[1] == lanes
        and modal_loads.shape[1] == lanes
        and mine == lanes
    )
    body = on_device_fast if fits else on_device_general
    return body(modal_loads, receptance, shapes, coupling, panel_coords, panel_areas)


def solution(mesh):
    in_specs = (
        P("blk", None),
        P(None, ("tgt", "sec"), "blk"),
        P(("blk", "tgt", "sec"), None, None),
        P(("blk", "tgt", "sec"), None),
        P(None, ("blk", "tgt", "sec")),
        P(("blk", "tgt", "sec")),
    )
    out_specs = (P(("blk", "tgt", "sec"), None), P(("blk", "tgt", "sec"), None))
    return jax.shard_map(
        on_device, mesh=mesh, in_specs=in_specs, out_specs=out_specs, check_vma=False
    )
```

```python
import functools
import math

import jax
import jax.numpy as jnp
import numpy as np
from jax import lax
from jax.experimental import pallas as pl
from jax.experimental.pallas import tpu as pltpu
from jax.sharding import PartitionSpec as P

wave_number = 40.0
turns = wave_number / (2.0 * math.pi)
bf16 = jnp.bfloat16
f32 = jnp.float32
AXES = ("blk", "tgt", "sec")
GEO = 16


def fit(values, terms):
    nodes = 0.125 + 0.125 * np.cos(np.pi * (np.arange(400) + 0.5) / 400)
    matrix = np.vander(nodes, terms, increasing=True)
    return [float(c) for c in np.linalg.lstsq(matrix, values(nodes), rcond=None)[0]]


sin_terms = fit(lambda u: math.sqrt(2.0) * np.sin(np.pi * np.sqrt(u)) / np.sqrt(u), 4)
cos_terms = fit(lambda u: math.sqrt(2.0) * np.cos(np.pi * np.sqrt(u)), 4)


def exchange_plane(x, mask):
    nb, nt = lax.axis_size("blk"), lax.axis_size("tgt")
    pairs = [
        (b * nt + t, (b ^ (mask & 1)) * nt + (t ^ (2 * (mask >> 1))))
        for b in range(nb)
        for t in range(nt)
    ]
    return lax.ppermute(x, ("blk", "tgt"), pairs)


def exchange_sec(x, mask):
    return lax.ppermute(x, "sec", [(s, s ^ mask) for s in range(lax.axis_size("sec"))])


def exchange_core(x):
    return lax.ppermute(x, "tgt", [(t, t ^ 1) for t in range(lax.axis_size("tgt"))])


VMEM = pl.BlockSpec(memory_space=pltpu.VMEM)
SMEM = pl.BlockSpec(memory_space=pltpu.SMEM)
HBM = pl.BlockSpec(memory_space=pltpu.HBM)


def place():
    t = lax.axis_index("tgt")
    return lax.axis_index("blk"), t >> 1, t & 1, lax.axis_index("sec")


def limit(mib):
    return pltpu.CompilerParams(vmem_limit_bytes=mib << 20)


def bits_of(n):
    return n.bit_length() - 1


def three_parts(x):
    first = x.astype(bf16).astype(f32)
    rest = x - first
    second = rest.astype(bf16).astype(f32)
    return first, second, rest - second


def amplitude_kernel(panels, r_hbm, l_hbm, xyz_hbm, area_hbm, cpl_hbm, own_ref, s1_ref, s2_ref, s3_ref, geo_ref, r_buf, l_buf, xyz, areas, cpl, amp_t, geo, sems):
    rows, lanes = r_buf.shape[1], 128
    blocks = rows // lanes
    small = [
        pltpu.make_async_copy(s, d, sems.at[i])
        for i, (s, d) in enumerate(((xyz_hbm, xyz), (area_hbm, areas), (cpl_hbm, cpl)))
    ]
    fetch_loads = pltpu.make_async_copy(l_hbm, l_buf, sems.at[3])
    fetch = [
        pltpu.make_async_copy(
            r_hbm.at[part, b * lanes : (b + 1) * lanes, :], r_buf.at[part, b * lanes : (b + 1) * lanes, :], sems.at[4 + 2 * b + part]
        )
        for b in range(blocks)
        for part in range(2)
    ]
    for copy in [fetch_loads] + small + fetch:
        copy.start()
    width = l_buf.shape[1]
    half = width // 2
    quarter = half // 4
    x, y, _, _ = place()
    mine = x + 2 * y
    fetch_loads.wait()
    for b in range(blocks):
        span = slice(b * lanes, (b + 1) * lanes)
        fetch[2 * b].wait()
        lead = jnp.dot(r_buf[0, span, :], l_buf[...], preferred_element_type=f32)
        fetch[2 * b + 1].wait()
        turned = pltpu.roll(jnp.dot(r_buf[1, span, :], l_buf[...], preferred_element_type=f32), half, 1)
        lane = lax.broadcasted_iota(jnp.int32, turned.shape, 1)
        amp_t[...] = (lead + jnp.where(lane < half, -turned, turned)).T
        for mask, out in enumerate((own_ref, s1_ref, s2_ref, s3_ref)):
            at = pl.multiple_of((mine ^ mask) * quarter, quarter)
            for part in range(2):
                r0 = (2 * b + part) * quarter
                out[r0 : r0 + quarter, :] = amp_t[pl.ds(part * half + at, quarter), :].astype(out.dtype)

    for copy in small:
        copy.wait()
    scaled = (xyz[...] - 0.5) * turns
    area = areas[...]
    norm = jnp.sum(scaled * scaled, axis=0, keepdims=True) + area * (turns * turns / panels)
    geo[...] = jnp.zeros_like(geo)
    for i, part in enumerate(three_parts(scaled)):
        geo[3 * i : 3 * i + 3, :] = part
    for i, part in enumerate(three_parts(norm)):
        geo[9 + i : 10 + i, :] = part
    for i, part in enumerate(three_parts(area)):
        geo[12 + i : 13 + i, :] = part
    geo[15:16, 0 : cpl.shape[1]] = cpl[...].astype(f32)
    packed = geo[...].astype(bf16)
    geo_ref[...] = packed
    for out in (s1_ref, s2_ref, s3_ref):
        out[out.shape[0] - GEO :, :] = packed


def amplitude_parts(panels, receptance, loads, xyz, area, coupling):
    _, rows, depth = receptance.shape
    width = loads.shape[1]
    blocks = rows // 128
    chunk = blocks * (width // 4)
    outs = [((chunk, 128), f32)] + [((chunk + GEO, 128), bf16)] * 3 + [((GEO, 128), bf16)]
    return pl.pallas_call(
        functools.partial(amplitude_kernel, panels),
        in_specs=[HBM] * 5,
        out_specs=[VMEM] * len(outs),
        out_shape=[jax.ShapeDtypeStruct(s, d) for s, d in outs],
        scratch_shapes=[
            pltpu.VMEM(receptance.shape, bf16),
            pltpu.VMEM(loads.shape, bf16),
            pltpu.VMEM(xyz.shape, f32),
            pltpu.VMEM(area.shape, f32),
            pltpu.VMEM(coupling.shape, jnp.int32),
            pltpu.VMEM((width, 128), f32),
            pltpu.VMEM((GEO, 128), f32),
            pltpu.SemaphoreType.DMA((4 + 2 * blocks,)),
        ],
        compiler_params=limit(12),
        cost_estimate=pl.CostEstimate(flops=4 * rows * depth * width, bytes_accessed=1, transcendentals=0),
        name="amplitude_parts",
    )(receptance, loads, xyz, area, coupling)


def amplitude_sum_kernel(count, *refs):
    own_ref, geo_ref, x_ref, y_ref, d_ref, out_ref, cpl_ref = refs[count:]
    n = own_ref.shape[0]
    out_ref[0:n, :] = (own_ref[...] + x_ref[0:n, :].astype(f32)).astype(bf16)
    out_ref[n : 2 * n, :] = (y_ref[0:n, :].astype(f32) + d_ref[0:n, :].astype(f32)).astype(bf16)
    geos = [geo_ref[...]] + [r[n:, :] for r in (x_ref, y_ref, d_ref)]
    for i, g in enumerate(geos):
        out_ref[2 * n + GEO * i : 2 * n + GEO * (i + 1), :] = g
        cpl_ref[i : i + 1, :] = g.astype(f32)[GEO - 1 :, :].astype(jnp.int32)


def amplitude_sum(early, own, geo, x, y, d):
    n = own.shape[0]
    return pl.pallas_call(
        functools.partial(amplitude_sum_kernel, 0),
        in_specs=[pl.BlockSpec(memory_space=pl.ANY)] * len(early) + [VMEM] * 5,
        out_specs=[VMEM] * 2,
        out_shape=[jax.ShapeDtypeStruct((2 * n + 4 * GEO, 128), bf16), jax.ShapeDtypeStruct((4, 128), jnp.int32)],
        compiler_params=limit(4),
        name="amplitude_sum",
    )(own, geo, x, y, d)


def stack_kernel(count, *refs):
    for i, r in enumerate(refs[:count]):
        refs[-1][i] = r[...]


def stack(parts, after=()):
    return pl.pallas_call(
        functools.partial(stack_kernel, len(parts)),
        in_specs=[VMEM] * len(parts) + [pl.BlockSpec(memory_space=pl.ANY)] * len(after),
        out_specs=VMEM,
        out_shape=jax.ShapeDtypeStruct((len(parts),) + parts[0].shape, parts[0].dtype),
        compiler_params=limit(4),
        name="stack",
    )(*parts, *after)


def velocity_kernel(width, blocks, scale, secs, cpl, *refs):
    near, far_ref = refs[0:secs], refs[secs]
    modes, out_ref, table, picked = refs[secs + 1 : secs + 5], *refs[-3:]
    _, y, c, z = place()
    used = 2 * blocks * width
    for i in range(secs):
        table[0, i] = near[i][0:used, :]
        table[1, i] = far_ref[i, 0:used, :]
    sec_bits, block_bits = bits_of(secs), bits_of(blocks)
    count = modes[0].shape[1] // 128
    for j, m_ref in enumerate(modes):
        for k in range(count):
            b = cpl[j, k]
            h = b & (blocks - 1)
            s = (b >> block_bits) & (secs - 1)
            t = b >> (block_bits + sec_bits)
            row = pl.multiple_of((((((t >> 1) ^ y) << block_bits) + h) * width), width)
            picked[j, :, k * 128 : (k + 1) * 128] = table[(t & 1) ^ c, s ^ z, pl.ds(row, width), :]
    for j, m_ref in enumerate(modes):
        vel = lax.dot_general(picked[j], m_ref[...], (((1,), (1,)), ((), ())), preferred_element_type=f32)
        g = near[0][used + GEO * j : used + GEO * (j + 1), :].astype(f32)
        area = (g[12:13] + g[13:14] + g[14:15]) * scale
        out_ref[j] = (vel * area).astype(bf16)


def velocities(panels, cpl, near, far, modes, width, blocks):
    count, depth = modes[0].shape
    secs = len(near)
    return pl.pallas_call(
        functools.partial(velocity_kernel, width, blocks, turns / math.sqrt(panels), secs),
        in_specs=[VMEM] * (secs + 6),
        out_specs=VMEM,
        out_shape=jax.ShapeDtypeStruct((4, width, count), bf16),
        scratch_shapes=[
            pltpu.VMEM((2, secs, 2 * blocks * width, 128), bf16),
            pltpu.VMEM((4, width, depth), bf16),
        ],
        compiler_params=limit(6),
        name="velocities",
    )(cpl, *near, far, *modes)


def target_kernel(panels, tgt_ref, out_ref, mat):
    lanes = tgt_ref.shape[1]
    mat[...] = jnp.zeros_like(mat)
    for j in range(tgt_ref.shape[0] // GEO):
        g = tgt_ref[j * GEO : (j + 1) * GEO, :].astype(f32)
        area = g[12:13] + g[13:14] + g[14:15]
        norm = g[9:10] + g[10:11] + g[11:12] - area * (turns * turns / panels)
        col = slice(j * lanes, (j + 1) * lanes)
        for a in range(3):
            for b in range(3):
                mat[GEO * a + 3 * b : GEO * a + 3 * b + 3, col] = -2.0 * g[3 * a : 3 * a + 3]
        mat[9:12, col] = jnp.ones((3, lanes), f32)
        for i, part in enumerate(three_parts(norm)):
            mat[3 * GEO + i : 3 * GEO + i + 1, col] = part
    out_ref[...] = mat[...].astype(bf16)


def target_matrix(panels, geo):
    side = geo.shape[0] // GEO * geo.shape[1]
    return pl.pallas_call(
        functools.partial(target_kernel, panels),
        in_specs=[VMEM],
        out_specs=VMEM,
        out_shape=jax.ShapeDtypeStruct((4 * GEO, side), bf16),
        scratch_shapes=[pltpu.VMEM((4 * GEO, side), f32)],
        compiler_params=limit(4),
        name="target_matrix",
    )(geo)


def helmholtz_kernel(at, tgt_ref, src_ref, *refs):
    re_ref, im_ref = refs[-2:]
    src = src_ref if at is None else src_ref.at[at]
    side = tgt_ref.shape[1]
    first = src.shape[0] - side // 128 * GEO
    c0, c1, c2 = (c / cos_terms[3] for c in cos_terms[:3])
    strip = 128
    for r in range(0, side, strip):
        at_row = first + r // 128 * GEO
        one = src[at_row : at_row + GEO, :]
        full = jnp.concatenate([one, one, one, jnp.ones_like(one)], axis=0)
        square = lax.dot_general(full, tgt_ref[...], (((0,), (0,)), ((), ())), preferred_element_type=f32)
        inverse = lax.rsqrt(square)
        t = square * inverse
        f = t - jnp.round(t)
        u = f * f
        s = (((sin_terms[3] * u + sin_terms[2]) * u + sin_terms[1]) * u + sin_terms[0]) * f
        c = ((u + c2) * u + c1) * u + c0
        part = s * inverse
        re_ref[r : r + strip, :] = (inverse - s * part).astype(bf16)
        im_ref[r : r + strip, :] = (c * part).astype(bf16)


def helmholtz(targets, payload, at=None, after=(), cost=1.0):
    side = targets.shape[1]
    return pl.pallas_call(
        functools.partial(helmholtz_kernel, at),
        in_specs=[VMEM] * 2 + [pl.BlockSpec(memory_space=pl.ANY)] * len(after),
        out_specs=[VMEM] * 2,
        out_shape=[jax.ShapeDtypeStruct((side, side), bf16)] * 2,
        compiler_params=limit(4),
        cost_estimate=pl.CostEstimate(flops=int(cost * 3900 * side * side), bytes_accessed=1, transcendentals=0),
        name="helmholtz",
    )(targets, payload, *after)


def product(velocity, mats, lead, turned):
    count = len(mats) // 2
    side = mats[0].shape[0]
    lanes = 128
    half = lead.shape[0] // 2
    re = im = 0.0
    for i in range(count):
        for j in range(side // lanes):
            v = velocity(i, j)
            col = slice(i * side + j * lanes, i * side + (j + 1) * lanes)
            lead[:, col] = v
            turned[0:half, col] = -v[half:]
            turned[half:, col] = v[0:half]
    for i in range(count):
        col = slice(i * side, (i + 1) * side)
        re += jnp.dot(lead[:, col], mats[2 * i][...], preferred_element_type=f32)
        im += jnp.dot(turned[:, col], mats[2 * i + 1][...], preferred_element_type=f32)
    return re + im * cos_terms[3]


def near_kernel(secs, *refs):
    out_ref, lead, turned = refs[-3:]
    out_ref[...] = product(lambda i, j: refs[i][j], refs[secs : 3 * secs], lead, turned)


def near_pressures(v_near, mats):
    secs = len(v_near)
    groups, width, lanes = v_near[0].shape
    side = groups * lanes
    return pl.pallas_call(
        functools.partial(near_kernel, secs),
        in_specs=[VMEM] * (3 * secs),
        out_specs=VMEM,
        out_shape=jax.ShapeDtypeStruct((width, side), f32),
        scratch_shapes=[pltpu.VMEM((width, secs * side), bf16)] * 2,
        compiler_params=limit(4),
        cost_estimate=pl.CostEstimate(flops=3900 * side * side, bytes_accessed=1, transcendentals=0),
        name="near_pressures",
    )(*v_near, *mats)


def pressure_kernel(secs, tgt_n, cpl, part_ref, v_far, *refs):
    mats, geo_ref, modes = refs[0 : 2 * secs], refs[2 * secs], refs[2 * secs + 1 : 2 * secs + 5]
    pt_ref, near_ref, far_ref, lead, turned, total = refs[2 * secs + 5 :]
    _, groups, width, lanes = v_far.shape
    p = (part_ref[...] + product(lambda i, j: v_far[i, j], mats, lead, turned)).astype(bf16)
    total[...] = jnp.zeros_like(total)
    x, y, c, z = place()
    sec_bits, tgt_bits = bits_of(secs), bits_of(tgt_n)
    for j, m_ref in enumerate(modes):
        pj = p[:, j * lanes : (j + 1) * lanes]
        pt_ref[j] = pj
        g = geo_ref[j * GEO : (j + 1) * GEO, :].astype(f32)
        weighted = (pj.astype(f32) * (g[12:13] + g[13:14] + g[14:15])).astype(bf16)
        terms = jnp.dot(weighted, m_ref[...], preferred_element_type=f32)
        for k in range(m_ref.shape[1] // lanes):
            b = cpl[j, k]
            s = b & (secs - 1)
            t = (b >> sec_bits) & (tgt_n - 1)
            xb = b >> (sec_bits + tgt_bits)
            at = ((((t & 1) ^ c) * secs + (s ^ z)) * groups) + (xb ^ x) + 2 * ((t >> 1) ^ y)
            total[at] += terms[:, k * lanes : (k + 1) * lanes]
    n = near_ref.shape[0]
    near_ref[...] = total[0:n]
    far_ref[...] = total[n:].astype(bf16)


def pressures(cpl, part, v_far, mats, geo, modes, tgt_n):
    secs, groups, width, lanes = v_far.shape
    side = groups * lanes
    n = secs * groups
    args = [part, v_far, *mats, geo, *modes]
    return pl.pallas_call(
        functools.partial(pressure_kernel, secs, tgt_n),
        in_specs=[VMEM] * (1 + len(args)),
        out_specs=[VMEM] * 3,
        out_shape=[
            jax.ShapeDtypeStruct((groups, width, lanes), bf16),
            jax.ShapeDtypeStruct((n, width, lanes), f32),
            jax.ShapeDtypeStruct((n, width, lanes), bf16),
        ],
        scratch_shapes=[
            pltpu.VMEM((width, secs * side), bf16),
            pltpu.VMEM((width, secs * side), bf16),
            pltpu.VMEM((2 * n, width, lanes), f32),
        ],
        compiler_params=limit(8),
        name="pressures",
    )(cpl, *args)


def core_sum_kernel(near_ref, got_ref, own_ref, *send):
    groups = own_ref.shape[0]
    own_ref[...] = near_ref[0:groups] + got_ref[0:groups].astype(f32)
    for i, s in enumerate(send):
        r = slice((i + 1) * groups, (i + 2) * groups)
        s[...] = (near_ref[r] + got_ref[r].astype(f32)).astype(bf16)


def core_sum(near, got, secs):
    groups = near.shape[0] // secs
    shape = (groups,) + near.shape[1:]
    return pl.pallas_call(
        core_sum_kernel,
        in_specs=[VMEM] * 2,
        out_specs=[VMEM] * secs,
        out_shape=[jax.ShapeDtypeStruct(shape, f32)] + [jax.ShapeDtypeStruct(shape, bf16)] * (secs - 1),
        compiler_params=limit(4),
        name="core_sum",
    )(near, got)


def sec_sum_kernel(count, *refs):
    own, got, pt, outs = refs[0], refs[count:0:-1], refs[1 + count], refs[2 + count :]
    for j, out in enumerate(outs):
        value = own[j]
        for g in got:
            value = value + g[j].astype(f32)
        out[0] = value.astype(out.dtype)
        out[1] = pt[j].astype(out.dtype)


def sec_sum(own, got, pt):
    shape = (2,) + own.shape[1:]
    return pl.pallas_call(
        functools.partial(sec_sum_kernel, len(got)),
        in_specs=[VMEM] * (2 + len(got)),
        out_specs=[VMEM] * 4,
        out_shape=[jax.ShapeDtypeStruct(shape, f32)] + [jax.ShapeDtypeStruct(shape, bf16)] * 3,
        compiler_params=limit(4),
        name="sec_sum",
    )(own, *got[::-1], pt)


def output_kernel(r0, r3, r1, r2, loads_ref, press_ref, loads_t, press_t):
    half = loads_t.shape[0] // 2
    quarter = half // 4
    x, y, _, _ = place()
    for mask, r in enumerate((r0, r1, r2, r3)):
        at = pl.multiple_of(((x + 2 * y) ^ mask) * quarter, quarter)
        for part in range(2):
            rows = pl.ds(part * half + at, quarter)
            loads_t[rows, :] = r[0, part * quarter : (part + 1) * quarter, :].astype(f32)
            press_t[rows, :] = r[1, part * quarter : (part + 1) * quarter, :].astype(f32)
    loads_ref[...] = loads_t[...].T
    press_ref[...] = press_t[...].T.astype(bf16)


def outputs(parts):
    _, width, lanes = parts[0].shape
    cols = 4 * width
    return pl.pallas_call(
        output_kernel,
        in_specs=[VMEM] * 4,
        out_shape=[jax.ShapeDtypeStruct((lanes, cols), f32), jax.ShapeDtypeStruct((lanes, cols), bf16)],
        scratch_shapes=[pltpu.VMEM((cols, lanes), f32)] * 2,
        compiler_params=limit(4),
        name="outputs",
    )(parts[0], parts[3], parts[1], parts[2])


def on_device_fast(modal_loads, receptance, shapes, coupling, panel_coords, panel_areas):
    secs, tgts = lax.axis_size("sec"), lax.axis_size("tgt")
    device_count = lax.axis_size("blk") * tgts * secs
    pan_dev = panel_coords.shape[1]
    panels = float(pan_dev * device_count)
    width = modal_loads.shape[1] // 4
    blocks = receptance.shape[1] // shapes.shape[2]

    held = [
        pltpu.with_memory_space_constraint(a, pltpu.HBM)
        for a in (receptance, modal_loads, panel_coords, panel_areas[None, :], coupling)
    ]
    own, s1, s2, s3, geo = amplitude_parts(panels, *held)
    got = [exchange_plane(s, m) for m, s in ((1, s1), (2, s2), (3, s3))]
    flat = shapes.reshape(pan_dev, -1)
    modes = [flat] + [exchange_plane(flat, m) for m in (1, 2, 3)]
    payload, cpl = amplitude_sum([], own, geo, *got)
    near = [payload] + [exchange_sec(payload, m) for m in range(1, secs)]
    far = exchange_core(stack(near))
    targets = payload[-4 * GEO :, :]
    across = target_matrix(panels, targets)
    vel = velocities(panels, cpl, near, far, modes, width, blocks)
    mats = [helmholtz(across, n) for n in near] + [helmholtz(across, far, i, (vel,), 1.4) for i in range(secs)]
    mats = [m for pair in mats for m in pair]
    v_near = [vel] + [exchange_sec(vel, m) for m in range(1, secs)]
    v_far = exchange_core(stack(v_near, mats[-1:]))
    part = near_pressures(v_near, mats[: 2 * secs])
    pt, n_near, n_far = pressures(cpl, part, v_far, mats[2 * secs :], targets, modes, tgts)
    parts = core_sum(n_near, exchange_core(n_far), secs)
    sec_got = [exchange_sec(p, m) for m, p in zip(range(1, secs), parts[1:])]
    finals = sec_sum(parts[0], sec_got, pt)
    mine = [finals[0]] + [exchange_plane(f, m) for m, f in zip((1, 2, 3), finals[1:])]
    return outputs(mine)


def rotate_combine(leading, second):
    half_width = leading.shape[1] // 2
    return jnp.concatenate(
        [
            leading[:, :half_width] - second[:, half_width:],
            leading[:, half_width:] + second[:, :half_width],
        ],
        axis=1,
    )


def pressure_block(target_geometry, source_geometry, source_vel, total_panels):
    delta_x = target_geometry[0][:, None] - source_geometry[0][None, :]
    delta_y = target_geometry[1][:, None] - source_geometry[1][None, :]
    delta_z = target_geometry[2][:, None] - source_geometry[2][None, :]
    source_area = source_geometry[3][None, :]
    distance = jnp.sqrt(
        delta_x * delta_x + delta_y * delta_y + delta_z * delta_z + source_area / total_panels
    )
    weight = source_area / (distance * math.sqrt(total_panels))
    phase_angle = wave_number * distance
    kernel = jnp.concatenate(
        [
            (jnp.cos(phase_angle) * weight).astype(jnp.bfloat16),
            (jnp.sin(phase_angle) * weight).astype(jnp.bfloat16),
        ],
        axis=0,
    )
    products = lax.dot_general(
        kernel, source_vel, (((1,), (1,)), ((), ())), preferred_element_type=jnp.float32
    )
    target_count = target_geometry.shape[1]
    return rotate_combine(products[:target_count], products[target_count:])


def on_device_general(modal_loads, receptance, shapes, coupling, panel_coords, panel_areas):
    pan_dev = panel_coords.shape[1]
    case_width = modal_loads.shape[1]
    device_count = lax.axis_size("blk") * lax.axis_size("tgt") * lax.axis_size("sec")
    total_panels = float(pan_dev * device_count)
    row_share = receptance.shape[1]
    stacked = jnp.dot(
        receptance.reshape(2 * row_share, receptance.shape[2]),
        modal_loads,
        preferred_element_type=jnp.float32,
    )
    modal_sum = rotate_combine(stacked[:row_share], stacked[row_share:])
    modal_sum = lax.psum(modal_sum, "blk")
    amplitudes = lax.all_gather(modal_sum.astype(jnp.bfloat16), ("tgt", "sec"), axis=0, tiled=True)
    mode_block = shapes.shape[2]
    blocks = amplitudes.reshape(-1, mode_block, case_width)
    chosen = blocks[coupling]
    block_count = coupling.shape[0]
    shaped = shapes.reshape(block_count, -1, shapes.shape[1], mode_block)
    vel_t = (
        jnp.einsum("bpkm,bkmc->cbp", shaped, chosen, preferred_element_type=jnp.float32)
        .reshape(case_width, pan_dev)
        .astype(jnp.bfloat16)
    )
    geometry = jnp.concatenate([panel_coords, panel_areas[None, :]], axis=0)
    source_vel, source_geometry = (
        lax.all_gather(vel_t.astype(jnp.float32), ("tgt", "sec"), axis=1, tiled=True).astype(
            vel_t.dtype
        ),
        lax.all_gather(geometry, ("tgt", "sec"), axis=1, tiled=True),
    )
    target_geometry = lax.all_gather(geometry, "blk", axis=1, tiled=True)
    target_groups = pan_dev * lax.axis_size("blk") // pan_dev

    def single_block(block_index):
        target_block = lax.dynamic_slice_in_dim(target_geometry, block_index * pan_dev, pan_dev, 1)
        return pressure_block(target_block, source_geometry, source_vel, total_panels)

    stacked_terms = lax.map(single_block, jnp.arange(target_groups, dtype=jnp.int32))
    pressure_f = lax.psum_scatter(
        stacked_terms.reshape(pan_dev * lax.axis_size("blk"), case_width).astype(jnp.bfloat16),
        "blk",
        scatter_dimension=0,
        tiled=True,
    )
    weighted = (panel_areas[:, None] * pressure_f.astype(jnp.float32)).astype(jnp.bfloat16)
    contrib = jnp.einsum(
        "bpkm,bpc->bkmc",
        shaped,
        weighted.reshape(block_count, -1, case_width),
        preferred_element_type=jnp.float32,
    )
    onehot = (
        coupling[:, :, None] == jnp.arange(blocks.shape[0], dtype=jnp.int32)[None, None, :]
    ).astype(jnp.float32)
    partial_loads = jnp.einsum(
        "bkj,bkmc->jmc", onehot, contrib, precision=lax.Precision.HIGHEST
    ).reshape(-1, case_width)
    new_loads = lax.psum_scatter(
        partial_loads, ("blk", "tgt", "sec"), scatter_dimension=0, tiled=True
    )
    return (new_loads, pressure_f)


def on_device(modal_loads, receptance, shapes, coupling, panel_coords, panel_areas):
    lanes = 128
    secs = lax.axis_size("sec")
    mine = modal_loads.shape[0] * lax.axis_size("blk") // (lax.axis_size("blk") * lax.axis_size("tgt") * secs)
    fits = (
        lax.axis_size("blk") == 2
        and lax.axis_size("tgt") == 4
        and secs & (secs - 1) == 0
        and coupling.shape[0] == 1
        and shapes.shape[2] == lanes
        and panel_coords.shape[1] == lanes
        and modal_loads.shape[1] == lanes
        and mine == lanes
    )
    body = on_device_fast if fits else on_device_general
    return body(modal_loads, receptance, shapes, coupling, panel_coords, panel_areas)


def rotate_combine(leading, second):
    half_width = leading.shape[1] // 2
    return jnp.concatenate(
        [
            leading[:, :half_width] - second[:, half_width:],
            leading[:, half_width:] + second[:, :half_width],
        ],
        axis=1,
    )


def pressure_block(target_geometry, source_geometry, source_vel, total_panels):
    delta_x = target_geometry[0][:, None] - source_geometry[0][None, :]
    delta_y = target_geometry[1][:, None] - source_geometry[1][None, :]
    delta_z = target_geometry[2][:, None] - source_geometry[2][None, :]
    source_area = source_geometry[3][None, :]
    distance = jnp.sqrt(
        delta_x * delta_x + delta_y * delta_y + delta_z * delta_z + source_area / total_panels
    )
    weight = source_area / (distance * math.sqrt(total_panels))
    phase_angle = wave_number * distance
    kernel = jnp.concatenate(
        [
            (jnp.cos(phase_angle) * weight).astype(jnp.bfloat16),
            (jnp.sin(phase_angle) * weight).astype(jnp.bfloat16),
        ],
        axis=0,
    )
    products = lax.dot_general(
        kernel, source_vel, (((1,), (1,)), ((), ())), preferred_element_type=jnp.float32
    )
    target_count = target_geometry.shape[1]
    return rotate_combine(products[:target_count], products[target_count:])


def on_device_general(modal_loads, receptance, shapes, coupling, panel_coords, panel_areas):
    pan_dev = panel_coords.shape[1]
    case_width = modal_loads.shape[1]
    device_count = lax.axis_size("blk") * lax.axis_size("tgt") * lax.axis_size("sec")
    total_panels = float(pan_dev * device_count)
    row_share = receptance.shape[1]
    stacked = jnp.dot(
        receptance.reshape(2 * row_share, receptance.shape[2]),
        modal_loads,
        preferred_element_type=jnp.float32,
    )
    modal_sum = rotate_combine(stacked[:row_share], stacked[row_share:])
    modal_sum = lax.psum(modal_sum, "blk")
    amplitudes = lax.all_gather(modal_sum.astype(jnp.bfloat16), ("tgt", "sec"), axis=0, tiled=True)
    mode_block = shapes.shape[2]
    blocks = amplitudes.reshape(-1, mode_block, case_width)
    chosen = blocks[coupling]
    block_count = coupling.shape[0]
    shaped = shapes.reshape(block_count, -1, shapes.shape[1], mode_block)
    vel_t = (
        jnp.einsum("bpkm,bkmc->cbp", shaped, chosen, preferred_element_type=jnp.float32)
        .reshape(case_width, pan_dev)
        .astype(jnp.bfloat16)
    )
    geometry = jnp.concatenate([panel_coords, panel_areas[None, :]], axis=0)
    source_vel, source_geometry = (
        lax.all_gather(vel_t.astype(jnp.float32), ("tgt", "sec"), axis=1, tiled=True).astype(
            vel_t.dtype
        ),
        lax.all_gather(geometry, ("tgt", "sec"), axis=1, tiled=True),
    )
    target_geometry = lax.all_gather(geometry, "blk", axis=1, tiled=True)
    target_groups = pan_dev * lax.axis_size("blk") // pan_dev

    def single_block(block_index):
        target_block = lax.dynamic_slice_in_dim(target_geometry, block_index * pan_dev, pan_dev, 1)
        return pressure_block(target_block, source_geometry, source_vel, total_panels)

    stacked_terms = lax.map(single_block, jnp.arange(target_groups, dtype=jnp.int32))
    pressure_f = lax.psum_scatter(
        stacked_terms.reshape(pan_dev * lax.axis_size("blk"), case_width).astype(jnp.bfloat16),
        "blk",
        scatter_dimension=0,
        tiled=True,
    )
    weighted = (panel_areas[:, None] * pressure_f.astype(jnp.float32)).astype(jnp.bfloat16)
    contrib = jnp.einsum(
        "bpkm,bpc->bkmc",
        shaped,
        weighted.reshape(block_count, -1, case_width),
        preferred_element_type=jnp.float32,
    )
    onehot = (
        coupling[:, :, None] == jnp.arange(blocks.shape[0], dtype=jnp.int32)[None, None, :]
    ).astype(jnp.float32)
    partial_loads = jnp.einsum(
        "bkj,bkmc->jmc", onehot, contrib, precision=lax.Precision.HIGHEST
    ).reshape(-1, case_width)
    new_loads = lax.psum_scatter(
        partial_loads, ("blk", "tgt", "sec"), scatter_dimension=0, tiled=True
    )
    return (new_loads, pressure_f)


def on_device(modal_loads, receptance, shapes, coupling, panel_coords, panel_areas):
    lanes = 128
    secs = lax.axis_size("sec")
    mine = modal_loads.shape[0] * lax.axis_size("blk") // (lax.axis_size("blk") * lax.axis_size("tgt") * secs)
    fits = (
        lax.axis_size("blk") == 2
        and lax.axis_size("tgt") == 4
        and secs & (secs - 1) == 0
        and coupling.shape[0] == 1
        and shapes.shape[2] == lanes
        and panel_coords.shape[1] == lanes
        and modal_loads.shape[1] == lanes
        and mine == lanes
    )
    body = on_device_fast if fits else on_device_general
    return body(modal_loads, receptance, shapes, coupling, panel_coords, panel_areas)


def solution(mesh):
    in_specs = (
        P("blk", None),
        P(None, ("tgt", "sec"), "blk"),
        P(("blk", "tgt", "sec"), None, None),
        P(("blk", "tgt", "sec"), None),
        P(None, ("blk", "tgt", "sec")),
        P(("blk", "tgt", "sec")),
    )
    out_specs = (P(("blk", "tgt", "sec"), None), P(("blk", "tgt", "sec"), None))
    return jax.shard_map(
        on_device, mesh=mesh, in_specs=in_specs, out_specs=out_specs, check_vma=False
    )
```
